256 devices in a mesh: queue: 64 (over x, z, y_hi), tok: 4 (over y_lo, core).
Axes of the slice: x: 4, y: 4 (y_hi: 2, y_lo: 2; y = y_hi * 2 + y_lo), z: 8, core: 2. Of those that a mesh axis runs over, the one named last changes fastest.
Arguments:
- frames: bfloat16 [64, 256, 3072], P('queue', 'tok'), may hold values from -6 to 6
- levels: int32 [64], P('queue'), may hold values from 0 to 63
- frame_mask: int32 [64, 64], P('queue'), may hold values from 0 to 1, as said below
- modulation: bfloat16 [64, 9216], replicated, may hold values from -3 to 3
- w_query: bfloat16 [3072, 1536], P(None, 'tok'), may hold values from -0.109375 to 0.109375
- w_key: bfloat16 [3072, 1536], P(None, 'tok'), may hold values from -0.109375 to 0.109375
- w_value: bfloat16 [3072, 1536], P(None, 'tok'), may hold values from -0.109375 to 0.109375
- w_out: bfloat16 [1536, 3072], P('tok'), may hold values from -0.15625 to 0.15625
- query_gain: float32 [64], replicated, may hold values from 0.5 to 200
- key_gain: float32 [64], replicated, may hold values from 0.25 to 1.75
Outputs:
- next_queue: bfloat16 [64, 256, 3072], P('queue', 'tok')
The draws below stay inside these ranges and needn't reach their ends.
Inputs may be any that keep to these rules, and one draw needn't show every extreme that they name: frame_mask is 1 on the diagonal, 0 above it, 0 or 1 below it.
All inputs are finite; a program needn't handle non-finite values.
Results may differ from the reference program's by a relative error of at most 0.019.
Values may be sent and summed in bfloat16 or wider, within the bound.
A program may use at most 192 MiB of HBM per device.

```python
import jax
import jax.numpy as jnp
from jax import lax

D = 3072
HDIM = 64
HEADS = 24
LEVELS = 64
TOKF = 256
FRAMES = 64


def draw_frame_mask(key, part):
    key = jax.random.fold_in(key, 11)
    coin_key, far_key = jax.random.split(key, 2)
    coins = (jax.random.randint(coin_key, (FRAMES, FRAMES), 0, 16) == 0).astype(jnp.int32)
    far_coins = jax.random.randint(far_key, (FRAMES, FRAMES), 0, 2)
    rows_index = jnp.arange(FRAMES)[:, None]
    cols_index = jnp.arange(FRAMES)[None, :]
    below = jnp.where(cols_index < rows_index, coins, 0)
    below = jnp.where(cols_index == rows_index - FRAMES // 2, far_coins, below)
    return jnp.where(cols_index == rows_index, 1, below).astype(jnp.int32)


def draw_query_gain(key, part):
    key = jax.random.fold_in(key, 23)
    base_key = jax.random.fold_in(key, 0)
    return jax.random.uniform(base_key, (HDIM,), jnp.float32, 0.5, 2.0)


def place_ends(entries, stream_key, low, top_value):
    longest = entries.shape.index(max(entries.shape))
    spots = []
    for shift in (0, 1):
        where = [jax.random.randint(jax.random.fold_in(stream_key, axis), (), 0, length) for axis, length in enumerate(entries.shape)]
        where[longest] = (where[longest] + shift) % entries.shape[longest]
        spots.append(tuple(where))
    return entries.at[spots[0]].set(low).at[spots[1]].set(top_value)


def shard_levels(rng, extent, cuts, low, largest):
    gain, own = 1.0, jax.random.fold_in(rng, 6)
    for position, shards_of in cuts:
        steps = jnp.exp(jax.random.uniform(jax.random.fold_in(own, position), (shards_of,), jnp.float32, low / len(cuts), largest / len(cuts)))
        gain = gain * jnp.repeat(steps, extent[position] // shards_of).reshape([-1 if axis == position else 1 for axis in range(len(extent))])
    return gain


def scatter_about(rng, dims, deviation, bound, pieces=(), kind=jnp.bfloat16):
    values = jax.random.normal(rng, dims, jnp.float32) * deviation
    if len(pieces) > 0:
        values = shard_levels(rng, dims, pieces, -0.22, 0.18) * values
    return jnp.clip(values, min=-bound, max=bound).astype(kind)


def setup_inputs(seed: int = 0) -> dict:
    key_list = jax.random.split(jax.random.key(seed), 11)
    return {
        "frames": scatter_about(key_list[0], (FRAMES, TOKF, D), 1.0, 6.0, ((0, 64), (1, 4))),
        "levels": place_ends(jax.random.randint(key_list[1], (FRAMES,), 0, LEVELS), jax.random.fold_in(key_list[1], 1), 0, LEVELS - 1).astype(jnp.int32),
        "frame_mask": draw_frame_mask(jax.random.fold_in(key_list[10], 71), 0),
        "modulation": scatter_about(key_list[3], (LEVELS, 3 * D), 0.5, 3.0),
        "w_query": scatter_about(key_list[4], (D, HEADS * HDIM), D ** -0.5, 0.109375, ((1, 4),)),
        "w_key": scatter_about(key_list[5], (D, HEADS * HDIM), D ** -0.5, 0.109375, ((1, 4),)),
        "w_value": scatter_about(key_list[6], (D, HEADS * HDIM), D ** -0.5, 0.109375, ((1, 4),)),
        "w_out": scatter_about(key_list[7], (HEADS * HDIM, D), (HEADS * HDIM) ** -0.5, 0.15625, ((0, 4),)),
        "query_gain": draw_query_gain(jax.random.fold_in(key_list[10], 71), 0),
        "key_gain": jnp.clip(1.0 + 0.15 * jax.random.normal(key_list[9], (HDIM,), jnp.float32), 0.25, 1.75),
    }


def layer_norm(values_in):
    center = lax.optimization_barrier(jnp.mean(values_in, axis=-1, keepdims=True))
    spread = lax.optimization_barrier(jnp.mean(jnp.square(values_in - center), axis=-1, keepdims=True))
    return (values_in - center) * lax.rsqrt(spread + 1e-06)

def reference(frames, levels, frame_mask, modulation, w_query, w_key, w_value, w_out, query_gain, key_gain):
    residual = frames.astype(jnp.float32)
    one_hot = (levels[:, None] == jnp.arange(LEVELS, dtype=jnp.int32)[None, :]).astype(jnp.bfloat16)
    mod_rows = jnp.dot(one_hot, modulation, preferred_element_type=jnp.float32)
    shift = mod_rows[:, :D]
    scale = mod_rows[:, D:2 * D]
    gate = mod_rows[:, 2 * D:]
    modulated = (layer_norm(residual) * (1.0 + scale[:, None, :]) + shift[:, None, :]).astype(jnp.bfloat16)
    modulated = modulated.reshape(FRAMES * TOKF, D)
    queries = jnp.dot(modulated, w_query, preferred_element_type=jnp.float32).reshape(-1, HEADS, HDIM)
    queries = (layer_norm(queries) * query_gain).astype(jnp.bfloat16)
    keys = jnp.dot(modulated, w_key, preferred_element_type=jnp.float32).reshape(-1, HEADS, HDIM)
    keys = (layer_norm(keys) * key_gain).astype(jnp.bfloat16)
    values = jnp.dot(modulated, w_value, preferred_element_type=jnp.float32).astype(jnp.bfloat16)
    values = values.reshape(-1, HEADS, HDIM)
    key_float = keys.astype(jnp.float32)
    value_float = values.astype(jnp.float32)
    key_frame = (jnp.arange(FRAMES * TOKF, dtype=jnp.int32) // TOKF).astype(jnp.int32)

    def one_frame(frame_index):
        query_rows = lax.dynamic_slice_in_dim(queries, (frame_index * TOKF).astype(jnp.int32), TOKF, 0).astype(jnp.float32)
        scores = jnp.einsum('qhd,khd->hqk', query_rows, key_float) * HDIM ** (-0.5)
        visible = frame_mask[frame_index][key_frame] > 0
        scores = jnp.where(visible[None, None, :], scores, -jnp.inf)
        row_max = lax.optimization_barrier(jnp.max(scores, axis=-1, keepdims=True))
        weights = jnp.exp(scores - row_max)
        total = lax.optimization_barrier(jnp.sum(weights, axis=-1))
        rounded = lax.optimization_barrier(weights.astype(jnp.bfloat16)).astype(jnp.float32)
        summed = jnp.einsum('hqk,khd->qhd', rounded, value_float)
        attended = summed / jnp.transpose(total)[:, :, None]
        return attended.reshape(TOKF, HEADS * HDIM).astype(jnp.bfloat16)
    attended = lax.map(one_frame, jnp.arange(FRAMES, dtype=jnp.int32))
    projected = jnp.dot(attended.reshape(FRAMES * TOKF, HEADS * HDIM), w_out, preferred_element_type=jnp.float32)
    projected = projected.reshape(FRAMES, TOKF, D)
    updated = (residual + gate[:, None, :] * projected).astype(jnp.bfloat16)
    return jnp.concatenate([updated[FRAMES - 1:], updated[:FRAMES - 1]], axis=0)
```

```python
import jax
import jax.numpy as jnp
from jax import lax
from jax.experimental import pallas as pl
from jax.experimental.pallas import tpu as pltpu
from jax.sharding import PartitionSpec as P

HDIM = 64
NX, NZ, NYH = 4, 8, 2
PLACES = NX * NYH
HEADS_HERE = 6
CHUNKS = 4
TILES = 6
MESH = pl.DeviceIdType.MESH


def queue_index(place, z):
    return ((place // NYH) * NZ + z) * NYH + place % NYH


def layer_norm(values_in):
    center = jnp.mean(values_in, axis=-1, keepdims=True)
    spread = jnp.mean(jnp.square(values_in - center), axis=-1, keepdims=True)
    return (values_in - center) * lax.rsqrt(spread + 1e-06)


def positions():
    q_at = lax.axis_index("queue")
    return (q_at // (NZ * NYH)) * NYH + q_at % NYH, (q_at // NYH) % NZ, lax.axis_index("tok")


def send(src, dst, send_sem, recv_sem, place, z, tok):
    copy = pltpu.make_async_remote_copy(
        src_ref=src,
        dst_ref=dst,
        send_sem=send_sem,
        recv_sem=recv_sem,
        device_id=(queue_index(place, z), tok),
        device_id_type=MESH,
    )
    copy.start()
    return copy


def landed(ref, sem):
    pltpu.make_async_copy(ref, ref, sem).wait()


def gather_kernel(
    frames_ref, shift_ref, scale_ref, wq_ref, wk_ref, wv_ref, qg_ref, kg_ref,
    q_all, kv_all,
    x_buf, w_buf, q_buf, kv_buf,
    w_sem, tok_send, tok_recv, kv_send, kv_recv, q_send, q_recv, ring_send, ring_recv,
):
    place, z, tok = positions()
    up, down = lax.rem(z + 1, NZ), lax.rem(z + NZ - 1, NZ)
    sibling = tok + 1 - 2 * lax.rem(tok, 2)
    across = lax.rem(tok + 2, 4)
    sibling_across = lax.rem(sibling + 2, 4)
    weights = [
        pltpu.make_async_copy(w, w_buf.at[n], w_sem.at[n]) for n, w in enumerate((wq_ref, wk_ref, wv_ref))
    ]
    for copy in weights:
        copy.start()

    barrier = pltpu.get_barrier_semaphore()
    for other_tok in (sibling, across):
        pl.semaphore_signal(
            barrier, inc=1, device_id=(queue_index(place, z), other_tok), device_id_type=MESH
        )
    for p in range(PLACES):
        for other_z in (up, down):
            pl.semaphore_signal(barrier, inc=1, device_id=(queue_index(p, other_z), tok), device_id_type=MESH)

        @pl.when(p != place)
        def _():
            pl.semaphore_signal(barrier, inc=1, device_id=(queue_index(p, z), tok), device_id_type=MESH)

    rows = frames_ref.shape[0]
    step = rows // CHUNKS

    def x_rows(owner, c):
        return x_buf.at[pl.ds(pl.multiple_of(owner * rows + c * step, step), step)]

    started = []
    for c in range(CHUNKS):
        part = layer_norm(frames_ref[c * step : (c + 1) * step].astype(jnp.float32))
        part = part * (1.0 + scale_ref[...]) + shift_ref[...]
        x_buf[pl.ds(pl.multiple_of(tok * rows + c * step, step), step)] = part.astype(jnp.bfloat16)
        if c == 0:
            pl.semaphore_wait(barrier, 2 + 3 * PLACES - 1)
        for way, other_tok in ((1, across), (0, sibling)):
            mine = x_rows(tok, c)
            started.append(send(mine, mine, tok_send.at[way, c], tok_recv.at[way, c], place, z, other_tok))
    for c in range(CHUNKS):
        theirs = x_rows(across, c)
        landed(theirs, tok_recv.at[1, c])
        started.append(send(theirs, theirs, tok_send.at[2, c], tok_recv.at[2, c], place, z, sibling))
    for c in range(CHUNKS):
        landed(x_rows(sibling, c), tok_recv.at[0, c])
    for copy in weights:
        copy.wait()
    for c in range(CHUNKS):
        landed(x_rows(sibling_across, c), tok_recv.at[2, c])

    after = lax.rem(queue_index(place, z) + 1, NX * NZ * NYH)
    after_place = (after // (NZ * NYH)) * NYH + after % NYH
    after_z = (after // NYH) % NZ
    x = x_buf[...]
    half = x.shape[0] // 2
    for i in range(HEADS_HERE // 2):
        cols = slice(2 * HDIM * i, 2 * HDIM * (i + 1))
        k = jnp.dot(x, w_buf[1, :, cols], preferred_element_type=jnp.float32)
        v = jnp.dot(x, w_buf[2, :, cols], preferred_element_type=jnp.float32)
        for j in range(2):
            d = 2 * i + j
            head = slice(j * HDIM, (j + 1) * HDIM)
            kn = layer_norm(k[:, head]) * kg_ref[...]
            kv_buf[d] = jnp.concatenate([kn, v[:, head]], axis=1).astype(jnp.bfloat16)

            @pl.when(d != place)
            def _():
                send(kv_buf.at[d], kv_all.at[z, place], kv_send.at[d], kv_recv.at[place], d, z, tok)

            @pl.when(d == place)
            def _():
                pltpu.make_async_copy(kv_buf.at[d], kv_all.at[z, place], kv_recv.at[place]).start()

    for i in range(HEADS_HERE // 2):
        cols = slice(2 * HDIM * i, 2 * HDIM * (i + 1))
        q = jnp.dot(x, w_buf[0, :, cols], preferred_element_type=jnp.float32)
        for j in range(2):
            d = 2 * i + j
            head = slice(j * HDIM, (j + 1) * HDIM)
            qn = (layer_norm(q[:, head]) * qg_ref[...]).astype(jnp.bfloat16).astype(jnp.float32)
            qn = qn * HDIM ** (-0.5)
            q_buf[d] = jnp.concatenate([qn[:half], qn[half:]], axis=1).astype(jnp.bfloat16)
            stays = jnp.logical_and(d == place, after_z == z)

            @pl.when(jnp.logical_not(stays))
            def _():
                send(
                    q_buf.at[d], q_all.at[after_place], q_send.at[d], q_recv.at[after_place], d, after_z, tok
                )

            @pl.when(stays)
            def _():
                pltpu.make_async_copy(q_buf.at[d], q_all.at[after_place], q_recv.at[after_place]).start()

    @pl.when(place < HEADS_HERE)
    def _():
        sent = []
        last = NZ // 2
        for hop in range(1, last + 1):
            for c in range(PLACES):
                if hop == 1:
                    landed(kv_all.at[z, c], kv_recv.at[c])
                for way, target in ((0, up), (1, down)):
                    source = lax.rem(z + NZ - (hop - 1), NZ) if way == 0 else lax.rem(z + hop - 1, NZ)
                    block = kv_all.at[source, c]
                    if hop > 1:
                        landed(block, ring_recv.at[way, hop - 2, c])
                    if hop == last and (c < PLACES // 2) != (way == 0):
                        continue
                    sent.append(
                        send(
                            block, block, ring_send.at[way, hop - 1, c], ring_recv.at[way, hop - 1, c],
                            place, target, tok,
                        )
                    )
        opposite = lax.rem(z + last, NZ)
        for c in range(PLACES):
            way = 0 if c < PLACES // 2 else 1
            landed(kv_all.at[opposite, c], ring_recv.at[way, last - 1, c])
        for c in range(PLACES):
            landed(q_all.at[c], q_recv.at[c])
        for copy in sent:
            copy.wait_send()

    for copy in started:
        copy.wait_send()
    for d in range(HEADS_HERE):
        @pl.when(d != place)
        def _():
            landed(kv_buf.at[d], kv_send.at[d])

        @pl.when(jnp.logical_not(jnp.logical_and(d == place, after_z == z)))
        def _():
            landed(q_buf.at[d], q_send.at[d])


def gather(frames, shift, scale, wq, wk, wv, query_gain, key_gain):
    rows, width = frames.shape
    tokens = rows * 4
    vmem, hbm = pl.BlockSpec(memory_space=pltpu.VMEM), pl.BlockSpec(memory_space=pl.ANY)
    dma = pltpu.SemaphoreType.DMA
    return pl.pallas_call(
        gather_kernel,
        in_specs=[vmem, vmem, vmem, hbm, hbm, hbm, vmem, vmem],
        out_specs=[hbm, hbm],
        out_shape=[
            jax.ShapeDtypeStruct((PLACES, tokens // 2, 2 * HDIM), jnp.bfloat16),
            jax.ShapeDtypeStruct((NZ, PLACES, tokens, 2 * HDIM), jnp.bfloat16),
        ],
        scratch_shapes=[
            pltpu.VMEM((tokens, width), jnp.bfloat16),
            pltpu.VMEM((3,) + wq.shape, jnp.bfloat16),
            pltpu.VMEM((HEADS_HERE, tokens // 2, 2 * HDIM), jnp.bfloat16),
            pltpu.VMEM((HEADS_HERE, tokens, 2 * HDIM), jnp.bfloat16),
            dma((3,)),
            dma((3, CHUNKS)),
            dma((3, CHUNKS)),
            dma((HEADS_HERE,)),
            dma((PLACES,)),
            dma((HEADS_HERE,)),
            dma((PLACES,)),
            dma((2, NZ // 2, PLACES)),
            dma((2, NZ // 2, PLACES)),
        ],
        compiler_params=pltpu.CompilerParams(
            collective_id=0, has_side_effects=True, vmem_limit_bytes=48 * 1024 * 1024
        ),
    )(frames, shift, scale, wq, wk, wv, query_gain.reshape(1, HDIM), key_gain.reshape(1, HDIM))


def attend_kernel(count_ref, list_ref, q_ref, kv_ref, out_ref):
    frames_here, half, lanes = q_ref.shape
    rows = 2 * half
    low = lax.broadcasted_iota(jnp.int32, (half, lanes), 1) < HDIM

    def one_frame(i, _):
        packed = q_ref[i].astype(jnp.float32)
        top = jnp.where(low, packed, 0.0)
        bottom = jnp.where(low, pltpu.roll(packed, HDIM, 1), 0.0)
        q = jnp.concatenate([top, bottom], axis=0).astype(jnp.bfloat16)

        def one_block(j, state):
            running_max, running_sum, weighted = state
            kv = kv_ref[list_ref[i, j]]
            scores = lax.dot_general(kv, q, (((1,), (1,)), ((), ())), preferred_element_type=jnp.float32)
            new_max = jnp.maximum(running_max, jnp.max(scores, axis=0, keepdims=True))
            weights = jnp.exp(scores - new_max)
            rescale = jnp.exp(running_max - new_max)
            new_sum = running_sum * rescale + jnp.sum(weights, axis=0, keepdims=True)
            added = lax.dot_general(
                kv, weights.astype(jnp.bfloat16), (((0,), (0,)), ((), ())), preferred_element_type=jnp.float32
            )
            return new_max, new_sum, weighted * rescale + added

        state = (
            jnp.full((1, rows), -1e30, jnp.float32),
            jnp.zeros((1, rows), jnp.float32),
            jnp.zeros((lanes, rows), jnp.float32),
        )
        _, total, weighted = lax.fori_loop(0, count_ref[i], one_block, state)
        attended = jnp.transpose(weighted[HDIM:] / total)
        chunk = rows // 4
        for c in range(4):
            part = attended[c * chunk : (c + 1) * chunk]
            out_ref[i, c] = jnp.concatenate([part[: chunk // 2], part[chunk // 2 :]], axis=1).astype(jnp.bfloat16)
        return 0

    lax.fori_loop(0, frames_here, one_frame, 0)


def attend(count, visible_list, q, kv):
    frames_here, half, lanes = q.shape
    return pl.pallas_call(
        attend_kernel,
        grid_spec=pltpu.PrefetchScalarGridSpec(
            num_scalar_prefetch=2,
            grid=(1,),
            in_specs=[
                pl.BlockSpec(q.shape, lambda i, *_: (0, 0, 0)),
                pl.BlockSpec(kv.shape, lambda i, *_: (0, 0, 0)),
            ],
            out_specs=pl.BlockSpec((frames_here, 4, half // 4, lanes), lambda i, *_: (0, 0, 0, 0)),
        ),
        out_shape=jax.ShapeDtypeStruct((frames_here, 4, half // 4, lanes), jnp.bfloat16),
        compiler_params=pltpu.CompilerParams(vmem_limit_bytes=48 * 1024 * 1024),
    )(count, visible_list, q, kv)


def finish_kernel(
    att_ref, w_ref, frames_ref, gate_ref, out_ref, got, att_buf, w_buf, w_sem, send_sem, recv_sem
):
    place, z, tok = positions()
    width = out_ref.shape[1]
    tile = width // TILES
    weights = [
        pltpu.make_async_copy(w_ref.at[:, pl.ds(n * tile, tile)], w_buf.at[n], w_sem.at[n]) for n in range(TILES)
    ]
    for copy in weights:
        copy.start()
    barrier = pltpu.get_barrier_semaphore()
    for p in range(PLACES):
        for t in range(4):
            @pl.when(jnp.logical_not(jnp.logical_and(p == place, t == tok)))
            def _():
                pl.semaphore_signal(barrier, inc=1, device_id=(queue_index(p, z), t), device_id_type=MESH)
    pl.semaphore_wait(barrier, 4 * PLACES - 1)

    slot = tok * HEADS_HERE + place

    @pl.when(place < HEADS_HERE)
    def _():
        for p in range(PLACES):
            for t in range(4):
                here = jnp.logical_and(p == place, t == tok)

                @pl.when(jnp.logical_not(here))
                def _():
                    send(att_ref.at[p, t], got.at[slot], send_sem.at[p, t], recv_sem.at[slot], p, z, t)

                @pl.when(here)
                def _():
                    pltpu.make_async_copy(att_ref.at[p, t], got.at[slot], recv_sem.at[slot]).start()

    heads, half, lanes = got.shape
    low = lax.broadcasted_iota(jnp.int32, (half, lanes), 1) < HDIM
    for m in range(heads // 2):
        landed(got.at[2 * m], recv_sem.at[2 * m])
        landed(got.at[2 * m + 1], recv_sem.at[2 * m + 1])
        first, second = got[2 * m].astype(jnp.float32), got[2 * m + 1].astype(jnp.float32)
        cols = slice(m * lanes, (m + 1) * lanes)
        att_buf[:half, cols] = jnp.where(low, first, pltpu.roll(second, HDIM, 1)).astype(jnp.bfloat16)
        att_buf[half:, cols] = jnp.where(low, pltpu.roll(first, HDIM, 1), second).astype(jnp.bfloat16)
    attended = att_buf[...]
    for n in range(TILES):
        weights[n].wait()
        projected = jnp.dot(attended, w_buf[n], preferred_element_type=jnp.float32)
        cols = slice(n * tile, (n + 1) * tile)
        updated = frames_ref[:, cols].astype(jnp.float32) + gate_ref[:, cols] * projected
        out_ref[:, cols] = updated.astype(jnp.bfloat16)

    @pl.when(place < HEADS_HERE)
    def _():
        for p in range(PLACES):
            for t in range(4):
                @pl.when(jnp.logical_not(jnp.logical_and(p == place, t == tok)))
                def _():
                    landed(att_ref.at[p, t], send_sem.at[p, t])


def finish(attended, w_full, frames, gate):
    vmem, hbm = pl.BlockSpec(memory_space=pltpu.VMEM), pl.BlockSpec(memory_space=pl.ANY)
    dma = pltpu.SemaphoreType.DMA
    depth, width = w_full.shape
    return pl.pallas_call(
        finish_kernel,
        in_specs=[hbm, hbm, vmem, vmem],
        out_specs=vmem,
        out_shape=jax.ShapeDtypeStruct(frames.shape, jnp.bfloat16),
        scratch_shapes=[
            pltpu.VMEM((4 * HEADS_HERE,) + attended.shape[2:], jnp.bfloat16),
            pltpu.VMEM((frames.shape[0], depth), jnp.bfloat16),
            pltpu.VMEM((TILES, depth, width // TILES), jnp.bfloat16),
            dma((TILES,)),
            dma((PLACES, 4)),
            dma((4 * HEADS_HERE,)),
        ],
        compiler_params=pltpu.CompilerParams(
            collective_id=1, has_side_effects=True, vmem_limit_bytes=48 * 1024 * 1024
        ),
    )(attended, w_full, frames, gate)


def next_slot(block):
    n = lax.axis_size("queue")
    return lax.ppermute(block, "queue", [(i, (i + 1) % n) for i in range(n)])


def body(
    frames, levels, frame_mask, modulation, w_query, w_key, w_value, w_out, query_gain, key_gain
):
    width = frames.shape[2]
    slots = frame_mask.shape[1]
    q_at = lax.axis_index("queue")
    place, z, _ = positions()

    prev_frames = next_slot(frames)[0]
    table = lax.all_gather(
        jnp.concatenate([frame_mask, levels[:, None]], axis=1), "queue", axis=0, tiled=True
    )
    table = jnp.concatenate([table[-1:], table[:-1]], axis=0)
    prev_level = lax.dynamic_slice(table, (q_at, slots), (1, 1))[0, 0]
    gate = lax.dynamic_slice(modulation, (prev_level, 2 * width), (1, width)).astype(jnp.float32)

    rows = lax.dynamic_slice_in_dim(table[:, :slots].reshape(NX, NZ, NYH, slots), z, 1, 1)
    rows = rows.reshape(PLACES, NX, NZ, NYH).transpose(0, 2, 1, 3).reshape(PLACES, slots) > 0
    slot_ids = jnp.arange(slots, dtype=jnp.int32)
    before = rows[:, None, :] & (slot_ids[None, None, :] < slot_ids[None, :, None])
    rank = jnp.sum(before.astype(jnp.int32), axis=2)
    hit = rows[:, :, None] & (rank[:, :, None] == slot_ids[None, None, :])
    visible_list = jnp.sum(jnp.where(hit, slot_ids[None, :, None], 0), axis=1).astype(jnp.int32)
    count = jnp.where(place < HEADS_HERE, jnp.sum(rows.astype(jnp.int32), axis=1), 0)

    own = lax.dynamic_slice(modulation, (levels[0], 0), (1, 2 * width)).astype(jnp.float32)
    w_full = lax.all_gather(w_out, "tok", axis=0, tiled=True)
    q, kv = gather(
        frames[0], own[:, :width], own[:, width:], w_query, w_key, w_value, query_gain, key_gain
    )
    kv = kv.reshape((slots,) + kv.shape[2:])
    attended = attend(count, visible_list, q, kv)
    return finish(attended, w_full, prev_frames, gate)[None]


def solution(mesh):
    return jax.shard_map(
        body,
        mesh=mesh,
        in_specs=(
            P("queue", "tok", None),
            P("queue"),
            P("queue", None),
            P(),
            P(None, "tok"),
            P(None, "tok"),
            P(None, "tok"),
            P("tok", None),
            P(),
            P(),
        ),
        out_specs=P("queue", "tok", None),
        check_vma=False,
    )
```

```python
import jax
import jax.numpy as jnp
from jax import lax
from jax.experimental import pallas as pl
from jax.experimental.pallas import tpu as pltpu
from jax.sharding import PartitionSpec as P

HDIM = 64
NX, NZ, NYH = 4, 8, 2
PLACES = NX * NYH
HEADS_HERE = 6
CHUNKS = 4
TILES = 6
MESH = pl.DeviceIdType.MESH


def queue_index(place, z):
    return ((place // NYH) * NZ + z) * NYH + place % NYH


def layer_norm(values_in):
    center = jnp.mean(values_in, axis=-1, keepdims=True)
    spread = jnp.mean(jnp.square(values_in - center), axis=-1, keepdims=True)
    return (values_in - center) * lax.rsqrt(spread + 1e-06)


def positions():
    q_at = lax.axis_index("queue")
    return (q_at // (NZ * NYH)) * NYH + q_at % NYH, (q_at // NYH) % NZ, lax.axis_index("tok")


def send(src, dst, send_sem, recv_sem, place, z, tok):
    copy = pltpu.make_async_remote_copy(
        src_ref=src,
        dst_ref=dst,
        send_sem=send_sem,
        recv_sem=recv_sem,
        device_id=(queue_index(place, z), tok),
        device_id_type=MESH,
    )
    copy.start()
    return copy


def landed(ref, sem):
    pltpu.make_async_copy(ref, ref, sem).wait()


def gather_kernel(
    frames_ref, shift_ref, scale_ref, mask_ref, level_ref, wq_ref, wk_ref, wv_ref, qg_ref, kg_ref,
    q_all, kv_all, info_ref,
    x_buf, wq_buf, wkv_buf, q_buf, kv_buf, row_buf, rows_got,
    wq_sem, wkv_sem, tok_send, tok_recv, row_send, row_recv, kv_send, kv_recv, q_send, q_recv,
    ring_send, ring_recv, relay_send, relay_recv,
):
    place, z, tok = positions()
    up, down = lax.rem(z + 1, NZ), lax.rem(z + NZ - 1, NZ)
    sibling = tok + 1 - 2 * lax.rem(tok, 2)
    across = lax.rem(tok + 2, 4)
    sibling_across = lax.rem(sibling + 2, 4)
    pair = 2 * HDIM
    pairs = HEADS_HERE // 2
    weights = []
    for i in range(pairs):
        for j, w in enumerate((wk_ref, wv_ref)):
            weights.append(
                pltpu.make_async_copy(
                    w.at[:, pl.ds(i * pair, pair)], wkv_buf.at[i, :, pl.ds(j * pair, pair)], wkv_sem.at[i, j]
                )
            )
    weights.append(pltpu.make_async_copy(wq_ref, wq_buf, wq_sem))
    for copy in weights:
        copy.start()

    barrier = pltpu.get_barrier_semaphore()
    for other_tok in (sibling, across):
        pl.semaphore_signal(
            barrier, inc=1, device_id=(queue_index(place, z), other_tok), device_id_type=MESH
        )
    for p in range(PLACES):
        for other_z in (up, down):
            pl.semaphore_signal(barrier, inc=1, device_id=(queue_index(p, other_z), tok), device_id_type=MESH)

        @pl.when(p != place)
        def _():
            pl.semaphore_signal(barrier, inc=1, device_id=(queue_index(p, z), tok), device_id_type=MESH)

    rows = frames_ref.shape[0]
    step = rows // CHUNKS

    def x_rows(owner, c):
        return x_buf.at[pl.ds(pl.multiple_of(owner * rows + c * step, step), step)]

    started = []
    for c in range(CHUNKS):
        part = layer_norm(frames_ref[c * step : (c + 1) * step].astype(jnp.float32))
        part = part * (1.0 + scale_ref[...]) + shift_ref[...]
        x_buf[pl.ds(pl.multiple_of(tok * rows + c * step, step), step)] = part.astype(jnp.bfloat16)
        if c == 0:
            pl.semaphore_wait(barrier, 2 + 3 * PLACES - 1)
        for way, other_tok in ((1, across), (0, sibling)):
            mine = x_rows(tok, c)
            started.append(send(mine, mine, tok_send.at[way, c], tok_recv.at[way, c], place, z, other_tok))

    after = lax.rem(queue_index(place, z) + 1, NX * NZ * NYH)
    after_place = (after // (NZ * NYH)) * NYH + after % NYH
    after_z = (after // NYH) % NZ
    slots = mask_ref.shape[1]
    row_buf[...] = jnp.zeros_like(row_buf)
    row_buf[0:1, :slots] = mask_ref[...]
    row_buf[0:1, slots:] = jnp.broadcast_to(level_ref[...], (1, row_buf.shape[1] - slots))
    for d in range(PLACES):
        stays = jnp.logical_and(d == place, after_z == z)

        @pl.when(jnp.logical_not(stays))
        def _():
            send(row_buf, rows_got.at[after_place], row_send.at[d], row_recv.at[after_place], d, after_z, tok)

        @pl.when(stays)
        def _():
            pltpu.make_async_copy(row_buf, rows_got.at[after_place], row_recv.at[after_place]).start()

    half = x_buf.shape[0] // 2
    first = tok // 2
    at = [pl.multiple_of(first * half, half), pl.multiple_of((1 - first) * half, half)]

    def part_of(ref, n):
        return ref.at[pl.ds(at[n], half)]

    def keys_values(n):
        x = x_buf[pl.ds(at[n], half)]
        for i in range(pairs):
            if n == 0:
                weights[2 * i].wait()
                weights[2 * i + 1].wait()
            both = jnp.dot(x, wkv_buf[i], preferred_element_type=jnp.float32)
            for j in range(2):
                d = 2 * i + j
                kn = layer_norm(both[:, j * HDIM : (j + 1) * HDIM]) * kg_ref[...]
                v = both[:, pair + j * HDIM : pair + (j + 1) * HDIM]
                kv_buf[d, pl.ds(at[n], half)] = jnp.concatenate([kn, v], axis=1).astype(jnp.bfloat16)
                block = part_of(kv_buf.at[d], n)
                here = part_of(kv_all.at[z, place], n)

                @pl.when(d != place)
                def _():
                    send(block, here, kv_send.at[d, n], kv_recv.at[place, n], d, z, tok)

                @pl.when(d == place)
                def _():
                    pltpu.make_async_copy(block, here, kv_recv.at[place, n]).start()

                @pl.when(place >= HEADS_HERE)
                def _():
                    pltpu.make_async_copy(block, part_of(kv_all.at[z, d], n), kv_recv.at[d, n]).start()

    last = NZ // 2

    def relay(source, way, hop, n, c):
        k = 2 * (hop - 1) + way if hop < last else 2 * (last - 1)

        @pl.when(place >= HEADS_HERE)
        def _():
            send(
                part_of(kv_all.at[source, c], n), part_of(kv_all.at[source, place], n),
                relay_send.at[k, n, c], relay_recv.at[k, n, place - HEADS_HERE], c, z, tok,
            )

    def pass_on(hop, n):
        for c in range(HEADS_HERE):
            if hop == 1:
                landed(part_of(kv_all.at[z, c], n), kv_recv.at[c, n])
            for way, target in ((0, up), (1, down)):
                source = lax.rem(z + NZ - (hop - 1), NZ) if way == 0 else lax.rem(z + hop - 1, NZ)
                block = part_of(kv_all.at[source, c], n)
                if hop > 1:
                    landed(block, ring_recv.at[way, hop - 2, n, c])
                if hop < last or (c < HEADS_HERE // 2) == (way == 0):
                    started.append(
                        send(
                            block, block, ring_send.at[way, hop - 1, n, c], ring_recv.at[way, hop - 1, n, c],
                            place, target, tok,
                        )
                    )
                if hop > 1:
                    relay(source, way, hop - 1, n, c)

    for c in range(CHUNKS):
        landed(x_rows(sibling, c), tok_recv.at[0, c])
    keys_values(0)
    pass_on(1, 0)
    for c in range(CHUNKS):
        theirs = x_rows(across, c)
        landed(theirs, tok_recv.at[1, c])
        started.append(send(theirs, theirs, tok_send.at[2, c], tok_recv.at[2, c], place, z, sibling))
    for c in range(CHUNKS):
        landed(x_rows(sibling_across, c), tok_recv.at[2, c])
    keys_values(1)
    pass_on(1, 1)

    weights[-1].wait()
    x = x_buf[...]
    for i in range(pairs):
        q = jnp.dot(x, wq_buf[:, i * pair : (i + 1) * pair], preferred_element_type=jnp.float32)
        for j in range(2):
            d = 2 * i + j
            qn = layer_norm(q[:, j * HDIM : (j + 1) * HDIM]) * qg_ref[...]
            qn = qn.astype(jnp.bfloat16).astype(jnp.float32) * HDIM ** (-0.5)
            q_buf[d] = jnp.concatenate([qn[:half], qn[half:]], axis=1).astype(jnp.bfloat16)
            stays = jnp.logical_and(d == place, after_z == z)

            @pl.when(jnp.logical_not(stays))
            def _():
                send(
                    q_buf.at[d], q_all.at[after_place], q_send.at[d], q_recv.at[after_place], d, after_z, tok
                )

            @pl.when(stays)
            def _():
                pltpu.make_async_copy(q_buf.at[d], q_all.at[after_place], q_recv.at[after_place]).start()

    for hop in range(2, last + 1):
        for n in range(2):
            pass_on(hop, n)

    for p in range(PLACES):
        landed(rows_got.at[p], row_recv.at[p])
    table = rows_got[:, 0, :]
    lanes = table.shape[1]
    lane = lax.broadcasted_iota(jnp.int32, (PLACES, lanes), 1)
    seen = jnp.where(jnp.logical_and(table > 0, lane < slots), 1.0, 0.0)
    by_row = lax.broadcasted_iota(jnp.int32, (lanes, lanes), 0)
    by_lane = lax.broadcasted_iota(jnp.int32, (lanes, lanes), 1)
    ahead = jnp.where(by_row < by_lane, 1.0, 0.0)
    rank = jnp.dot(seen, ahead, preferred_element_type=jnp.float32)
    spot = jnp.where(seen > 0, rank, -1.0)
    spot_t = jnp.transpose(jnp.concatenate([spot] * (lanes // PLACES), axis=0))
    kept_at = ((by_row >> 1) & (NZ - 1)) * PLACES + (by_row >> 4) * NYH + (by_row & 1)
    kept_at = kept_at.astype(jnp.float32)
    lane_f = by_lane.astype(jnp.float32)
    listed = [
        jnp.sum(jnp.where(spot_t[:, p : p + 1] == lane_f, kept_at, 0.0), axis=0, keepdims=True)
        for p in range(PLACES)
    ]
    listed = jnp.concatenate(listed, axis=0).astype(jnp.int32)
    count = jnp.sum(seen, axis=1, keepdims=True).astype(jnp.int32)
    count = jnp.where(place < HEADS_HERE, count, 0)
    info_ref[...] = jnp.where(lane == slots, count, jnp.where(lane == slots + 1, table, listed))

    opposite = lax.rem(z + last, NZ)
    for n in range(2):
        for c in range(HEADS_HERE):
            way = 0 if c < HEADS_HERE // 2 else 1
            landed(part_of(kv_all.at[opposite, c], n), ring_recv.at[way, last - 1, n, c])
            relay(opposite, way, last, n, c)

    @pl.when(place < HEADS_HERE)
    def _():
        for n in range(2):
            for p in range(HEADS_HERE, PLACES):
                landed(part_of(kv_all.at[z, p], n), kv_recv.at[p, n])
                for hop in range(1, last):
                    landed(part_of(kv_all.at[lax.rem(z + NZ - hop, NZ), p], n), relay_recv.at[2 * (hop - 1), n, p - HEADS_HERE])
                    landed(part_of(kv_all.at[lax.rem(z + hop, NZ), p], n), relay_recv.at[2 * (hop - 1) + 1, n, p - HEADS_HERE])
                landed(part_of(kv_all.at[opposite, p], n), relay_recv.at[2 * (last - 1), n, p - HEADS_HERE])
        for p in range(PLACES):
            landed(q_all.at[p], q_recv.at[p])

    for copy in started:
        copy.wait_send()
    for d in range(PLACES):
        @pl.when(jnp.logical_not(jnp.logical_and(d == place, after_z == z)))
        def _():
            landed(row_buf, row_send.at[d])
            if d < HEADS_HERE:
                landed(q_buf.at[d], q_send.at[d])

    for d in range(HEADS_HERE):
        for n in range(2):
            @pl.when(d != place)
            def _():
                landed(part_of(kv_buf.at[d], n), kv_send.at[d, n])

    @pl.when(place >= HEADS_HERE)
    def _():
        for n in range(2):
            for c in range(HEADS_HERE):
                for hop in range(1, last):
                    for way in range(2):
                        source = lax.rem(z + NZ - hop, NZ) if way == 0 else lax.rem(z + hop, NZ)
                        landed(part_of(kv_all.at[source, c], n), relay_send.at[2 * (hop - 1) + way, n, c])
                landed(part_of(kv_all.at[opposite, c], n), relay_send.at[2 * (last - 1), n, c])


def gather(frames, shift, scale, mask, level, wq, wk, wv, query_gain, key_gain):
    rows, width = frames.shape
    tokens = rows * 4
    pair = 2 * HDIM
    vmem, hbm = pl.BlockSpec(memory_space=pltpu.VMEM), pl.BlockSpec(memory_space=pl.ANY)
    dma = pltpu.SemaphoreType.DMA
    relays = 2 * (NZ // 2 - 1) + 1
    return pl.pallas_call(
        gather_kernel,
        in_specs=[vmem, vmem, vmem, vmem, vmem, hbm, hbm, hbm, vmem, vmem],
        out_specs=[hbm, hbm, vmem],
        out_shape=[
            jax.ShapeDtypeStruct((PLACES, tokens // 2, pair), jnp.bfloat16),
            jax.ShapeDtypeStruct((NZ, PLACES, tokens, pair), jnp.bfloat16),
            jax.ShapeDtypeStruct((PLACES, 128), jnp.int32),
        ],
        scratch_shapes=[
            pltpu.VMEM((tokens, width), jnp.bfloat16),
            pltpu.VMEM(wq.shape, jnp.bfloat16),
            pltpu.VMEM((HEADS_HERE // 2, width, 2 * pair), jnp.bfloat16),
            pltpu.VMEM((HEADS_HERE, tokens // 2, pair), jnp.bfloat16),
            pltpu.VMEM((HEADS_HERE, tokens, pair), jnp.bfloat16),
            pltpu.VMEM((8, 128), jnp.int32),
            pltpu.VMEM((PLACES, 8, 128), jnp.int32),
            dma,
            dma((HEADS_HERE // 2, 2)),
            dma((3, CHUNKS)),
            dma((3, CHUNKS)),
            dma((PLACES,)),
            dma((PLACES,)),
            dma((HEADS_HERE, 2)),
            dma((PLACES, 2)),
            dma((HEADS_HERE,)),
            dma((PLACES,)),
            dma((2, NZ // 2, 2, HEADS_HERE)),
            dma((2, NZ // 2, 2, HEADS_HERE)),
            dma((relays, 2, HEADS_HERE)),
            dma((relays, 2, PLACES - HEADS_HERE)),
        ],
        compiler_params=pltpu.CompilerParams(
            collective_id=0, has_side_effects=True, vmem_limit_bytes=60 * 1024 * 1024
        ),
    )(frames, shift, scale, mask, level, wq, wk, wv, query_gain.reshape(1, HDIM), key_gain.reshape(1, HDIM))


def attend_kernel(info_ref, q_ref, kv_ref, out_ref):
    frames_here, half, lanes = q_ref.shape
    rows = 2 * half
    slots = kv_ref.shape[0]
    low = lax.broadcasted_iota(jnp.int32, (half, lanes), 1) < HDIM

    def one_frame(i, _):
        packed = q_ref[i].astype(jnp.float32)
        top = jnp.where(low, packed, 0.0)
        bottom = jnp.where(low, pltpu.roll(packed, HDIM, 1), 0.0)
        q = jnp.concatenate([top, bottom], axis=0).astype(jnp.bfloat16)

        def blocks(state, *numbers):
            running_max, running_sum, weighted = state
            kvs = [kv_ref[info_ref[i, j]] for j in numbers]
            scores = [
                lax.dot_general(kv, q, (((1,), (1,)), ((), ())), preferred_element_type=jnp.float32) for kv in kvs
            ]
            new_max = running_max
            for s in scores:
                new_max = jnp.maximum(new_max, jnp.max(s, axis=0, keepdims=True))
            rescale = jnp.exp(running_max - new_max)
            running_sum, weighted = running_sum * rescale, weighted * rescale
            for kv, s in zip(kvs, scores):
                weights = jnp.exp(s - new_max)
                running_sum = running_sum + jnp.sum(weights, axis=0, keepdims=True)
                weighted = weighted + lax.dot_general(
                    kv, weights.astype(jnp.bfloat16), (((0,), (0,)), ((), ())), preferred_element_type=jnp.float32
                )
            return new_max, running_sum, weighted

        state = (
            jnp.full((1, rows), -1e30, jnp.float32),
            jnp.zeros((1, rows), jnp.float32),
            jnp.zeros((lanes, rows), jnp.float32),
        )
        count = info_ref[i, slots]
        twos = count // 2
        state = lax.fori_loop(0, twos, lambda j, s: blocks(s, 2 * j, 2 * j + 1), state)
        _, total, weighted = lax.fori_loop(2 * twos, count, lambda j, s: blocks(s, j), state)
        attended = jnp.transpose(weighted[HDIM:] / total)
        chunk = rows // 4
        for c in range(4):
            part = attended[c * chunk : (c + 1) * chunk]
            out_ref[i, c] = jnp.concatenate([part[: chunk // 2], part[chunk // 2 :]], axis=1).astype(jnp.bfloat16)
        return 0

    lax.fori_loop(0, frames_here, one_frame, 0)


def attend(info, q, kv):
    frames_here, half, lanes = q.shape
    return pl.pallas_call(
        attend_kernel,
        grid_spec=pltpu.PrefetchScalarGridSpec(
            num_scalar_prefetch=1,
            grid=(1,),
            in_specs=[
                pl.BlockSpec(q.shape, lambda i, *_: (0, 0, 0)),
                pl.BlockSpec(kv.shape, lambda i, *_: (0, 0, 0)),
            ],
            out_specs=pl.BlockSpec((frames_here, 4, half // 4, lanes), lambda i, *_: (0, 0, 0, 0)),
        ),
        out_shape=jax.ShapeDtypeStruct((frames_here, 4, half // 4, lanes), jnp.bfloat16),
        compiler_params=pltpu.CompilerParams(vmem_limit_bytes=48 * 1024 * 1024),
    )(info, q, kv)


def finish_kernel(
    att_ref, w_ref, frames_ref, gate_ref, out_ref, got, att_buf, w_buf, w_sem, send_sem, recv_sem
):
    place, z, tok = positions()
    width = out_ref.shape[1]
    tile = width // TILES
    weights = [
        pltpu.make_async_copy(w_ref.at[:, pl.ds(n * tile, tile)], w_buf.at[n], w_sem.at[n]) for n in range(TILES)
    ]
    for copy in weights:
        copy.start()
    barrier = pltpu.get_barrier_semaphore()
    for p in range(PLACES):
        for t in range(4):
            @pl.when(jnp.logical_not(jnp.logical_and(p == place, t == tok)))
            def _():
                pl.semaphore_signal(barrier, inc=1, device_id=(queue_index(p, z), t), device_id_type=MESH)
    pl.semaphore_wait(barrier, 4 * PLACES - 1)

    slot = tok * HEADS_HERE + place

    @pl.when(place < HEADS_HERE)
    def _():
        for p in range(PLACES):
            for t in range(4):
                here = jnp.logical_and(p == place, t == tok)

                @pl.when(jnp.logical_not(here))
                def _():
                    send(att_ref.at[p, t], got.at[slot], send_sem.at[p, t], recv_sem.at[slot], p, z, t)

                @pl.when(here)
                def _():
                    pltpu.make_async_copy(att_ref.at[p, t], got.at[slot], recv_sem.at[slot]).start()

    heads, half, lanes = got.shape
    low = lax.broadcasted_iota(jnp.int32, (half, lanes), 1) < HDIM
    for m in range(heads // 2):
        landed(got.at[2 * m], recv_sem.at[2 * m])
        landed(got.at[2 * m + 1], recv_sem.at[2 * m + 1])
        first, second = got[2 * m].astype(jnp.float32), got[2 * m + 1].astype(jnp.float32)
        cols = slice(m * lanes, (m + 1) * lanes)
        att_buf[:half, cols] = jnp.where(low, first, pltpu.roll(second, HDIM, 1)).astype(jnp.bfloat16)
        att_buf[half:, cols] = jnp.where(low, pltpu.roll(first, HDIM, 1), second).astype(jnp.bfloat16)
    attended = att_buf[...]
    for n in range(TILES):
        weights[n].wait()
        projected = jnp.dot(attended, w_buf[n], preferred_element_type=jnp.float32)
        cols = slice(n * tile, (n + 1) * tile)
        updated = frames_ref[:, cols].astype(jnp.float32) + gate_ref[:, cols] * projected
        out_ref[:, cols] = updated.astype(jnp.bfloat16)

    @pl.when(place < HEADS_HERE)
    def _():
        for p in range(PLACES):
            for t in range(4):
                @pl.when(jnp.logical_not(jnp.logical_and(p == place, t == tok)))
                def _():
                    landed(att_ref.at[p, t], send_sem.at[p, t])


def finish(attended, w_full, frames, gate):
    vmem, hbm = pl.BlockSpec(memory_space=pltpu.VMEM), pl.BlockSpec(memory_space=pl.ANY)
    dma = pltpu.SemaphoreType.DMA
    depth, width = w_full.shape
    return pl.pallas_call(
        finish_kernel,
        in_specs=[hbm, hbm, vmem, vmem],
        out_specs=vmem,
        out_shape=jax.ShapeDtypeStruct(frames.shape, jnp.bfloat16),
        scratch_shapes=[
            pltpu.VMEM((4 * HEADS_HERE,) + attended.shape[2:], jnp.bfloat16),
            pltpu.VMEM((frames.shape[0], depth), jnp.bfloat16),
            pltpu.VMEM((TILES, depth, width // TILES), jnp.bfloat16),
            dma((TILES,)),
            dma((PLACES, 4)),
            dma((4 * HEADS_HERE,)),
        ],
        compiler_params=pltpu.CompilerParams(
            collective_id=1, has_side_effects=True, vmem_limit_bytes=48 * 1024 * 1024
        ),
    )(attended, w_full, frames, gate)


def next_slot(block):
    n = lax.axis_size("queue")
    return lax.ppermute(block, "queue", [(i, (i + 1) % n) for i in range(n)])


def body(
    frames, levels, frame_mask, modulation, w_query, w_key, w_value, w_out, query_gain, key_gain
):
    width = frames.shape[2]
    slots = frame_mask.shape[1]
    place, _, _ = positions()

    prev_frames = next_slot(frames)[0]
    w_full = lax.all_gather(w_out, "tok", axis=0, tiled=True)
    own = lax.dynamic_slice(modulation, (levels[0], 0), (1, 2 * width)).astype(jnp.float32)
    q, kv, info = gather(
        frames[0], own[:, :width], own[:, width:], frame_mask, levels[None],
        w_query, w_key, w_value, query_gain, key_gain,
    )
    attended = attend(info, q, kv.reshape((slots,) + kv.shape[2:]))
    prev_level = lax.dynamic_slice(info, (place, slots + 1), (1, 1))[0, 0]
    gate = lax.dynamic_slice(modulation, (prev_level, 2 * width), (1, width)).astype(jnp.float32)
    return finish(attended, w_full, prev_frames, gate)[None]


def solution(mesh):
    return jax.shard_map(
        body,
        mesh=mesh,
        in_specs=(
            P("queue", "tok", None),
            P("queue"),
            P("queue", None),
            P(),
            P(None, "tok"),
            P(None, "tok"),
            P(None, "tok"),
            P("tok", None),
            P(),
            P(),
        ),
        out_specs=P("queue", "tok", None),
        check_vma=False,
    )
```

```python
import jax
import jax.numpy as jnp
from jax import lax
from jax.experimental import pallas as pl
from jax.experimental.pallas import tpu as pltpu
from jax.sharding import PartitionSpec as P

HDIM = 64
NX, NZ, NYH = 4, 8, 2
PLACES = NX * NYH
HEADS_HERE = 6
CHUNKS = 4
TILES = 6
PIECES = 3
KV_LOADS = 16
MESH = pl.DeviceIdType.MESH


def queue_index(place, z):
    return ((place // NYH) * NZ + z) * NYH + place % NYH


def layer_norm(values_in):
    center = jnp.mean(values_in, axis=-1, keepdims=True)
    spread = jnp.mean(jnp.square(values_in - center), axis=-1, keepdims=True)
    return (values_in - center) * lax.rsqrt(spread + 1e-06)


def positions():
    q_at = lax.axis_index("queue")
    return (q_at // (NZ * NYH)) * NYH + q_at % NYH, (q_at // NYH) % NZ, lax.axis_index("tok")


def send(src, dst, send_sem, recv_sem, place, z, tok):
    copy = pltpu.make_async_remote_copy(
        src_ref=src,
        dst_ref=dst,
        send_sem=send_sem,
        recv_sem=recv_sem,
        device_id=(queue_index(place, z), tok),
        device_id_type=MESH,
    )
    copy.start()
    return copy


def landed(ref, sem):
    pltpu.make_async_copy(ref, ref, sem).wait()


def gather_kernel(
    frames_ref, shift_ref, scale_ref, gate_ref, mask_ref, wq_ref, wk_ref, wv_ref, wo_ref, qg_ref, kg_ref,
    q_all, kv_all, info_ref, prev_frames, prev_gate, wo_all,
    x_buf, wq_buf, wkv_buf, q_buf, kv_buf, row_buf, rows_got,
    wq_sem, wkv_sem, tok_send, tok_recv, row_send, row_recv, kv_send, kv_recv, q_send, q_recv,
    ring_send, ring_recv, relay_send, relay_recv, prev_send, prev_recv, wo_send, wo_recv, wo_own,
):
    place, z, tok = positions()
    up, down = lax.rem(z + 1, NZ), lax.rem(z + NZ - 1, NZ)
    sibling = tok + 1 - 2 * lax.rem(tok, 2)
    across = lax.rem(tok + 2, 4)
    sibling_across = lax.rem(sibling + 2, 4)
    pair = 2 * HDIM
    pairs = HEADS_HERE // 2
    weights = []
    for i in range(pairs):
        for j, w in enumerate((wk_ref, wv_ref)):
            weights.append(
                pltpu.make_async_copy(
                    w.at[:, pl.ds(i * pair, pair)], wkv_buf.at[i, :, pl.ds(j * pair, pair)], wkv_sem.at[i, j]
                )
            )
    weights.append(pltpu.make_async_copy(wq_ref, wq_buf, wq_sem))
    for copy in weights:
        copy.start()
    own_block = pltpu.make_async_copy(wo_ref, wo_all.at[tok], wo_own)
    twin = place + 1 - 2 * lax.rem(place, NYH)

    barrier = pltpu.get_barrier_semaphore()
    for other_tok in (sibling, across):
        pl.semaphore_signal(
            barrier, inc=1, device_id=(queue_index(place, z), other_tok), device_id_type=MESH
        )
    pl.semaphore_signal(barrier, inc=1, device_id=(queue_index(twin, z), across), device_id_type=MESH)
    for p in range(PLACES):
        for other_z in (up, down):
            pl.semaphore_signal(barrier, inc=1, device_id=(queue_index(p, other_z), tok), device_id_type=MESH)

        @pl.when(p != place)
        def _():
            pl.semaphore_signal(barrier, inc=1, device_id=(queue_index(p, z), tok), device_id_type=MESH)

    rows = frames_ref.shape[0]
    step = rows // CHUNKS

    def x_rows(owner, c):
        return x_buf.at[pl.ds(pl.multiple_of(owner * rows + c * step, step), step)]

    started = []
    for c in range(CHUNKS):
        part = layer_norm(frames_ref[c * step : (c + 1) * step].astype(jnp.float32))
        part = part * (1.0 + scale_ref[...]) + shift_ref[...]
        x_buf[pl.ds(pl.multiple_of(tok * rows + c * step, step), step)] = part.astype(jnp.bfloat16)
        if c == 0:
            pl.semaphore_wait(barrier, 3 + 3 * PLACES - 1)
        for way, other_tok in ((1, across), (0, sibling)):
            mine = x_rows(tok, c)
            started.append(send(mine, mine, tok_send.at[way, c], tok_recv.at[way, c], place, z, other_tok))

    after = lax.rem(queue_index(place, z) + 1, NX * NZ * NYH)
    after_place = (after // (NZ * NYH)) * NYH + after % NYH
    after_z = (after // NYH) % NZ
    slots = mask_ref.shape[1]
    row_buf[...] = jnp.zeros_like(row_buf)
    row_buf[0:1, :slots] = mask_ref[...]
    for d in range(PLACES):
        stays = jnp.logical_and(d == place, after_z == z)

        @pl.when(jnp.logical_not(stays))
        def _():
            send(row_buf, rows_got.at[after_place], row_send.at[d], row_recv.at[after_place], d, after_z, tok)

        @pl.when(stays)
        def _():
            pltpu.make_async_copy(row_buf, rows_got.at[after_place], row_recv.at[after_place]).start()

    started.append(
        send(gate_ref, prev_gate, prev_send.at[0], prev_recv.at[0], after_place, after_z, tok)
    )

    half = x_buf.shape[0] // 2
    first = tok // 2
    at = [pl.multiple_of(first * half, half), pl.multiple_of((1 - first) * half, half)]

    def part_of(ref, n):
        return ref.at[pl.ds(at[n], half)]

    def keys_values(n):
        x = x_buf[pl.ds(at[n], half)]
        for i in range(pairs):
            if n == 0:
                weights[2 * i].wait()
                weights[2 * i + 1].wait()
            both = jnp.dot(x, wkv_buf[i], preferred_element_type=jnp.float32)
            for j in range(2):
                d = 2 * i + j
                kn = layer_norm(both[:, j * HDIM : (j + 1) * HDIM]) * kg_ref[...]
                v = both[:, pair + j * HDIM : pair + (j + 1) * HDIM]
                kv_buf[d, pl.ds(at[n], half)] = jnp.concatenate([kn, v], axis=1).astype(jnp.bfloat16)
                block = part_of(kv_buf.at[d], n)
                here = part_of(kv_all.at[z, place], n)

                @pl.when(d != place)
                def _():
                    send(block, here, kv_send.at[d, n], kv_recv.at[place, n], d, z, tok)

                @pl.when(d == place)
                def _():
                    pltpu.make_async_copy(block, here, kv_recv.at[place, n]).start()

                @pl.when(place >= HEADS_HERE)
                def _():
                    pltpu.make_async_copy(block, part_of(kv_all.at[z, d], n), kv_recv.at[d, n]).start()

    last = NZ // 2

    def relay(source, way, hop, n, c):
        k = 2 * (hop - 1) + way if hop < last else 2 * (last - 1)

        @pl.when(place >= HEADS_HERE)
        def _():
            send(
                part_of(kv_all.at[source, c], n), part_of(kv_all.at[source, place], n),
                relay_send.at[k, n, c], relay_recv.at[k, n, place - HEADS_HERE], c, z, tok,
            )

    def pass_on(hop, n):
        for c in range(HEADS_HERE):
            if hop == 1:
                landed(part_of(kv_all.at[z, c], n), kv_recv.at[c, n])
            for way, target in ((0, up), (1, down)):
                source = lax.rem(z + NZ - (hop - 1), NZ) if way == 0 else lax.rem(z + hop - 1, NZ)
                block = part_of(kv_all.at[source, c], n)
                if hop > 1:
                    landed(block, ring_recv.at[way, hop - 2, n, c])
                if hop < last or (c < HEADS_HERE // 2) == (way == 0):
                    started.append(
                        send(
                            block, block, ring_send.at[way, hop - 1, n, c], ring_recv.at[way, hop - 1, n, c],
                            place, target, tok,
                        )
                    )
                if hop > 1:
                    relay(source, way, hop - 1, n, c)

    for c in range(CHUNKS):
        landed(x_rows(sibling, c), tok_recv.at[0, c])
    keys_values(0)
    pass_on(1, 0)
    for c in range(CHUNKS):
        theirs = x_rows(across, c)
        landed(theirs, tok_recv.at[1, c])
        started.append(send(theirs, theirs, tok_send.at[2, c], tok_recv.at[2, c], place, z, sibling))
    for c in range(CHUNKS):
        landed(x_rows(sibling_across, c), tok_recv.at[2, c])
    keys_values(1)
    pass_on(1, 1)

    depth = wo_ref.shape[0]
    piece = depth // (2 * PIECES)
    own_block.start()
    started.append(send(wo_ref, wo_all.at[tok], wo_send.at[0], wo_recv.at[0], place, z, sibling))
    for m in range(PIECES):
        for side, target in ((0, place), (1, twin)):
            part = pl.ds((side * PIECES + m) * piece, piece)
            k = 1 + side * PIECES + m
            started.append(
                send(wo_ref.at[part], wo_all.at[tok, part], wo_send.at[k], wo_recv.at[k], target, z, across)
            )

    def share_weights(m):
        for side in range(2):
            part = pl.ds((side * PIECES + m) * piece, piece)
            k = 1 + side * PIECES + m
            block = wo_all.at[across, part]
            landed(block, wo_recv.at[k])
            k = k + 2 * PIECES
            started.append(send(block, block, wo_send.at[k], wo_recv.at[k], place, z, sibling))

    weights[-1].wait()
    x = x_buf[...]
    for i in range(pairs):
        q = jnp.dot(x, wq_buf[:, i * pair : (i + 1) * pair], preferred_element_type=jnp.float32)
        for j in range(2):
            d = 2 * i + j
            qn = layer_norm(q[:, j * HDIM : (j + 1) * HDIM]) * qg_ref[...]
            qn = qn.astype(jnp.bfloat16).astype(jnp.float32) * HDIM ** (-0.5)
            q_buf[d] = jnp.concatenate([qn[:half], qn[half:]], axis=1).astype(jnp.bfloat16)
            stays = jnp.logical_and(d == place, after_z == z)

            @pl.when(jnp.logical_not(stays))
            def _():
                send(
                    q_buf.at[d], q_all.at[after_place], q_send.at[d], q_recv.at[after_place], d, after_z, tok
                )

            @pl.when(stays)
            def _():
                pltpu.make_async_copy(q_buf.at[d], q_all.at[after_place], q_recv.at[after_place]).start()

    started.append(
        send(frames_ref, prev_frames, prev_send.at[1], prev_recv.at[1], after_place, after_z, tok)
    )
    for hop in range(2, last + 1):
        for n in range(2):
            pass_on(hop, n)
    for m in range(PIECES):
        share_weights(m)

    for p in range(PLACES):
        landed(rows_got.at[p], row_recv.at[p])
    table = rows_got[:, 0, :]
    lanes = table.shape[1]
    lane = lax.broadcasted_iota(jnp.int32, (PLACES, lanes), 1)
    seen = jnp.where(jnp.logical_and(table > 0, lane < slots), 1.0, 0.0)
    by_row = lax.broadcasted_iota(jnp.int32, (lanes, lanes), 0)
    by_lane = lax.broadcasted_iota(jnp.int32, (lanes, lanes), 1)
    ahead = jnp.where(by_row < by_lane, 1.0, 0.0)
    rank = jnp.dot(seen, ahead, preferred_element_type=jnp.float32)
    spot = jnp.where(seen > 0, rank, -1.0)
    spot_t = jnp.transpose(jnp.concatenate([spot] * (lanes // PLACES), axis=0))
    kept_at = ((by_row >> 1) & (NZ - 1)) * PLACES + (by_row >> 4) * NYH + (by_row & 1)
    kept_at = kept_at.astype(jnp.float32)
    lane_f = by_lane.astype(jnp.float32)
    listed = [
        jnp.sum(jnp.where(spot_t[:, p : p + 1] == lane_f, kept_at, 0.0), axis=0, keepdims=True)
        for p in range(PLACES)
    ]
    listed = jnp.concatenate(listed, axis=0).astype(jnp.int32)
    count = jnp.sum(seen, axis=1, keepdims=True).astype(jnp.int32)
    count = jnp.where(place < HEADS_HERE, count, 0)
    info_ref[...] = jnp.where(lane == slots, count, listed)

    opposite = lax.rem(z + last, NZ)
    for n in range(2):
        for c in range(HEADS_HERE):
            way = 0 if c < HEADS_HERE // 2 else 1
            landed(part_of(kv_all.at[opposite, c], n), ring_recv.at[way, last - 1, n, c])
            relay(opposite, way, last, n, c)

    @pl.when(place < HEADS_HERE)
    def _():
        for n in range(2):
            for p in range(HEADS_HERE, PLACES):
                landed(part_of(kv_all.at[z, p], n), kv_recv.at[p, n])
                for hop in range(1, last):
                    landed(part_of(kv_all.at[lax.rem(z + NZ - hop, NZ), p], n), relay_recv.at[2 * (hop - 1), n, p - HEADS_HERE])
                    landed(part_of(kv_all.at[lax.rem(z + hop, NZ), p], n), relay_recv.at[2 * (hop - 1) + 1, n, p - HEADS_HERE])
                landed(part_of(kv_all.at[opposite, p], n), relay_recv.at[2 * (last - 1), n, p - HEADS_HERE])
        for p in range(PLACES):
            landed(q_all.at[p], q_recv.at[p])

    landed(prev_gate, prev_recv.at[0])
    landed(prev_frames, prev_recv.at[1])
    own_block.wait()
    landed(wo_all.at[sibling], wo_recv.at[0])
    for k in range(2 * PIECES):
        landed(wo_all.at[sibling_across, pl.ds(k * piece, piece)], wo_recv.at[1 + 2 * PIECES + k])
    for copy in started:
        copy.wait_send()
    for d in range(PLACES):
        @pl.when(jnp.logical_not(jnp.logical_and(d == place, after_z == z)))
        def _():
            landed(row_buf, row_send.at[d])
            if d < HEADS_HERE:
                landed(q_buf.at[d], q_send.at[d])

    for d in range(HEADS_HERE):
        for n in range(2):
            @pl.when(d != place)
            def _():
                landed(part_of(kv_buf.at[d], n), kv_send.at[d, n])

    @pl.when(place >= HEADS_HERE)
    def _():
        for n in range(2):
            for c in range(HEADS_HERE):
                for hop in range(1, last):
                    for way in range(2):
                        source = lax.rem(z + NZ - hop, NZ) if way == 0 else lax.rem(z + hop, NZ)
                        landed(part_of(kv_all.at[source, c], n), relay_send.at[2 * (hop - 1) + way, n, c])
                landed(part_of(kv_all.at[opposite, c], n), relay_send.at[2 * (last - 1), n, c])


def gather(frames, shift, scale, gate, mask, wq, wk, wv, wo, query_gain, key_gain):
    rows, width = frames.shape
    tokens = rows * 4
    pair = 2 * HDIM
    vmem, hbm = pl.BlockSpec(memory_space=pltpu.VMEM), pl.BlockSpec(memory_space=pl.ANY)
    dma = pltpu.SemaphoreType.DMA
    relays = 2 * (NZ // 2 - 1) + 1
    return pl.pallas_call(
        gather_kernel,
        in_specs=[vmem, vmem, vmem, vmem, vmem, hbm, hbm, hbm, hbm, vmem, vmem],
        out_specs=[hbm, hbm, vmem, hbm, vmem, hbm],
        out_shape=[
            jax.ShapeDtypeStruct((PLACES, tokens // 2, pair), jnp.bfloat16),
            jax.ShapeDtypeStruct((NZ, PLACES, tokens, pair), jnp.bfloat16),
            jax.ShapeDtypeStruct((PLACES, 128), jnp.int32),
            jax.ShapeDtypeStruct(frames.shape, jnp.bfloat16),
            jax.ShapeDtypeStruct(gate.shape, jnp.float32),
            jax.ShapeDtypeStruct((4,) + wo.shape, jnp.bfloat16),
        ],
        scratch_shapes=[
            pltpu.VMEM((tokens, width), jnp.bfloat16),
            pltpu.VMEM(wq.shape, jnp.bfloat16),
            pltpu.VMEM((HEADS_HERE // 2, width, 2 * pair), jnp.bfloat16),
            pltpu.VMEM((HEADS_HERE, tokens // 2, pair), jnp.bfloat16),
            pltpu.VMEM((HEADS_HERE, tokens, pair), jnp.bfloat16),
            pltpu.VMEM((8, 128), jnp.int32),
            pltpu.VMEM((PLACES, 8, 128), jnp.int32),
            dma,
            dma((HEADS_HERE // 2, 2)),
            dma((3, CHUNKS)),
            dma((3, CHUNKS)),
            dma((PLACES,)),
            dma((PLACES,)),
            dma((HEADS_HERE, 2)),
            dma((PLACES, 2)),
            dma((HEADS_HERE,)),
            dma((PLACES,)),
            dma((2, NZ // 2, 2, HEADS_HERE)),
            dma((2, NZ // 2, 2, HEADS_HERE)),
            dma((relays, 2, HEADS_HERE)),
            dma((relays, 2, PLACES - HEADS_HERE)),
            dma((2,)),
            dma((2,)),
            dma((1 + 4 * PIECES,)),
            dma((1 + 4 * PIECES,)),
            dma,
        ],
        compiler_params=pltpu.CompilerParams(
            collective_id=0, has_side_effects=True, vmem_limit_bytes=60 * 1024 * 1024
        ),
    )(frames, shift, scale, gate, mask, wq, wk, wv, wo, query_gain.reshape(1, HDIM), key_gain.reshape(1, HDIM))


def attend_kernel(info_ref, q_hbm, kv_hbm, out_ref, q_ref, kv_ref, q_sem, kv_sem):
    loads = [pltpu.make_async_copy(q_hbm, q_ref, q_sem)]
    each = kv_ref.shape[0] // KV_LOADS
    for n in range(KV_LOADS):
        part = pl.ds(n * each, each)
        loads.append(pltpu.make_async_copy(kv_hbm.at[part], kv_ref.at[part], kv_sem.at[n]))
    for copy in loads:
        copy.start()
    for copy in loads:
        copy.wait()
    frames_here, half, lanes = q_ref.shape
    rows = 2 * half
    slots = kv_ref.shape[0]
    low = lax.broadcasted_iota(jnp.int32, (half, lanes), 1) < HDIM

    def one_frame(i, _):
        packed = q_ref[i].astype(jnp.float32)
        top = jnp.where(low, packed, 0.0)
        bottom = jnp.where(low, pltpu.roll(packed, HDIM, 1), 0.0)
        q = jnp.concatenate([top, bottom], axis=0).astype(jnp.bfloat16)

        def blocks(state, *numbers):
            running_max, running_sum, weighted = state
            kvs = [kv_ref[info_ref[i, j]] for j in numbers]
            scores = [
                lax.dot_general(kv, q, (((1,), (1,)), ((), ())), preferred_element_type=jnp.float32) for kv in kvs
            ]
            new_max = running_max
            for s in scores:
                new_max = jnp.maximum(new_max, jnp.max(s, axis=0, keepdims=True))
            rescale = jnp.exp(running_max - new_max)
            running_sum, weighted = running_sum * rescale, weighted * rescale
            for kv, s in zip(kvs, scores):
                weights = jnp.exp(s - new_max)
                running_sum = running_sum + jnp.sum(weights, axis=0, keepdims=True)
                weighted = weighted + lax.dot_general(
                    kv, weights.astype(jnp.bfloat16), (((0,), (0,)), ((), ())), preferred_element_type=jnp.float32
                )
            return new_max, running_sum, weighted

        state = (
            jnp.full((1, rows), -1e30, jnp.float32),
            jnp.zeros((1, rows), jnp.float32),
            jnp.zeros((lanes, rows), jnp.float32),
        )
        count = info_ref[i, slots]
        twos = count // 2
        state = lax.fori_loop(0, twos, lambda j, s: blocks(s, 2 * j, 2 * j + 1), state)
        _, total, weighted = lax.fori_loop(2 * twos, count, lambda j, s: blocks(s, j), state)
        attended = jnp.transpose(weighted[HDIM:] / total)
        chunk = rows // 4
        for c in range(4):
            part = attended[c * chunk : (c + 1) * chunk]
            out_ref[i, c] = jnp.concatenate([part[: chunk // 2], part[chunk // 2 :]], axis=1).astype(jnp.bfloat16)
        return 0

    lax.fori_loop(0, frames_here, one_frame, 0)


def attend(info, q, kv):
    frames_here, half, lanes = q.shape
    return pl.pallas_call(
        attend_kernel,
        grid_spec=pltpu.PrefetchScalarGridSpec(
            num_scalar_prefetch=1,
            grid=(1,),
            in_specs=[pl.BlockSpec(memory_space=pl.ANY)] * 2,
            out_specs=pl.BlockSpec((frames_here, 4, half // 4, lanes), lambda i, *_: (0, 0, 0, 0)),
            scratch_shapes=[
                pltpu.VMEM(q.shape, q.dtype),
                pltpu.VMEM(kv.shape, kv.dtype),
                pltpu.SemaphoreType.DMA,
                pltpu.SemaphoreType.DMA((KV_LOADS,)),
            ],
        ),
        out_shape=jax.ShapeDtypeStruct((frames_here, 4, half // 4, lanes), jnp.bfloat16),
        compiler_params=pltpu.CompilerParams(vmem_limit_bytes=60 * 1024 * 1024),
    )(info, q, kv)


def finish_kernel(
    att_ref, w_ref, frames_ref, gate_ref, out_ref, got, att_buf, w_buf, w_sem, send_sem, recv_sem
):
    place, z, tok = positions()
    width = out_ref.shape[1]
    tile = width // TILES
    weights = [
        pltpu.make_async_copy(w_ref.at[:, pl.ds(n * tile, tile)], w_buf.at[n], w_sem.at[n]) for n in range(TILES)
    ]
    for copy in weights:
        copy.start()
    barrier = pltpu.get_barrier_semaphore()
    for p in range(PLACES):
        for t in range(4):
            @pl.when(jnp.logical_not(jnp.logical_and(p == place, t == tok)))
            def _():
                pl.semaphore_signal(barrier, inc=1, device_id=(queue_index(p, z), t), device_id_type=MESH)
    pl.semaphore_wait(barrier, 4 * PLACES - 1)

    slot = tok * HEADS_HERE + place

    @pl.when(place < HEADS_HERE)
    def _():
        for p in range(PLACES):
            for t in range(4):
                here = jnp.logical_and(p == place, t == tok)

                @pl.when(jnp.logical_not(here))
                def _():
                    send(att_ref.at[p, t], got.at[slot], send_sem.at[p, t], recv_sem.at[slot], p, z, t)

                @pl.when(here)
                def _():
                    pltpu.make_async_copy(att_ref.at[p, t], got.at[slot], recv_sem.at[slot]).start()

    heads, half, lanes = got.shape
    low = lax.broadcasted_iota(jnp.int32, (half, lanes), 1) < HDIM
    for m in range(heads // 2):
        landed(got.at[2 * m], recv_sem.at[2 * m])
        landed(got.at[2 * m + 1], recv_sem.at[2 * m + 1])
        first, second = got[2 * m].astype(jnp.float32), got[2 * m + 1].astype(jnp.float32)
        cols = slice(m * lanes, (m + 1) * lanes)
        att_buf[:half, cols] = jnp.where(low, first, pltpu.roll(second, HDIM, 1)).astype(jnp.bfloat16)
        att_buf[half:, cols] = jnp.where(low, pltpu.roll(first, HDIM, 1), second).astype(jnp.bfloat16)
    attended = att_buf[...]
    for n in range(TILES):
        weights[n].wait()
        projected = jnp.dot(attended, w_buf[n], preferred_element_type=jnp.float32)
        cols = slice(n * tile, (n + 1) * tile)
        updated = frames_ref[:, cols].astype(jnp.float32) + gate_ref[:, cols] * projected
        out_ref[:, cols] = updated.astype(jnp.bfloat16)

    @pl.when(place < HEADS_HERE)
    def _():
        for p in range(PLACES):
            for t in range(4):
                @pl.when(jnp.logical_not(jnp.logical_and(p == place, t == tok)))
                def _():
                    landed(att_ref.at[p, t], send_sem.at[p, t])


def finish(attended, w_full, frames, gate):
    vmem, hbm = pl.BlockSpec(memory_space=pltpu.VMEM), pl.BlockSpec(memory_space=pl.ANY)
    dma = pltpu.SemaphoreType.DMA
    depth, width = w_full.shape
    return pl.pallas_call(
        finish_kernel,
        in_specs=[hbm, hbm, vmem, vmem],
        out_specs=vmem,
        out_shape=jax.ShapeDtypeStruct(frames.shape, jnp.bfloat16),
        scratch_shapes=[
            pltpu.VMEM((4 * HEADS_HERE,) + attended.shape[2:], jnp.bfloat16),
            pltpu.VMEM((frames.shape[0], depth), jnp.bfloat16),
            pltpu.VMEM((TILES, depth, width // TILES), jnp.bfloat16),
            dma((TILES,)),
            dma((PLACES, 4)),
            dma((4 * HEADS_HERE,)),
        ],
        compiler_params=pltpu.CompilerParams(
            collective_id=1, has_side_effects=True, vmem_limit_bytes=60 * 1024 * 1024
        ),
    )(attended, w_full, frames, gate)


def body(
    frames, levels, frame_mask, modulation, w_query, w_key, w_value, w_out, query_gain, key_gain
):
    width = frames.shape[2]
    slots = frame_mask.shape[1]
    own = lax.dynamic_slice(modulation, (levels[0], 0), (1, 3 * width)).astype(jnp.float32)
    q, kv, info, prev_frames, prev_gate, w_all = gather(
        frames[0], own[:, :width], own[:, width : 2 * width], own[:, 2 * width :], frame_mask,
        w_query, w_key, w_value, w_out, query_gain, key_gain,
    )
    attended = attend(info, q, kv.reshape((slots,) + kv.shape[2:]))
    w_full = w_all.reshape(-1, width)
    return finish(attended, w_full, prev_frames, prev_gate)[None]


def solution(mesh):
    return jax.shard_map(
        body,
        mesh=mesh,
        in_specs=(
            P("queue", "tok", None),
            P("queue"),
            P("queue", None),
            P(),
            P(None, "tok"),
            P(None, "tok"),
            P(None, "tok"),
            P("tok", None),
            P(),
            P(),
        ),
        out_specs=P("queue", "tok", None),
        check_vma=False,
    )
```

```python
import jax
import jax.numpy as jnp
from jax import lax
from jax.experimental import pallas as pl
from jax.experimental.pallas import tpu as pltpu
from jax.sharding import PartitionSpec as P

HDIM = 64
NX, NZ, NYH = 4, 8, 2
PLACES = NX * NYH
HEADS_HERE = 6
CHUNKS = 4
TILES = 6
PIECES = 6
NEXT_PIECES = (1, 4)
MESH = pl.DeviceIdType.MESH


def queue_index(place, z):
    return ((place // NYH) * NZ + z) * NYH + place % NYH


def layer_norm(values_in):
    center = jnp.mean(values_in, axis=-1, keepdims=True)
    spread = jnp.mean(jnp.square(values_in - center), axis=-1, keepdims=True)
    return (values_in - center) * lax.rsqrt(spread + 1e-06)


def positions():
    q_at = lax.axis_index("queue")
    return (q_at // (NZ * NYH)) * NYH + q_at % NYH, (q_at // NYH) % NZ, lax.axis_index("tok")


def send(src, dst, send_sem, recv_sem, place, z, tok):
    copy = pltpu.make_async_remote_copy(
        src_ref=src,
        dst_ref=dst,
        send_sem=send_sem,
        recv_sem=recv_sem,
        device_id=(queue_index(place, z), tok),
        device_id_type=MESH,
    )
    copy.start()
    return copy


def landed(ref, sem):
    pltpu.make_async_copy(ref, ref, sem).wait()


def gather_kernel(
    frames_ref, shift_ref, scale_ref, gate_ref, mask_ref, wq_ref, wk_ref, wv_ref, wo_ref, qg_ref, kg_ref,
    q_all, kv_all, info_ref, prev_frames, prev_gate, wo_all,
    x_buf, wq_buf, wkv_buf, q_buf, kv_buf, row_buf, rows_got,
    wq_sem, wkv_sem, tok_send, tok_recv, row_send, row_recv, kv_send, kv_recv, q_send, q_recv,
    ring_send, ring_recv, prev_send, prev_recv, wo_send, wo_recv, wo_own,
):
    place, z, tok = positions()
    up, down = lax.rem(z + 1, NZ), lax.rem(z + NZ - 1, NZ)
    sibling = tok + 1 - 2 * lax.rem(tok, 2)
    across = lax.rem(tok + 2, 4)
    sibling_across = lax.rem(sibling + 2, 4)
    pair = 2 * HDIM
    pairs = HEADS_HERE // 2
    weights = []
    for i in range(pairs):
        for j, w in enumerate((wk_ref, wv_ref)):
            weights.append(
                pltpu.make_async_copy(
                    w.at[:, pl.ds(i * pair, pair)], wkv_buf.at[i, :, pl.ds(j * pair, pair)], wkv_sem.at[i, j]
                )
            )
    weights.append(pltpu.make_async_copy(wq_ref, wq_buf, wq_sem))
    for copy in weights:
        copy.start()
    own_block = pltpu.make_async_copy(wo_ref, wo_all.at[tok], wo_own)
    twin = place + 1 - 2 * lax.rem(place, NYH)

    barrier = pltpu.get_barrier_semaphore()
    for other_tok in (sibling, across):
        pl.semaphore_signal(
            barrier, inc=1, device_id=(queue_index(place, z), other_tok), device_id_type=MESH
        )
    pl.semaphore_signal(barrier, inc=1, device_id=(queue_index(twin, z), across), device_id_type=MESH)
    for p in range(PLACES):
        for other_z in (up, down):
            pl.semaphore_signal(barrier, inc=1, device_id=(queue_index(p, other_z), tok), device_id_type=MESH)

        @pl.when(p != place)
        def _():
            pl.semaphore_signal(barrier, inc=1, device_id=(queue_index(p, z), tok), device_id_type=MESH)

    rows = frames_ref.shape[0]
    step = rows // CHUNKS

    def x_rows(owner, c):
        return x_buf.at[pl.ds(pl.multiple_of(owner * rows + c * step, step), step)]

    started = []
    for c in range(CHUNKS):
        part = layer_norm(frames_ref[c * step : (c + 1) * step].astype(jnp.float32))
        part = part * (1.0 + scale_ref[...]) + shift_ref[...]
        x_buf[pl.ds(pl.multiple_of(tok * rows + c * step, step), step)] = part.astype(jnp.bfloat16)
        if c == 0:
            pl.semaphore_wait(barrier, 3 + 3 * PLACES - 1)
        for way, other_tok in ((1, across), (0, sibling)):
            mine = x_rows(tok, c)
            started.append(send(mine, mine, tok_send.at[way, c], tok_recv.at[way, c], place, z, other_tok))

    after = lax.rem(queue_index(place, z) + 1, NX * NZ * NYH)
    after_place = (after // (NZ * NYH)) * NYH + after % NYH
    after_z = (after // NYH) % NZ
    slots = mask_ref.shape[1]
    row_buf[...] = jnp.zeros_like(row_buf)
    row_buf[0:1, :slots] = mask_ref[...]
    for d in range(PLACES):
        stays = jnp.logical_and(d == place, after_z == z)

        @pl.when(jnp.logical_not(stays))
        def _():
            send(row_buf, rows_got.at[after_place], row_send.at[d], row_recv.at[after_place], d, after_z, tok)

        @pl.when(stays)
        def _():
            pltpu.make_async_copy(row_buf, rows_got.at[after_place], row_recv.at[after_place]).start()

    started.append(
        send(gate_ref, prev_gate, prev_send.at[0], prev_recv.at[0], after_place, after_z, tok)
    )

    half = x_buf.shape[0] // 2
    first = tok // 2
    at = [pl.multiple_of(first * half, half), pl.multiple_of((1 - first) * half, half)]

    def part_of(ref, n):
        return ref.at[pl.ds(at[n], half)]

    def keys_values(n):
        x = x_buf[pl.ds(at[n], half)]
        for i in range(pairs):
            if n == 0:
                weights[2 * i].wait()
                weights[2 * i + 1].wait()
            both = jnp.dot(x, wkv_buf[i], preferred_element_type=jnp.float32)
            for j in range(2):
                d = 2 * i + j
                kn = layer_norm(both[:, j * HDIM : (j + 1) * HDIM]) * kg_ref[...]
                v = both[:, pair + j * HDIM : pair + (j + 1) * HDIM]
                kv_buf[d, pl.ds(at[n], half)] = jnp.concatenate([kn, v], axis=1).astype(jnp.bfloat16)
                block = part_of(kv_buf.at[d], n)
                here = part_of(kv_all.at[z, place], n)

                @pl.when(d != place)
                def _():
                    send(block, here, kv_send.at[d, n], kv_recv.at[place, n], d, z, tok)

                @pl.when(d == place)
                def _():
                    pltpu.make_async_copy(block, here, kv_recv.at[place, n]).start()

    last = NZ // 2

    def ring_copy(hop, way, n, c):
        source = lax.rem(z + NZ - (hop - 1), NZ) if way == 0 else lax.rem(z + hop - 1, NZ)
        block = part_of(kv_all.at[source, c], n)
        return pltpu.make_async_remote_copy(
            src_ref=block,
            dst_ref=block,
            send_sem=ring_send.at[way, hop - 1, n, c],
            recv_sem=ring_recv.at[way, hop - 1, n, c],
            device_id=(queue_index(place, down if way else up), tok),
            device_id_type=MESH,
        )

    def goes(hop, way, c):
        return hop < last or (c < PLACES // 2) == (way == 0)

    def pass_on(hop, n):
        @pl.when(place < HEADS_HERE)
        def _():
            for c in range(PLACES):
                if hop == 1:
                    landed(part_of(kv_all.at[z, c], n), kv_recv.at[c, n])
                for way in range(2):
                    if hop > 1:
                        source = lax.rem(z + NZ - (hop - 1), NZ) if way == 0 else lax.rem(z + hop - 1, NZ)
                        landed(part_of(kv_all.at[source, c], n), ring_recv.at[way, hop - 2, n, c])
                    if goes(hop, way, c):
                        ring_copy(hop, way, n, c).start()

    for c in range(CHUNKS):
        landed(x_rows(sibling, c), tok_recv.at[0, c])
    keys_values(0)
    pass_on(1, 0)
    for c in range(CHUNKS):
        theirs = x_rows(across, c)
        landed(theirs, tok_recv.at[1, c])
        started.append(send(theirs, theirs, tok_send.at[2, c], tok_recv.at[2, c], place, z, sibling))
    for c in range(CHUNKS):
        landed(x_rows(sibling_across, c), tok_recv.at[2, c])
    keys_values(1)
    pass_on(1, 1)

    piece = wo_ref.shape[0] // PIECES
    lower = tok // 2 == 0
    y_next = jnp.where(lower, place, twin)
    y_before = jnp.where(lower, twin, place)
    own_block.start()
    started.append(send(wo_ref, wo_all.at[tok], wo_send.at[0], wo_recv.at[0], place, z, sibling))

    def offer_weights(m):
        part = pl.ds(m * piece, piece)
        target = y_next if m in NEXT_PIECES else y_before
        started.append(
            send(wo_ref.at[part], wo_all.at[tok, part], wo_send.at[1 + m], wo_recv.at[1 + m], target, z, across)
        )

    def share_weights(m):
        block = wo_all.at[across, pl.ds(m * piece, piece)]
        k = 1 + PIECES + m
        landed(block, wo_recv.at[1 + m])
        started.append(send(block, block, wo_send.at[k], wo_recv.at[k], place, z, sibling))

    for m in range(PIECES):
        offer_weights(m)
    weights[-1].wait()
    x = x_buf[...]
    for i in range(pairs):
        q = jnp.dot(x, wq_buf[:, i * pair : (i + 1) * pair], preferred_element_type=jnp.float32)
        for j in range(2):
            d = 2 * i + j
            qn = layer_norm(q[:, j * HDIM : (j + 1) * HDIM]) * qg_ref[...]
            qn = qn.astype(jnp.bfloat16).astype(jnp.float32) * HDIM ** (-0.5)
            q_buf[d] = jnp.concatenate([qn[:half], qn[half:]], axis=1).astype(jnp.bfloat16)
            stays = jnp.logical_and(d == place, after_z == z)

            @pl.when(jnp.logical_not(stays))
            def _():
                send(
                    q_buf.at[d], q_all.at[after_place], q_send.at[d], q_recv.at[after_place], d, after_z, tok
                )

            @pl.when(stays)
            def _():
                pltpu.make_async_copy(q_buf.at[d], q_all.at[after_place], q_recv.at[after_place]).start()

    started.append(
        send(frames_ref, prev_frames, prev_send.at[1], prev_recv.at[1], after_place, after_z, tok)
    )
    for hop in range(2, last + 1):
        for n in range(2):
            pass_on(hop, n)
    for m in range(PIECES):
        share_weights(m)

    for p in range(PLACES):
        landed(rows_got.at[p], row_recv.at[p])
    table = rows_got[:, 0, :]
    lanes = table.shape[1]
    lane = lax.broadcasted_iota(jnp.int32, (PLACES, lanes), 1)
    seen = jnp.where(jnp.logical_and(table > 0, lane < slots), 1.0, 0.0)
    by_row = lax.broadcasted_iota(jnp.int32, (lanes, lanes), 0)
    by_lane = lax.broadcasted_iota(jnp.int32, (lanes, lanes), 1)
    ahead = jnp.where(by_row < by_lane, 1.0, 0.0)
    rank = jnp.dot(seen, ahead, preferred_element_type=jnp.float32)
    spot = jnp.where(seen > 0, rank, -1.0)
    spot_t = jnp.transpose(jnp.concatenate([spot] * (lanes // PLACES), axis=0))
    kept_at = ((by_row >> 1) & (NZ - 1)) * PLACES + (by_row >> 4) * NYH + (by_row & 1)
    kept_at = kept_at.astype(jnp.float32)
    lane_f = by_lane.astype(jnp.float32)
    listed = [
        jnp.sum(jnp.where(spot_t[:, p : p + 1] == lane_f, kept_at, 0.0), axis=0, keepdims=True)
        for p in range(PLACES)
    ]
    listed = jnp.concatenate(listed, axis=0).astype(jnp.int32)
    count = jnp.sum(seen, axis=1, keepdims=True).astype(jnp.int32)
    count = jnp.where(place < HEADS_HERE, count, 0)
    info_ref[...] = jnp.where(lane == slots, count, listed)

    @pl.when(place < HEADS_HERE)
    def _():
        opposite = lax.rem(z + last, NZ)
        for n in range(2):
            for c in range(PLACES):
                way = 0 if c < PLACES // 2 else 1
                landed(part_of(kv_all.at[opposite, c], n), ring_recv.at[way, last - 1, n, c])
        for p in range(PLACES):
            landed(q_all.at[p], q_recv.at[p])
        for hop in range(1, last + 1):
            for n in range(2):
                for c in range(PLACES):
                    for way in range(2):
                        if goes(hop, way, c):
                            ring_copy(hop, way, n, c).wait_send()

    landed(prev_gate, prev_recv.at[0])
    landed(prev_frames, prev_recv.at[1])
    own_block.wait()
    landed(wo_all.at[sibling], wo_recv.at[0])
    for m in range(PIECES):
        landed(wo_all.at[sibling_across, pl.ds(m * piece, piece)], wo_recv.at[1 + PIECES + m])
    for copy in started:
        copy.wait_send()
    for d in range(PLACES):
        @pl.when(jnp.logical_not(jnp.logical_and(d == place, after_z == z)))
        def _():
            landed(row_buf, row_send.at[d])
            if d < HEADS_HERE:
                landed(q_buf.at[d], q_send.at[d])

    for d in range(HEADS_HERE):
        for n in range(2):
            @pl.when(d != place)
            def _():
                landed(part_of(kv_buf.at[d], n), kv_send.at[d, n])


def gather(frames, shift, scale, gate, mask, wq, wk, wv, wo, query_gain, key_gain):
    rows, width = frames.shape
    tokens = rows * 4
    pair = 2 * HDIM
    vmem, hbm = pl.BlockSpec(memory_space=pltpu.VMEM), pl.BlockSpec(memory_space=pl.ANY)
    dma = pltpu.SemaphoreType.DMA
    return pl.pallas_call(
        gather_kernel,
        in_specs=[vmem, vmem, vmem, vmem, vmem, hbm, hbm, hbm, hbm, vmem, vmem],
        out_specs=[hbm, hbm, vmem, hbm, vmem, hbm],
        out_shape=[
            jax.ShapeDtypeStruct((PLACES, tokens // 2, pair), jnp.bfloat16),
            jax.ShapeDtypeStruct((NZ, PLACES, tokens, pair), jnp.bfloat16),
            jax.ShapeDtypeStruct((PLACES, 128), jnp.int32),
            jax.ShapeDtypeStruct(frames.shape, jnp.bfloat16),
            jax.ShapeDtypeStruct(gate.shape, jnp.float32),
            jax.ShapeDtypeStruct((4,) + wo.shape, jnp.bfloat16),
        ],
        scratch_shapes=[
            pltpu.VMEM((tokens, width), jnp.bfloat16),
            pltpu.VMEM(wq.shape, jnp.bfloat16),
            pltpu.VMEM((HEADS_HERE // 2, width, 2 * pair), jnp.bfloat16),
            pltpu.VMEM((HEADS_HERE, tokens // 2, pair), jnp.bfloat16),
            pltpu.VMEM((HEADS_HERE, tokens, pair), jnp.bfloat16),
            pltpu.VMEM((8, 128), jnp.int32),
            pltpu.VMEM((PLACES, 8, 128), jnp.int32),
            dma,
            dma((HEADS_HERE // 2, 2)),
            dma((3, CHUNKS)),
            dma((3, CHUNKS)),
            dma((PLACES,)),
            dma((PLACES,)),
            dma((HEADS_HERE, 2)),
            dma((PLACES, 2)),
            dma((HEADS_HERE,)),
            dma((PLACES,)),
            dma((2, NZ // 2, 2, PLACES)),
            dma((2, NZ // 2, 2, PLACES)),
            dma((2,)),
            dma((2,)),
            dma((1 + 2 * PIECES,)),
            dma((1 + 2 * PIECES,)),
            dma,
        ],
        compiler_params=pltpu.CompilerParams(
            collective_id=0, has_side_effects=True, vmem_limit_bytes=52 * 1024 * 1024
        ),
    )(frames, shift, scale, gate, mask, wq, wk, wv, wo, query_gain.reshape(1, HDIM), key_gain.reshape(1, HDIM))


def attend_kernel(info_ref, q_ref, kv_ref, out_ref):
    frames_here, half, lanes = q_ref.shape
    rows = 2 * half
    slots = kv_ref.shape[0]
    low = lax.broadcasted_iota(jnp.int32, (half, lanes), 1) < HDIM

    def one_frame(i, _):
        packed = q_ref[i].astype(jnp.float32)
        top = jnp.where(low, packed, 0.0)
        bottom = jnp.where(low, pltpu.roll(packed, HDIM, 1), 0.0)
        q = jnp.concatenate([top, bottom], axis=0).astype(jnp.bfloat16)

        def blocks(state, *numbers):
            running_max, running_sum, weighted = state
            kvs = [kv_ref[info_ref[i, j]] for j in numbers]
            scores = [
                lax.dot_general(kv, q, (((1,), (1,)), ((), ())), preferred_element_type=jnp.float32) for kv in kvs
            ]
            new_max = running_max
            for s in scores:
                new_max = jnp.maximum(new_max, jnp.max(s, axis=0, keepdims=True))
            rescale = jnp.exp(running_max - new_max)
            running_sum, weighted = running_sum * rescale, weighted * rescale
            for kv, s in zip(kvs, scores):
                weights = jnp.exp(s - new_max)
                running_sum = running_sum + jnp.sum(weights, axis=0, keepdims=True)
                weighted = weighted + lax.dot_general(
                    kv, weights.astype(jnp.bfloat16), (((0,), (0,)), ((), ())), preferred_element_type=jnp.float32
                )
            return new_max, running_sum, weighted

        state = (
            jnp.full((1, rows), -1e30, jnp.float32),
            jnp.zeros((1, rows), jnp.float32),
            jnp.zeros((lanes, rows), jnp.float32),
        )
        count = info_ref[i, slots]
        twos = count // 2
        state = lax.fori_loop(0, twos, lambda j, s: blocks(s, 2 * j, 2 * j + 1), state)
        _, total, weighted = lax.fori_loop(2 * twos, count, lambda j, s: blocks(s, j), state)
        attended = jnp.transpose(weighted[HDIM:] / total)
        chunk = rows // 4
        for c in range(4):
            part = attended[c * chunk : (c + 1) * chunk]
            out_ref[i, c] = jnp.concatenate([part[: chunk // 2], part[chunk // 2 :]], axis=1).astype(jnp.bfloat16)
        return 0

    lax.fori_loop(0, frames_here, one_frame, 0)


def attend(info, q, kv):
    frames_here, half, lanes = q.shape
    return pl.pallas_call(
        attend_kernel,
        grid_spec=pltpu.PrefetchScalarGridSpec(
            num_scalar_prefetch=1,
            grid=(1,),
            in_specs=[pl.BlockSpec(memory_space=pltpu.VMEM)] * 2,
            out_specs=pl.BlockSpec((frames_here, 4, half // 4, lanes), lambda i, *_: (0, 0, 0, 0)),
        ),
        out_shape=jax.ShapeDtypeStruct((frames_here, 4, half // 4, lanes), jnp.bfloat16),
        compiler_params=pltpu.CompilerParams(vmem_limit_bytes=40 * 1024 * 1024),
    )(info, q, kv)


def finish_kernel(
    att_ref, w_ref, frames_ref, gate_ref, out_ref, got, att_buf, w_buf, w_sem, send_sem, recv_sem
):
    place, z, tok = positions()
    width = out_ref.shape[1]
    tile = width // TILES
    weights = [
        pltpu.make_async_copy(w_ref.at[:, pl.ds(n * tile, tile)], w_buf.at[n], w_sem.at[n]) for n in range(TILES)
    ]
    for copy in weights:
        copy.start()
    barrier = pltpu.get_barrier_semaphore()
    for p in range(PLACES):
        for t in range(4):
            @pl.when(jnp.logical_not(jnp.logical_and(p == place, t == tok)))
            def _():
                pl.semaphore_signal(barrier, inc=1, device_id=(queue_index(p, z), t), device_id_type=MESH)
    pl.semaphore_wait(barrier, 4 * PLACES - 1)

    slot = tok * HEADS_HERE + place

    @pl.when(place < HEADS_HERE)
    def _():
        for p in range(PLACES):
            for t in range(4):
                here = jnp.logical_and(p == place, t == tok)

                @pl.when(jnp.logical_not(here))
                def _():
                    send(att_ref.at[p, t], got.at[slot], send_sem.at[p, t], recv_sem.at[slot], p, z, t)

                @pl.when(here)
                def _():
                    pltpu.make_async_copy(att_ref.at[p, t], got.at[slot], recv_sem.at[slot]).start()

    heads, half, lanes = got.shape
    low = lax.broadcasted_iota(jnp.int32, (half, lanes), 1) < HDIM
    for m in range(heads // 2):
        landed(got.at[2 * m], recv_sem.at[2 * m])
        landed(got.at[2 * m + 1], recv_sem.at[2 * m + 1])
        first, second = got[2 * m].astype(jnp.float32), got[2 * m + 1].astype(jnp.float32)
        cols = slice(m * lanes, (m + 1) * lanes)
        att_buf[:half, cols] = jnp.where(low, first, pltpu.roll(second, HDIM, 1)).astype(jnp.bfloat16)
        att_buf[half:, cols] = jnp.where(low, pltpu.roll(first, HDIM, 1), second).astype(jnp.bfloat16)
    attended = att_buf[...]
    for n in range(TILES):
        weights[n].wait()
        projected = jnp.dot(attended, w_buf[n], preferred_element_type=jnp.float32)
        cols = slice(n * tile, (n + 1) * tile)
        updated = frames_ref[:, cols].astype(jnp.float32) + gate_ref[:, cols] * projected
        out_ref[:, cols] = updated.astype(jnp.bfloat16)

    @pl.when(place < HEADS_HERE)
    def _():
        for p in range(PLACES):
            for t in range(4):
                @pl.when(jnp.logical_not(jnp.logical_and(p == place, t == tok)))
                def _():
                    landed(att_ref.at[p, t], send_sem.at[p, t])


def finish(attended, w_full, frames, gate):
    vmem, hbm = pl.BlockSpec(memory_space=pltpu.VMEM), pl.BlockSpec(memory_space=pl.ANY)
    dma = pltpu.SemaphoreType.DMA
    depth, width = w_full.shape
    return pl.pallas_call(
        finish_kernel,
        in_specs=[hbm, hbm, vmem, vmem],
        out_specs=vmem,
        out_shape=jax.ShapeDtypeStruct(frames.shape, jnp.bfloat16),
        scratch_shapes=[
            pltpu.VMEM((4 * HEADS_HERE,) + attended.shape[2:], jnp.bfloat16),
            pltpu.VMEM((frames.shape[0], depth), jnp.bfloat16),
            pltpu.VMEM((TILES, depth, width // TILES), jnp.bfloat16),
            dma((TILES,)),
            dma((PLACES, 4)),
            dma((4 * HEADS_HERE,)),
        ],
        compiler_params=pltpu.CompilerParams(
            collective_id=1, has_side_effects=True, vmem_limit_bytes=48 * 1024 * 1024
        ),
    )(attended, w_full, frames, gate)


def body(
    frames, levels, frame_mask, modulation, w_query, w_key, w_value, w_out, query_gain, key_gain
):
    width = frames.shape[2]
    slots = frame_mask.shape[1]
    own = lax.dynamic_slice(modulation, (levels[0], 0), (1, 3 * width)).astype(jnp.float32)
    q, kv, info, prev_frames, prev_gate, w_all = gather(
        frames[0], own[:, :width], own[:, width : 2 * width], own[:, 2 * width :], frame_mask,
        w_query, w_key, w_value, w_out, query_gain, key_gain,
    )
    attended = attend(info, q, kv.reshape((slots,) + kv.shape[2:]))
    w_full = w_all.reshape(-1, width)
    return finish(attended, w_full, prev_frames, prev_gate)[None]


def solution(mesh):
    return jax.shard_map(
        body,
        mesh=mesh,
        in_specs=(
            P("queue", "tok", None),
            P("queue"),
            P("queue", None),
            P(),
            P(None, "tok"),
            P(None, "tok"),
            P(None, "tok"),
            P("tok", None),
            P(),
            P(),
        ),
        out_specs=P("queue", "tok", None),
        check_vma=False,
    )
```

```python
import jax
import jax.numpy as jnp
from jax import lax
from jax.experimental import pallas as pl
from jax.experimental.pallas import tpu as pltpu
from jax.sharding import PartitionSpec as P

HDIM = 64
NX, NZ, NYH = 4, 8, 2
PLACES = NX * NYH
HEADS_HERE = 6
CHUNKS = 4
TILES = 6
MESH = pl.DeviceIdType.MESH


def queue_index(place, z):
    return ((place // NYH) * NZ + z) * NYH + place % NYH


def layer_norm(values_in):
    center = jnp.mean(values_in, axis=-1, keepdims=True)
    spread = jnp.mean(jnp.square(values_in - center), axis=-1, keepdims=True)
    return (values_in - center) * lax.rsqrt(spread + 1e-06)


def positions():
    q_at = lax.axis_index("queue")
    return (q_at // (NZ * NYH)) * NYH + q_at % NYH, (q_at // NYH) % NZ, lax.axis_index("tok")


def send(src, dst, send_sem, recv_sem, place, z, tok):
    copy = pltpu.make_async_remote_copy(
        src_ref=src,
        dst_ref=dst,
        send_sem=send_sem,
        recv_sem=recv_sem,
        device_id=(queue_index(place, z), tok),
        device_id_type=MESH,
    )
    copy.start()
    return copy


def landed(ref, sem):
    pltpu.make_async_copy(ref, ref, sem).wait()


def gather_kernel(
    frames_ref, shift_ref, scale_ref, gate_ref, mask_ref, wq_ref, wk_ref, wv_ref, wo_ref, qg_ref, kg_ref,
    q_all, kv_all, info_ref, prev_frames, prev_gate, wo_all,
    x_buf, wq_buf, wkv_buf, q_buf, kv_buf, row_buf, rows_got,
    wq_sem, wkv_sem, tok_send, tok_recv, row_send, row_recv, kv_send, kv_recv, q_send, q_recv,
    ring_send, ring_recv, prev_send, prev_recv, wo_send, wo_recv, wo_own,
):
    place, z, tok = positions()
    up, down = lax.rem(z + 1, NZ), lax.rem(z + NZ - 1, NZ)
    sibling = tok + 1 - 2 * lax.rem(tok, 2)
    across = lax.rem(tok + 2, 4)
    sibling_across = lax.rem(sibling + 2, 4)
    pair = 2 * HDIM
    pairs = HEADS_HERE // 2
    weights = []
    for i in range(pairs):
        for j, w in enumerate((wk_ref, wv_ref)):
            weights.append(
                pltpu.make_async_copy(
                    w.at[:, pl.ds(i * pair, pair)], wkv_buf.at[i, :, pl.ds(j * pair, pair)], wkv_sem.at[i, j]
                )
            )
    weights.append(pltpu.make_async_copy(wq_ref, wq_buf, wq_sem))
    for copy in weights:
        copy.start()
    own_block = pltpu.make_async_copy(wo_ref, wo_all.at[tok], wo_own)
    twin = place + 1 - 2 * lax.rem(place, NYH)

    barrier = pltpu.get_barrier_semaphore()
    for other_tok in (sibling, across):
        pl.semaphore_signal(
            barrier, inc=1, device_id=(queue_index(place, z), other_tok), device_id_type=MESH
        )
    pl.semaphore_signal(barrier, inc=1, device_id=(queue_index(twin, z), across), device_id_type=MESH)
    for p in range(PLACES):
        for other_z in (up, down):
            pl.semaphore_signal(barrier, inc=1, device_id=(queue_index(p, other_z), tok), device_id_type=MESH)

        @pl.when(p != place)
        def _():
            pl.semaphore_signal(barrier, inc=1, device_id=(queue_index(p, z), tok), device_id_type=MESH)

    rows = frames_ref.shape[0]
    step = rows // CHUNKS

    def x_rows(owner, c):
        return x_buf.at[pl.ds(pl.multiple_of(owner * rows + c * step, step), step)]

    started = []
    for c in range(CHUNKS):
        part = layer_norm(frames_ref[c * step : (c + 1) * step].astype(jnp.float32))
        part = part * (1.0 + scale_ref[...]) + shift_ref[...]
        x_buf[pl.ds(pl.multiple_of(tok * rows + c * step, step), step)] = part.astype(jnp.bfloat16)
        if c == 0:
            pl.semaphore_wait(barrier, 3 + 3 * PLACES - 1)
        for way, other_tok in ((1, across), (0, sibling)):
            mine = x_rows(tok, c)
            started.append(send(mine, mine, tok_send.at[way, c], tok_recv.at[way, c], place, z, other_tok))

    after = lax.rem(queue_index(place, z) + 1, NX * NZ * NYH)
    after_place = (after // (NZ * NYH)) * NYH + after % NYH
    after_z = (after // NYH) % NZ
    slots = mask_ref.shape[1]
    row_buf[...] = jnp.zeros_like(row_buf)
    row_buf[0:1, :slots] = mask_ref[...]
    for d in range(PLACES):
        stays = jnp.logical_and(d == place, after_z == z)

        @pl.when(jnp.logical_not(stays))
        def _():
            send(row_buf, rows_got.at[after_place], row_send.at[d], row_recv.at[after_place], d, after_z, tok)

        @pl.when(stays)
        def _():
            pltpu.make_async_copy(row_buf, rows_got.at[after_place], row_recv.at[after_place]).start()

    started.append(
        send(gate_ref, prev_gate, prev_send.at[0], prev_recv.at[0], after_place, after_z, tok)
    )

    half = x_buf.shape[0] // 2
    first = tok // 2
    at = [pl.multiple_of(first * half, half), pl.multiple_of((1 - first) * half, half)]

    def part_of(ref, n):
        return ref.at[pl.ds(at[n], half)]

    def keys_values(n):
        x = x_buf[pl.ds(at[n], half)]
        for i in range(pairs):
            if n == 0:
                weights[2 * i].wait()
                weights[2 * i + 1].wait()
            both = jnp.dot(x, wkv_buf[i], preferred_element_type=jnp.float32)
            for j in range(2):
                d = 2 * i + j
                kn = layer_norm(both[:, j * HDIM : (j + 1) * HDIM]) * kg_ref[...]
                v = both[:, pair + j * HDIM : pair + (j + 1) * HDIM]
                kv_buf[d, pl.ds(at[n], half)] = jnp.concatenate([kn, v], axis=1).astype(jnp.bfloat16)
                block = part_of(kv_buf.at[d], n)
                here = part_of(kv_all.at[z, place], n)

                @pl.when(d != place)
                def _():
                    send(block, here, kv_send.at[d, n], kv_recv.at[place, n], d, z, tok)

                @pl.when(d == place)
                def _():
                    pltpu.make_async_copy(block, here, kv_recv.at[place, n]).start()

    last = NZ // 2

    def ring_copy(hop, way, n, c):
        source = lax.rem(z + NZ - (hop - 1), NZ) if way == 0 else lax.rem(z + hop - 1, NZ)
        block = part_of(kv_all.at[source, c], n)
        return pltpu.make_async_remote_copy(
            src_ref=block,
            dst_ref=block,
            send_sem=ring_send.at[way, hop - 1, n, c],
            recv_sem=ring_recv.at[way, hop - 1, n, c],
            device_id=(queue_index(place, down if way else up), tok),
            device_id_type=MESH,
        )

    def goes(hop, way, c):
        return hop < last or (c < PLACES // 2) == (way == 0)

    def pass_on(hop, n):
        @pl.when(place < HEADS_HERE)
        def _():
            for c in range(PLACES):
                if hop == 1:
                    landed(part_of(kv_all.at[z, c], n), kv_recv.at[c, n])
                for way in range(2):
                    if hop > 1:
                        source = lax.rem(z + NZ - (hop - 1), NZ) if way == 0 else lax.rem(z + hop - 1, NZ)
                        landed(part_of(kv_all.at[source, c], n), ring_recv.at[way, hop - 2, n, c])
                    if goes(hop, way, c):
                        ring_copy(hop, way, n, c).start()

    rows_here = wo_ref.shape[0]
    quarter = rows_here // NX
    x_at = place // NYH
    x_next = lax.rem(place + NYH, PLACES)
    x_before = lax.rem(place + PLACES - NYH, PLACES)
    lower = tok // 2 == 0
    y_next = jnp.where(lower, place, twin)
    y_before = jnp.where(lower, twin, place)

    def part_rows(owner, shift, side):
        start = lax.rem(x_at + shift + NX, NX) * quarter
        if side is None:
            return wo_all.at[owner, pl.ds(pl.multiple_of(start, 16), quarter)]
        return wo_all.at[owner, pl.ds(pl.multiple_of(start + side * (quarter // 2), 16), quarter // 2)]

    def y_quarter():
        for side, target in ((0, y_next), (1, y_before)):
            start = pl.multiple_of(x_at * quarter + side * (quarter // 2), 16)
            part = wo_ref.at[pl.ds(start, quarter // 2)]
            started.append(
                send(part, part_rows(tok, 0, side), wo_send.at[side], wo_recv.at[side], target, z, across)
            )

    def x_ring_first():
        for side in range(2):
            landed(part_rows(across, 0, side), wo_recv.at[side])
        mine = part_rows(across, 0, None)
        for k, target in ((2, x_next), (3, x_before)):
            started.append(send(mine, mine, wo_send.at[k], wo_recv.at[k], target, z, tok))

    def x_ring_second():
        for k, shift, side, target in ((4, -1, 0, x_next), (5, 1, 1, x_before)):
            landed(part_rows(across, shift, None), wo_recv.at[k - 2])
            half_part = part_rows(across, shift, side)
            started.append(send(half_part, half_part, wo_send.at[k], wo_recv.at[k], target, z, tok))

    def share(k, block):
        started.append(send(block, block, wo_send.at[k], wo_recv.at[k], place, z, sibling))

    for c in range(CHUNKS):
        landed(x_rows(sibling, c), tok_recv.at[0, c])
    keys_values(0)
    pass_on(1, 0)
    for c in range(CHUNKS):
        theirs = x_rows(across, c)
        landed(theirs, tok_recv.at[1, c])
        started.append(send(theirs, theirs, tok_send.at[2, c], tok_recv.at[2, c], place, z, sibling))
    y_quarter()
    for c in range(CHUNKS):
        landed(x_rows(sibling_across, c), tok_recv.at[2, c])
    keys_values(1)
    pass_on(1, 1)

    own_block.start()
    started.append(send(wo_ref, wo_all.at[tok], wo_send.at[6], wo_recv.at[6], place, z, sibling))
    x_ring_first()

    weights[-1].wait()
    x = x_buf[...]
    for i in range(pairs):
        q = jnp.dot(x, wq_buf[:, i * pair : (i + 1) * pair], preferred_element_type=jnp.float32)
        for j in range(2):
            d = 2 * i + j
            qn = layer_norm(q[:, j * HDIM : (j + 1) * HDIM]) * qg_ref[...]
            qn = qn.astype(jnp.bfloat16).astype(jnp.float32) * HDIM ** (-0.5)
            q_buf[d] = jnp.concatenate([qn[:half], qn[half:]], axis=1).astype(jnp.bfloat16)
            stays = jnp.logical_and(d == place, after_z == z)

            @pl.when(jnp.logical_not(stays))
            def _():
                send(
                    q_buf.at[d], q_all.at[after_place], q_send.at[d], q_recv.at[after_place], d, after_z, tok
                )

            @pl.when(stays)
            def _():
                pltpu.make_async_copy(q_buf.at[d], q_all.at[after_place], q_recv.at[after_place]).start()

    started.append(
        send(frames_ref, prev_frames, prev_send.at[1], prev_recv.at[1], after_place, after_z, tok)
    )
    for hop in range(2, last + 1):
        for n in range(2):
            pass_on(hop, n)
        if hop == 2:
            share(7, part_rows(across, 0, None))
            x_ring_second()
        elif hop == 3:
            share(8, part_rows(across, -1, None))
            share(9, part_rows(across, 1, None))
    for k in (4, 5):
        landed(part_rows(across, 2, k - 4), wo_recv.at[k])
    share(10, part_rows(across, 2, None))

    for p in range(PLACES):
        landed(rows_got.at[p], row_recv.at[p])
    table = rows_got[:, 0, :]
    lanes = table.shape[1]
    lane = lax.broadcasted_iota(jnp.int32, (PLACES, lanes), 1)
    seen = jnp.where(jnp.logical_and(table > 0, lane < slots), 1.0, 0.0)
    by_row = lax.broadcasted_iota(jnp.int32, (lanes, lanes), 0)
    by_lane = lax.broadcasted_iota(jnp.int32, (lanes, lanes), 1)
    ahead = jnp.where(by_row < by_lane, 1.0, 0.0)
    rank = jnp.dot(seen, ahead, preferred_element_type=jnp.float32)
    spot = jnp.where(seen > 0, rank, -1.0)
    spot_t = jnp.transpose(jnp.concatenate([spot] * (lanes // PLACES), axis=0))
    kept_at = ((by_row >> 1) & (NZ - 1)) * PLACES + (by_row >> 4) * NYH + (by_row & 1)
    kept_at = kept_at.astype(jnp.float32)
    lane_f = by_lane.astype(jnp.float32)
    listed = [
        jnp.sum(jnp.where(spot_t[:, p : p + 1] == lane_f, kept_at, 0.0), axis=0, keepdims=True)
        for p in range(PLACES)
    ]
    listed = jnp.concatenate(listed, axis=0).astype(jnp.int32)
    count = jnp.sum(seen, axis=1, keepdims=True).astype(jnp.int32)
    count = jnp.where(place < HEADS_HERE, count, 0)
    info_ref[...] = jnp.where(lane == slots, count, listed)

    @pl.when(place < HEADS_HERE)
    def _():
        opposite = lax.rem(z + last, NZ)
        for n in range(2):
            for c in range(PLACES):
                way = 0 if c < PLACES // 2 else 1
                landed(part_of(kv_all.at[opposite, c], n), ring_recv.at[way, last - 1, n, c])
        for p in range(PLACES):
            landed(q_all.at[p], q_recv.at[p])
        for hop in range(1, last + 1):
            for n in range(2):
                for c in range(PLACES):
                    for way in range(2):
                        if goes(hop, way, c):
                            ring_copy(hop, way, n, c).wait_send()

    landed(prev_gate, prev_recv.at[0])
    landed(prev_frames, prev_recv.at[1])
    own_block.wait()
    landed(wo_all.at[sibling], wo_recv.at[6])
    for k, shift in ((7, 0), (8, -1), (9, 1), (10, 2)):
        landed(part_rows(sibling_across, shift, None), wo_recv.at[k])
    for copy in started:
        copy.wait_send()
    for d in range(PLACES):
        @pl.when(jnp.logical_not(jnp.logical_and(d == place, after_z == z)))
        def _():
            landed(row_buf, row_send.at[d])
            if d < HEADS_HERE:
                landed(q_buf.at[d], q_send.at[d])

    for d in range(HEADS_HERE):
        for n in range(2):
            @pl.when(d != place)
            def _():
                landed(part_of(kv_buf.at[d], n), kv_send.at[d, n])


def gather(frames, shift, scale, gate, mask, wq, wk, wv, wo, query_gain, key_gain):
    rows, width = frames.shape
    tokens = rows * 4
    pair = 2 * HDIM
    vmem, hbm = pl.BlockSpec(memory_space=pltpu.VMEM), pl.BlockSpec(memory_space=pl.ANY)
    dma = pltpu.SemaphoreType.DMA
    return pl.pallas_call(
        gather_kernel,
        in_specs=[vmem, vmem, vmem, vmem, vmem, hbm, hbm, hbm, hbm, vmem, vmem],
        out_specs=[hbm, hbm, vmem, hbm, vmem, hbm],
        out_shape=[
            jax.ShapeDtypeStruct((PLACES, tokens // 2, pair), jnp.bfloat16),
            jax.ShapeDtypeStruct((NZ, PLACES, tokens, pair), jnp.bfloat16),
            jax.ShapeDtypeStruct((PLACES, 128), jnp.int32),
            jax.ShapeDtypeStruct(frames.shape, jnp.bfloat16),
            jax.ShapeDtypeStruct(gate.shape, jnp.float32),
            jax.ShapeDtypeStruct((4,) + wo.shape, jnp.bfloat16),
        ],
        scratch_shapes=[
            pltpu.VMEM((tokens, width), jnp.bfloat16),
            pltpu.VMEM(wq.shape, jnp.bfloat16),
            pltpu.VMEM((HEADS_HERE // 2, width, 2 * pair), jnp.bfloat16),
            pltpu.VMEM((HEADS_HERE, tokens // 2, pair), jnp.bfloat16),
            pltpu.VMEM((HEADS_HERE, tokens, pair), jnp.bfloat16),
            pltpu.VMEM((8, 128), jnp.int32),
            pltpu.VMEM((PLACES, 8, 128), jnp.int32),
            dma,
            dma((HEADS_HERE // 2, 2)),
            dma((3, CHUNKS)),
            dma((3, CHUNKS)),
            dma((PLACES,)),
            dma((PLACES,)),
            dma((HEADS_HERE, 2)),
            dma((PLACES, 2)),
            dma((HEADS_HERE,)),
            dma((PLACES,)),
            dma((2, NZ // 2, 2, PLACES)),
            dma((2, NZ // 2, 2, PLACES)),
            dma((2,)),
            dma((2,)),
            dma((11,)),
            dma((11,)),
            dma,
        ],
        compiler_params=pltpu.CompilerParams(
            collective_id=0, has_side_effects=True, vmem_limit_bytes=52 * 1024 * 1024
        ),
    )(frames, shift, scale, gate, mask, wq, wk, wv, wo, query_gain.reshape(1, HDIM), key_gain.reshape(1, HDIM))


def attend_kernel(info_ref, q_ref, kv_ref, out_ref):
    frames_here, half, lanes = q_ref.shape
    rows = 2 * half
    slots = kv_ref.shape[0]
    low = lax.broadcasted_iota(jnp.int32, (half, lanes), 1) < HDIM

    def one_frame(i, _):
        packed = q_ref[i].astype(jnp.float32)
        top = jnp.where(low, packed, 0.0)
        bottom = jnp.where(low, pltpu.roll(packed, HDIM, 1), 0.0)
        q = jnp.concatenate([top, bottom], axis=0).astype(jnp.bfloat16)

        def blocks(state, *numbers):
            running_max, running_sum, weighted = state
            kvs = [kv_ref[info_ref[i, j]] for j in numbers]
            scores = [
                lax.dot_general(kv, q, (((1,), (1,)), ((), ())), preferred_element_type=jnp.float32) for kv in kvs
            ]
            new_max = running_max
            for s in scores:
                new_max = jnp.maximum(new_max, jnp.max(s, axis=0, keepdims=True))
            rescale = jnp.exp(running_max - new_max)
            running_sum, weighted = running_sum * rescale, weighted * rescale
            for kv, s in zip(kvs, scores):
                weights = jnp.exp(s - new_max)
                running_sum = running_sum + jnp.sum(weights, axis=0, keepdims=True)
                weighted = weighted + lax.dot_general(
                    kv, weights.astype(jnp.bfloat16), (((0,), (0,)), ((), ())), preferred_element_type=jnp.float32
                )
            return new_max, running_sum, weighted

        state = (
            jnp.full((1, rows), -1e30, jnp.float32),
            jnp.zeros((1, rows), jnp.float32),
            jnp.zeros((lanes, rows), jnp.float32),
        )
        count = info_ref[i, slots]
        twos = count // 2
        state = lax.fori_loop(0, twos, lambda j, s: blocks(s, 2 * j, 2 * j + 1), state)
        _, total, weighted = lax.fori_loop(2 * twos, count, lambda j, s: blocks(s, j), state)
        attended = jnp.transpose(weighted[HDIM:] / total)
        chunk = rows // 4
        for c in range(4):
            part = attended[c * chunk : (c + 1) * chunk]
            out_ref[i, c] = jnp.concatenate([part[: chunk // 2], part[chunk // 2 :]], axis=1).astype(jnp.bfloat16)
        return 0

    lax.fori_loop(0, frames_here, one_frame, 0)


def attend(info, q, kv):
    frames_here, half, lanes = q.shape
    return pl.pallas_call(
        attend_kernel,
        grid_spec=pltpu.PrefetchScalarGridSpec(
            num_scalar_prefetch=1,
            grid=(1,),
            in_specs=[pl.BlockSpec(memory_space=pltpu.VMEM)] * 2,
            out_specs=pl.BlockSpec((frames_here, 4, half // 4, lanes), lambda i, *_: (0, 0, 0, 0)),
        ),
        out_shape=jax.ShapeDtypeStruct((frames_here, 4, half // 4, lanes), jnp.bfloat16),
        compiler_params=pltpu.CompilerParams(vmem_limit_bytes=40 * 1024 * 1024),
    )(info, q, kv)


def finish_kernel(
    att_ref, w_ref, frames_ref, gate_ref, out_ref, got, att_buf, w_buf, w_sem, send_sem, recv_sem
):
    place, z, tok = positions()
    width = out_ref.shape[1]
    tile = width // TILES
    weights = [
        pltpu.make_async_copy(w_ref.at[:, pl.ds(n * tile, tile)], w_buf.at[n], w_sem.at[n]) for n in range(TILES)
    ]
    for copy in weights:
        copy.start()
    barrier = pltpu.get_barrier_semaphore()
    for p in range(PLACES):
        for t in range(4):
            @pl.when(jnp.logical_not(jnp.logical_and(p == place, t == tok)))
            def _():
                pl.semaphore_signal(barrier, inc=1, device_id=(queue_index(p, z), t), device_id_type=MESH)
    pl.semaphore_wait(barrier, 4 * PLACES - 1)

    slot = tok * HEADS_HERE + place

    @pl.when(place < HEADS_HERE)
    def _():
        for p in range(PLACES):
            for t in range(4):
                here = jnp.logical_and(p == place, t == tok)

                @pl.when(jnp.logical_not(here))
                def _():
                    send(att_ref.at[p, t], got.at[slot], send_sem.at[p, t], recv_sem.at[slot], p, z, t)

                @pl.when(here)
                def _():
                    pltpu.make_async_copy(att_ref.at[p, t], got.at[slot], recv_sem.at[slot]).start()

    heads, half, lanes = got.shape
    low = lax.broadcasted_iota(jnp.int32, (half, lanes), 1) < HDIM
    for m in range(heads // 2):
        landed(got.at[2 * m], recv_sem.at[2 * m])
        landed(got.at[2 * m + 1], recv_sem.at[2 * m + 1])
        first, second = got[2 * m].astype(jnp.float32), got[2 * m + 1].astype(jnp.float32)
        cols = slice(m * lanes, (m + 1) * lanes)
        att_buf[:half, cols] = jnp.where(low, first, pltpu.roll(second, HDIM, 1)).astype(jnp.bfloat16)
        att_buf[half:, cols] = jnp.where(low, pltpu.roll(first, HDIM, 1), second).astype(jnp.bfloat16)
    attended = att_buf[...]
    for n in range(TILES):
        weights[n].wait()
        projected = jnp.dot(attended, w_buf[n], preferred_element_type=jnp.float32)
        cols = slice(n * tile, (n + 1) * tile)
        updated = frames_ref[:, cols].astype(jnp.float32) + gate_ref[:, cols] * projected
        out_ref[:, cols] = updated.astype(jnp.bfloat16)

    @pl.when(place < HEADS_HERE)
    def _():
        for p in range(PLACES):
            for t in range(4):
                @pl.when(jnp.logical_not(jnp.logical_and(p == place, t == tok)))
                def _():
                    landed(att_ref.at[p, t], send_sem.at[p, t])


def finish(attended, w_full, frames, gate):
    vmem, hbm = pl.BlockSpec(memory_space=pltpu.VMEM), pl.BlockSpec(memory_space=pl.ANY)
    dma = pltpu.SemaphoreType.DMA
    depth, width = w_full.shape
    return pl.pallas_call(
        finish_kernel,
        in_specs=[hbm, hbm, vmem, vmem],
        out_specs=vmem,
        out_shape=jax.ShapeDtypeStruct(frames.shape, jnp.bfloat16),
        scratch_shapes=[
            pltpu.VMEM((4 * HEADS_HERE,) + attended.shape[2:], jnp.bfloat16),
            pltpu.VMEM((frames.shape[0], depth), jnp.bfloat16),
            pltpu.VMEM((TILES, depth, width // TILES), jnp.bfloat16),
            dma((TILES,)),
            dma((PLACES, 4)),
            dma((4 * HEADS_HERE,)),
        ],
        compiler_params=pltpu.CompilerParams(
            collective_id=1, has_side_effects=True, vmem_limit_bytes=48 * 1024 * 1024
        ),
    )(attended, w_full, frames, gate)


def body(
    frames, levels, frame_mask, modulation, w_query, w_key, w_value, w_out, query_gain, key_gain
):
    width = frames.shape[2]
    slots = frame_mask.shape[1]
    own = lax.dynamic_slice(modulation, (levels[0], 0), (1, 3 * width)).astype(jnp.float32)
    q, kv, info, prev_frames, prev_gate, w_all = gather(
        frames[0], own[:, :width], own[:, width : 2 * width], own[:, 2 * width :], frame_mask,
        w_query, w_key, w_value, w_out, query_gain, key_gain,
    )
    attended = attend(info, q, kv.reshape((slots,) + kv.shape[2:]))
    w_full = w_all.reshape(-1, width)
    return finish(attended, w_full, prev_frames, prev_gate)[None]


def solution(mesh):
    return jax.shard_map(
        body,
        mesh=mesh,
        in_specs=(
            P("queue", "tok", None),
            P("queue"),
            P("queue", None),
            P(),
            P(None, "tok"),
            P(None, "tok"),
            P(None, "tok"),
            P("tok", None),
            P(),
            P(),
        ),
        out_specs=P("queue", "tok", None),
        check_vma=False,
    )
```

```python
import jax
import jax.numpy as jnp
from jax import lax
from jax.experimental import pallas as pl
from jax.experimental.pallas import tpu as pltpu
from jax.sharding import PartitionSpec as P

HDIM = 64
NX, NZ, NYH = 4, 8, 2
PLACES = NX * NYH
HEADS_HERE = 6
CHUNKS = 4
TILES = 6
MESH = pl.DeviceIdType.MESH


def queue_index(place, z):
    return ((place // NYH) * NZ + z) * NYH + place % NYH


def layer_norm(values_in):
    center = jnp.mean(values_in, axis=-1, keepdims=True)
    spread = jnp.mean(jnp.square(values_in - center), axis=-1, keepdims=True)
    return (values_in - center) * lax.rsqrt(spread + 1e-06)


def positions():
    q_at = lax.axis_index("queue")
    return (q_at // (NZ * NYH)) * NYH + q_at % NYH, (q_at // NYH) % NZ, lax.axis_index("tok")


def send(src, dst, send_sem, recv_sem, place, z, tok):
    copy = pltpu.make_async_remote_copy(
        src_ref=src,
        dst_ref=dst,
        send_sem=send_sem,
        recv_sem=recv_sem,
        device_id=(queue_index(place, z), tok),
        device_id_type=MESH,
    )
    copy.start()
    return copy


def landed(ref, sem):
    pltpu.make_async_copy(ref, ref, sem).wait()


def gather_kernel(
    frames_ref, shift_ref, scale_ref, gate_ref, mask_ref, wq_ref, wk_ref, wv_ref, wo_ref, qg_ref, kg_ref,
    q_all, kv_all, info_ref, prev_frames, prev_gate, wo_all,
    x_buf, wq_buf, wkv_buf, q_buf, kv_buf, row_buf, rows_got,
    wq_sem, wkv_sem, tok_send, tok_recv, row_send, row_recv, kv_send, kv_recv, q_send, q_recv,
    ring_send, ring_recv, prev_send, prev_recv, wo_send, wo_recv,
):
    place, z, tok = positions()
    up, down = lax.rem(z + 1, NZ), lax.rem(z + NZ - 1, NZ)
    sibling = tok + 1 - 2 * lax.rem(tok, 2)
    across = lax.rem(tok + 2, 4)
    sibling_across = lax.rem(sibling + 2, 4)
    pair = 2 * HDIM
    pairs = HEADS_HERE // 2
    weights = []
    for i in range(pairs):
        for j, w in enumerate((wk_ref, wv_ref)):
            weights.append(
                pltpu.make_async_copy(
                    w.at[:, pl.ds(i * pair, pair)], wkv_buf.at[i, :, pl.ds(j * pair, pair)], wkv_sem.at[i, j]
                )
            )
    weights.append(pltpu.make_async_copy(wq_ref, wq_buf, wq_sem))
    for copy in weights:
        copy.start()
    twin = place + 1 - 2 * lax.rem(place, NYH)

    barrier = pltpu.get_barrier_semaphore()
    for other_tok in (sibling, across):
        pl.semaphore_signal(
            barrier, inc=1, device_id=(queue_index(place, z), other_tok), device_id_type=MESH
        )
    pl.semaphore_signal(barrier, inc=1, device_id=(queue_index(twin, z), across), device_id_type=MESH)
    for p in range(PLACES):
        for other_z in (up, down):
            pl.semaphore_signal(barrier, inc=1, device_id=(queue_index(p, other_z), tok), device_id_type=MESH)

        @pl.when(p != place)
        def _():
            pl.semaphore_signal(barrier, inc=1, device_id=(queue_index(p, z), tok), device_id_type=MESH)

    rows = frames_ref.shape[0]
    step = rows // CHUNKS

    def x_rows(owner, c):
        return x_buf.at[pl.ds(pl.multiple_of(owner * rows + c * step, step), step)]

    started = []
    for c in range(CHUNKS):
        part = layer_norm(frames_ref[c * step : (c + 1) * step].astype(jnp.float32))
        part = part * (1.0 + scale_ref[...]) + shift_ref[...]
        x_buf[pl.ds(pl.multiple_of(tok * rows + c * step, step), step)] = part.astype(jnp.bfloat16)
        if c == 0:
            pl.semaphore_wait(barrier, 3 + 3 * PLACES - 1)
        for way, other_tok in ((1, across), (0, sibling)):
            mine = x_rows(tok, c)
            started.append(send(mine, mine, tok_send.at[way, c], tok_recv.at[way, c], place, z, other_tok))

    after = lax.rem(queue_index(place, z) + 1, NX * NZ * NYH)
    after_place = (after // (NZ * NYH)) * NYH + after % NYH
    after_z = (after // NYH) % NZ
    slots = mask_ref.shape[1]
    row_buf[...] = jnp.zeros_like(row_buf)
    row_buf[0:1, :slots] = mask_ref[...]
    for d in range(PLACES):
        stays = jnp.logical_and(d == place, after_z == z)

        @pl.when(jnp.logical_not(stays))
        def _():
            send(row_buf, rows_got.at[after_place], row_send.at[d], row_recv.at[after_place], d, after_z, tok)

        @pl.when(stays)
        def _():
            pltpu.make_async_copy(row_buf, rows_got.at[after_place], row_recv.at[after_place]).start()

    started.append(
        send(gate_ref, prev_gate, prev_send.at[0], prev_recv.at[0], after_place, after_z, tok)
    )

    half = x_buf.shape[0] // 2
    first = tok // 2
    at = [pl.multiple_of(first * half, half), pl.multiple_of((1 - first) * half, half)]

    def part_of(ref, n):
        return ref.at[pl.ds(at[n], half)]

    def keys_values(n):
        x = x_buf[pl.ds(at[n], half)]
        for i in range(pairs):
            if n == 0:
                weights[2 * i].wait()
                weights[2 * i + 1].wait()
            both = jnp.dot(x, wkv_buf[i], preferred_element_type=jnp.float32)
            for j in range(2):
                d = 2 * i + j
                kn = layer_norm(both[:, j * HDIM : (j + 1) * HDIM]) * kg_ref[...]
                v = both[:, pair + j * HDIM : pair + (j + 1) * HDIM]
                kv_buf[d, pl.ds(at[n], half)] = jnp.concatenate([kn, v], axis=1).astype(jnp.bfloat16)
                block = part_of(kv_buf.at[d], n)
                here = part_of(kv_all.at[z, place], n)

                @pl.when(d != place)
                def _():
                    send(block, here, kv_send.at[d, n], kv_recv.at[place, n], d, z, tok)

                @pl.when(d == place)
                def _():
                    pltpu.make_async_copy(block, here, kv_recv.at[place, n]).start()

    last = NZ // 2

    def ring_copy(hop, way, n, c):
        source = lax.rem(z + NZ - (hop - 1), NZ) if way == 0 else lax.rem(z + hop - 1, NZ)
        block = part_of(kv_all.at[source, c], n)
        return pltpu.make_async_remote_copy(
            src_ref=block,
            dst_ref=block,
            send_sem=ring_send.at[way, hop - 1, n, c],
            recv_sem=ring_recv.at[way, hop - 1, n, c],
            device_id=(queue_index(place, down if way else up), tok),
            device_id_type=MESH,
        )

    def goes(hop, way, c):
        return hop < last or (c < PLACES // 2) == (way == 0)

    def pass_on(hop, n):
        @pl.when(place < HEADS_HERE)
        def _():
            for c in range(PLACES):
                if hop == 1:
                    landed(part_of(kv_all.at[z, c], n), kv_recv.at[c, n])
                for way in range(2):
                    if hop > 1:
                        source = lax.rem(z + NZ - (hop - 1), NZ) if way == 0 else lax.rem(z + hop - 1, NZ)
                        landed(part_of(kv_all.at[source, c], n), ring_recv.at[way, hop - 2, n, c])
                    if goes(hop, way, c):
                        ring_copy(hop, way, n, c).start()

    rows_here = wo_ref.shape[0]
    quarter = rows_here // NX
    x_at = place // NYH
    x_next = lax.rem(place + NYH, PLACES)
    x_before = lax.rem(place + PLACES - NYH, PLACES)
    lower = tok // 2 == 0
    y_next = jnp.where(lower, place, twin)
    y_before = jnp.where(lower, twin, place)

    def part_rows(owner, shift, side):
        start = lax.rem(x_at + shift + NX, NX) * quarter
        if side is None:
            return wo_all.at[owner, pl.ds(pl.multiple_of(start, 16), quarter)]
        return wo_all.at[owner, pl.ds(pl.multiple_of(start + side * (quarter // 2), 16), quarter // 2)]

    def y_quarter():
        for side, target in ((0, y_next), (1, y_before)):
            start = pl.multiple_of(x_at * quarter + side * (quarter // 2), 16)
            part = wo_ref.at[pl.ds(start, quarter // 2)]
            started.append(
                send(part, part_rows(tok, 0, side), wo_send.at[side], wo_recv.at[side], target, z, across)
            )

    def x_ring_first():
        for side in range(2):
            landed(part_rows(across, 0, side), wo_recv.at[side])
        mine = part_rows(across, 0, None)
        for k, target in ((2, x_next), (3, x_before)):
            started.append(send(mine, mine, wo_send.at[k], wo_recv.at[k], target, z, tok))

    def x_ring_second():
        for k, shift, side, target in ((4, -1, 0, x_next), (5, 1, 1, x_before)):
            landed(part_rows(across, shift, None), wo_recv.at[k - 2])
            half_part = part_rows(across, shift, side)
            started.append(send(half_part, half_part, wo_send.at[k], wo_recv.at[k], target, z, tok))

    def share(k, block):
        started.append(send(block, block, wo_send.at[k], wo_recv.at[k], place, z, sibling))

    for c in range(CHUNKS):
        landed(x_rows(sibling, c), tok_recv.at[0, c])
    keys_values(0)
    pass_on(1, 0)
    for c in range(CHUNKS):
        theirs = x_rows(across, c)
        landed(theirs, tok_recv.at[1, c])
        started.append(send(theirs, theirs, tok_send.at[2, c], tok_recv.at[2, c], place, z, sibling))
    y_quarter()
    for c in range(CHUNKS):
        landed(x_rows(sibling_across, c), tok_recv.at[2, c])
    keys_values(1)
    pass_on(1, 1)

    started.append(send(wo_ref, wo_all.at[tok], wo_send.at[6], wo_recv.at[6], place, z, sibling))
    x_ring_first()

    weights[-1].wait()
    x = x_buf[...]
    for i in range(pairs):
        q = jnp.dot(x, wq_buf[:, i * pair : (i + 1) * pair], preferred_element_type=jnp.float32)
        for j in range(2):
            d = 2 * i + j
            qn = layer_norm(q[:, j * HDIM : (j + 1) * HDIM]) * qg_ref[...]
            qn = qn.astype(jnp.bfloat16).astype(jnp.float32) * HDIM ** (-0.5)
            q_buf[d] = jnp.concatenate([qn[:half], qn[half:]], axis=1).astype(jnp.bfloat16)
            stays = jnp.logical_and(d == place, after_z == z)

            @pl.when(jnp.logical_not(stays))
            def _():
                send(
                    q_buf.at[d], q_all.at[after_place], q_send.at[d], q_recv.at[after_place], d, after_z, tok
                )

            @pl.when(stays)
            def _():
                pltpu.make_async_copy(q_buf.at[d], q_all.at[after_place], q_recv.at[after_place]).start()

    started.append(
        send(frames_ref, prev_frames, prev_send.at[1], prev_recv.at[1], after_place, after_z, tok)
    )
    for hop in range(2, last + 1):
        for n in range(2):
            pass_on(hop, n)
        if hop == 2:
            share(7, part_rows(across, 0, None))
            x_ring_second()
        elif hop == 3:
            share(8, part_rows(across, -1, None))
            share(9, part_rows(across, 1, None))
    for k in (4, 5):
        landed(part_rows(across, 2, k - 4), wo_recv.at[k])
    share(10, part_rows(across, 2, None))

    for p in range(PLACES):
        landed(rows_got.at[p], row_recv.at[p])
    table = rows_got[:, 0, :]
    lanes = table.shape[1]
    lane = lax.broadcasted_iota(jnp.int32, (PLACES, lanes), 1)
    seen = jnp.where(jnp.logical_and(table > 0, lane < slots), 1.0, 0.0)
    by_row = lax.broadcasted_iota(jnp.int32, (lanes, lanes), 0)
    by_lane = lax.broadcasted_iota(jnp.int32, (lanes, lanes), 1)
    ahead = jnp.where(by_row < by_lane, 1.0, 0.0)
    rank = jnp.dot(seen, ahead, preferred_element_type=jnp.float32)
    spot = jnp.where(seen > 0, rank, -1.0)
    spot_t = jnp.transpose(jnp.concatenate([spot] * (lanes // PLACES), axis=0))
    kept_at = ((by_row >> 1) & (NZ - 1)) * PLACES + (by_row >> 4) * NYH + (by_row & 1)
    kept_at = kept_at.astype(jnp.float32)
    lane_f = by_lane.astype(jnp.float32)
    listed = [
        jnp.sum(jnp.where(spot_t[:, p : p + 1] == lane_f, kept_at, 0.0), axis=0, keepdims=True)
        for p in range(PLACES)
    ]
    listed = jnp.concatenate(listed, axis=0).astype(jnp.int32)
    count = jnp.sum(seen, axis=1, keepdims=True).astype(jnp.int32)
    count = jnp.where(place < HEADS_HERE, count, 0)
    info_ref[...] = jnp.where(lane == slots, count, listed)

    @pl.when(place < HEADS_HERE)
    def _():
        opposite = lax.rem(z + last, NZ)
        for n in range(2):
            for c in range(PLACES):
                way = 0 if c < PLACES // 2 else 1
                landed(part_of(kv_all.at[opposite, c], n), ring_recv.at[way, last - 1, n, c])
        for p in range(PLACES):
            landed(q_all.at[p], q_recv.at[p])
        for hop in range(1, last + 1):
            for n in range(2):
                for c in range(PLACES):
                    for way in range(2):
                        if goes(hop, way, c):
                            ring_copy(hop, way, n, c).wait_send()

    landed(prev_gate, prev_recv.at[0])
    landed(prev_frames, prev_recv.at[1])
    landed(wo_all.at[sibling], wo_recv.at[6])
    for k, shift in ((7, 0), (8, -1), (9, 1), (10, 2)):
        landed(part_rows(sibling_across, shift, None), wo_recv.at[k])
    for copy in started:
        copy.wait_send()
    for d in range(PLACES):
        @pl.when(jnp.logical_not(jnp.logical_and(d == place, after_z == z)))
        def _():
            landed(row_buf, row_send.at[d])
            if d < HEADS_HERE:
                landed(q_buf.at[d], q_send.at[d])

    for d in range(HEADS_HERE):
        for n in range(2):
            @pl.when(d != place)
            def _():
                landed(part_of(kv_buf.at[d], n), kv_send.at[d, n])


def gather(frames, shift, scale, gate, mask, wq, wk, wv, wo, query_gain, key_gain):
    rows, width = frames.shape
    tokens = rows * 4
    pair = 2 * HDIM
    vmem, hbm = pl.BlockSpec(memory_space=pltpu.VMEM), pl.BlockSpec(memory_space=pl.ANY)
    dma = pltpu.SemaphoreType.DMA
    return pl.pallas_call(
        gather_kernel,
        in_specs=[vmem, vmem, vmem, vmem, vmem, hbm, hbm, hbm, hbm, vmem, vmem],
        out_specs=[hbm, hbm, vmem, hbm, vmem, hbm],
        out_shape=[
            jax.ShapeDtypeStruct((PLACES, tokens // 2, pair), jnp.bfloat16),
            jax.ShapeDtypeStruct((NZ, PLACES, tokens, pair), jnp.bfloat16),
            jax.ShapeDtypeStruct((PLACES, 128), jnp.int32),
            jax.ShapeDtypeStruct(frames.shape, jnp.bfloat16),
            jax.ShapeDtypeStruct(gate.shape, jnp.float32),
            jax.ShapeDtypeStruct((4,) + wo.shape, jnp.bfloat16),
        ],
        scratch_shapes=[
            pltpu.VMEM((tokens, width), jnp.bfloat16),
            pltpu.VMEM(wq.shape, jnp.bfloat16),
            pltpu.VMEM((HEADS_HERE // 2, width, 2 * pair), jnp.bfloat16),
            pltpu.VMEM((HEADS_HERE, tokens // 2, pair), jnp.bfloat16),
            pltpu.VMEM((HEADS_HERE, tokens, pair), jnp.bfloat16),
            pltpu.VMEM((8, 128), jnp.int32),
            pltpu.VMEM((PLACES, 8, 128), jnp.int32),
            dma,
            dma((HEADS_HERE // 2, 2)),
            dma((3, CHUNKS)),
            dma((3, CHUNKS)),
            dma((PLACES,)),
            dma((PLACES,)),
            dma((HEADS_HERE, 2)),
            dma((PLACES, 2)),
            dma((HEADS_HERE,)),
            dma((PLACES,)),
            dma((2, NZ // 2, 2, PLACES)),
            dma((2, NZ // 2, 2, PLACES)),
            dma((2,)),
            dma((2,)),
            dma((11,)),
            dma((11,)),
        ],
        compiler_params=pltpu.CompilerParams(
            collective_id=0, has_side_effects=True, vmem_limit_bytes=52 * 1024 * 1024
        ),
    )(frames, shift, scale, gate, mask, wq, wk, wv, wo, query_gain.reshape(1, HDIM), key_gain.reshape(1, HDIM))


def attend_kernel(info_ref, q_ref, kv_ref, out_ref):
    frames_here, half, lanes = q_ref.shape
    rows = 2 * half
    slots = kv_ref.shape[0]
    low = lax.broadcasted_iota(jnp.int32, (half, lanes), 1) < HDIM

    def one_frame(i, _):
        packed = q_ref[i].astype(jnp.float32)
        top = jnp.where(low, packed, 0.0)
        bottom = jnp.where(low, pltpu.roll(packed, HDIM, 1), 0.0)
        q = jnp.concatenate([top, bottom], axis=0).astype(jnp.bfloat16)

        def blocks(state, *numbers):
            running_max, running_sum, weighted = state
            kvs = [kv_ref[info_ref[i, j]] for j in numbers]
            scores = [
                lax.dot_general(kv, q, (((1,), (1,)), ((), ())), preferred_element_type=jnp.float32) for kv in kvs
            ]
            new_max = running_max
            for s in scores:
                new_max = jnp.maximum(new_max, jnp.max(s, axis=0, keepdims=True))
            rescale = jnp.exp(running_max - new_max)
            running_sum, weighted = running_sum * rescale, weighted * rescale
            for kv, s in zip(kvs, scores):
                weights = jnp.exp(s - new_max)
                running_sum = running_sum + jnp.sum(weights, axis=0, keepdims=True)
                weighted = weighted + lax.dot_general(
                    kv, weights.astype(jnp.bfloat16), (((0,), (0,)), ((), ())), preferred_element_type=jnp.float32
                )
            return new_max, running_sum, weighted

        state = (
            jnp.full((1, rows), -1e30, jnp.float32),
            jnp.zeros((1, rows), jnp.float32),
            jnp.zeros((lanes, rows), jnp.float32),
        )
        count = info_ref[i, slots]
        twos = count // 2
        state = lax.fori_loop(0, twos, lambda j, s: blocks(s, 2 * j, 2 * j + 1), state)
        _, total, weighted = lax.fori_loop(2 * twos, count, lambda j, s: blocks(s, j), state)
        attended = jnp.transpose(weighted[HDIM:] / total)
        chunk = rows // 4
        for c in range(4):
            part = attended[c * chunk : (c + 1) * chunk]
            out_ref[i, c] = jnp.concatenate([part[: chunk // 2], part[chunk // 2 :]], axis=1).astype(jnp.bfloat16)
        return 0

    lax.fori_loop(0, frames_here, one_frame, 0)


def attend(info, q, kv):
    frames_here, half, lanes = q.shape
    return pl.pallas_call(
        attend_kernel,
        grid_spec=pltpu.PrefetchScalarGridSpec(
            num_scalar_prefetch=1,
            grid=(1,),
            in_specs=[pl.BlockSpec(memory_space=pltpu.VMEM)] * 2,
            out_specs=pl.BlockSpec((frames_here, 4, half // 4, lanes), lambda i, *_: (0, 0, 0, 0)),
        ),
        out_shape=jax.ShapeDtypeStruct((frames_here, 4, half // 4, lanes), jnp.bfloat16),
        compiler_params=pltpu.CompilerParams(vmem_limit_bytes=40 * 1024 * 1024),
    )(info, q, kv)


def finish_kernel(
    att_ref, w_ref, own_ref, frames_ref, gate_ref, out_ref, got, att_buf, w_buf, w_sem, send_sem, recv_sem
):
    place, z, tok = positions()
    width = out_ref.shape[1]
    tile = width // TILES
    rows = own_ref.shape[0]
    weights = []
    for n in range(TILES):
        cols = pl.ds(n * tile, tile)
        for other in range(4):
            block = lax.rem(tok + other, 4)
            source = own_ref.at[:, cols] if other == 0 else w_ref.at[block, :, cols]
            place_in = w_buf.at[n, pl.ds(pl.multiple_of(block * rows, rows), rows)]
            weights.append(pltpu.make_async_copy(source, place_in, w_sem.at[n, other]))
    for copy in weights:
        copy.start()
    barrier = pltpu.get_barrier_semaphore()
    for p in range(PLACES):
        for t in range(4):
            @pl.when(jnp.logical_not(jnp.logical_and(p == place, t == tok)))
            def _():
                pl.semaphore_signal(barrier, inc=1, device_id=(queue_index(p, z), t), device_id_type=MESH)
    pl.semaphore_wait(barrier, 4 * PLACES - 1)

    slot = tok * HEADS_HERE + place

    @pl.when(place < HEADS_HERE)
    def _():
        for p in range(PLACES):
            for t in range(4):
                here = jnp.logical_and(p == place, t == tok)

                @pl.when(jnp.logical_not(here))
                def _():
                    send(att_ref.at[p, t], got.at[slot], send_sem.at[p, t], recv_sem.at[slot], p, z, t)

                @pl.when(here)
                def _():
                    pltpu.make_async_copy(att_ref.at[p, t], got.at[slot], recv_sem.at[slot]).start()

    heads, half, lanes = got.shape
    low = lax.broadcasted_iota(jnp.int32, (half, lanes), 1) < HDIM
    for m in range(heads // 2):
        landed(got.at[2 * m], recv_sem.at[2 * m])
        landed(got.at[2 * m + 1], recv_sem.at[2 * m + 1])
        first, second = got[2 * m].astype(jnp.float32), got[2 * m + 1].astype(jnp.float32)
        cols = slice(m * lanes, (m + 1) * lanes)
        att_buf[:half, cols] = jnp.where(low, first, pltpu.roll(second, HDIM, 1)).astype(jnp.bfloat16)
        att_buf[half:, cols] = jnp.where(low, pltpu.roll(first, HDIM, 1), second).astype(jnp.bfloat16)
    attended = att_buf[...]
    for n in range(TILES):
        for copy in weights[4 * n : 4 * n + 4]:
            copy.wait()
        projected = jnp.dot(attended, w_buf[n], preferred_element_type=jnp.float32)
        cols = slice(n * tile, (n + 1) * tile)
        updated = frames_ref[:, cols].astype(jnp.float32) + gate_ref[:, cols] * projected
        out_ref[:, cols] = updated.astype(jnp.bfloat16)

    @pl.when(place < HEADS_HERE)
    def _():
        for p in range(PLACES):
            for t in range(4):
                @pl.when(jnp.logical_not(jnp.logical_and(p == place, t == tok)))
                def _():
                    landed(att_ref.at[p, t], send_sem.at[p, t])


def finish(attended, w_all, w_own, frames, gate):
    vmem, hbm = pl.BlockSpec(memory_space=pltpu.VMEM), pl.BlockSpec(memory_space=pl.ANY)
    dma = pltpu.SemaphoreType.DMA
    depth, width = 4 * w_own.shape[0], w_own.shape[1]
    return pl.pallas_call(
        finish_kernel,
        in_specs=[hbm, hbm, hbm, vmem, vmem],
        out_specs=vmem,
        out_shape=jax.ShapeDtypeStruct(frames.shape, jnp.bfloat16),
        scratch_shapes=[
            pltpu.VMEM((4 * HEADS_HERE,) + attended.shape[2:], jnp.bfloat16),
            pltpu.VMEM((frames.shape[0], depth), jnp.bfloat16),
            pltpu.VMEM((TILES, depth, width // TILES), jnp.bfloat16),
            dma((TILES, 4)),
            dma((PLACES, 4)),
            dma((4 * HEADS_HERE,)),
        ],
        compiler_params=pltpu.CompilerParams(
            collective_id=1, has_side_effects=True, vmem_limit_bytes=48 * 1024 * 1024
        ),
    )(attended, w_all, w_own, frames, gate)


def body(
    frames, levels, frame_mask, modulation, w_query, w_key, w_value, w_out, query_gain, key_gain
):
    width = frames.shape[2]
    slots = frame_mask.shape[1]
    own = lax.dynamic_slice(modulation, (levels[0], 0), (1, 3 * width)).astype(jnp.float32)
    q, kv, info, prev_frames, prev_gate, w_all = gather(
        frames[0], own[:, :width], own[:, width : 2 * width], own[:, 2 * width :], frame_mask,
        w_query, w_key, w_value, w_out, query_gain, key_gain,
    )
    attended = attend(info, q, kv.reshape((slots,) + kv.shape[2:]))
    return finish(attended, w_all, w_out, prev_frames, prev_gate)[None]


def solution(mesh):
    return jax.shard_map(
        body,
        mesh=mesh,
        in_specs=(
            P("queue", "tok", None),
            P("queue"),
            P("queue", None),
            P(),
            P(None, "tok"),
            P(None, "tok"),
            P(None, "tok"),
            P("tok", None),
            P(),
            P(),
        ),
        out_specs=P("queue", "tok", None),
        check_vma=False,
    )
```

```python
import jax
import jax.numpy as jnp
from jax import lax
from jax.experimental import pallas as pl
from jax.experimental.pallas import tpu as pltpu
from jax.sharding import PartitionSpec as P

HDIM = 64
NX, NZ, NYH = 4, 8, 2
PLACES = NX * NYH
HEADS_HERE = 6
CHUNKS = 4
TILES = 6
MESH = pl.DeviceIdType.MESH


def queue_index(place, z):
    return ((place // NYH) * NZ + z) * NYH + place % NYH


def layer_norm(values_in):
    center = jnp.mean(values_in, axis=-1, keepdims=True)
    spread = jnp.mean(jnp.square(values_in - center), axis=-1, keepdims=True)
    return (values_in - center) * lax.rsqrt(spread + 1e-06)


def positions():
    q_at = lax.axis_index("queue")
    return (q_at // (NZ * NYH)) * NYH + q_at % NYH, (q_at // NYH) % NZ, lax.axis_index("tok")


def send(src, dst, send_sem, recv_sem, place, z, tok):
    copy = pltpu.make_async_remote_copy(
        src_ref=src,
        dst_ref=dst,
        send_sem=send_sem,
        recv_sem=recv_sem,
        device_id=(queue_index(place, z), tok),
        device_id_type=MESH,
    )
    copy.start()
    return copy


def landed(ref, sem):
    pltpu.make_async_copy(ref, ref, sem).wait()


def gather_kernel(
    frames_ref, shift_ref, scale_ref, gate_ref, mask_ref, wq_ref, wk_ref, wv_ref, wo_ref, qg_ref, kg_ref,
    q_all, kv_all, info_ref, prev_frames, prev_gate, wo_all,
    x_buf, wq_buf, wkv_buf, q_buf, kv_buf, row_buf, rows_got, frames_way,
    wq_sem, wkv_sem, tok_send, tok_recv, row_send, row_recv, kv_send, kv_recv, q_send, q_recv,
    ring_send, ring_recv, prev_send, prev_recv, wo_send, wo_recv, way_send, way_recv,
):
    place, z, tok = positions()
    up, down = lax.rem(z + 1, NZ), lax.rem(z + NZ - 1, NZ)
    sibling = tok + 1 - 2 * lax.rem(tok, 2)
    across = lax.rem(tok + 2, 4)
    sibling_across = lax.rem(sibling + 2, 4)
    pair = 2 * HDIM
    pairs = HEADS_HERE // 2
    weights = []
    for i in range(pairs):
        for j, w in enumerate((wk_ref, wv_ref)):
            weights.append(
                pltpu.make_async_copy(
                    w.at[:, pl.ds(i * pair, pair)], wkv_buf.at[i, :, pl.ds(j * pair, pair)], wkv_sem.at[i, j]
                )
            )
    weights.append(pltpu.make_async_copy(wq_ref, wq_buf, wq_sem))
    for copy in weights:
        copy.start()
    twin = place + 1 - 2 * lax.rem(place, NYH)

    barrier = pltpu.get_barrier_semaphore()
    for other_tok in (sibling, across):
        pl.semaphore_signal(
            barrier, inc=1, device_id=(queue_index(place, z), other_tok), device_id_type=MESH
        )
    pl.semaphore_signal(barrier, inc=1, device_id=(queue_index(twin, z), across), device_id_type=MESH)
    for p in range(PLACES):
        for other_z in (up, down):
            pl.semaphore_signal(barrier, inc=1, device_id=(queue_index(p, other_z), tok), device_id_type=MESH)

        @pl.when(p != place)
        def _():
            pl.semaphore_signal(barrier, inc=1, device_id=(queue_index(p, z), tok), device_id_type=MESH)

    rows = frames_ref.shape[0]
    step = rows // CHUNKS

    def x_rows(owner, c):
        return x_buf.at[pl.ds(pl.multiple_of(owner * rows + c * step, step), step)]

    started = []
    for c in range(CHUNKS):
        part = layer_norm(frames_ref[c * step : (c + 1) * step].astype(jnp.float32))
        part = part * (1.0 + scale_ref[...]) + shift_ref[...]
        x_buf[pl.ds(pl.multiple_of(tok * rows + c * step, step), step)] = part.astype(jnp.bfloat16)
        if c == 0:
            pl.semaphore_wait(barrier, 3 + 3 * PLACES - 1)
        for way, other_tok in ((1, across), (0, sibling)):
            mine = x_rows(tok, c)
            started.append(send(mine, mine, tok_send.at[way, c], tok_recv.at[way, c], place, z, other_tok))

    after = lax.rem(queue_index(place, z) + 1, NX * NZ * NYH)
    after_place = (after // (NZ * NYH)) * NYH + after % NYH
    after_z = (after // NYH) % NZ
    slots = mask_ref.shape[1]
    row_buf[...] = jnp.zeros_like(row_buf)
    row_buf[0:1, :slots] = mask_ref[...]
    for d in range(PLACES):
        stays = jnp.logical_and(d == place, after_z == z)

        @pl.when(jnp.logical_not(stays))
        def _():
            send(row_buf, rows_got.at[after_place], row_send.at[d], row_recv.at[after_place], d, after_z, tok)

        @pl.when(stays)
        def _():
            pltpu.make_async_copy(row_buf, rows_got.at[after_place], row_recv.at[after_place]).start()

    started.append(
        send(gate_ref, prev_gate, prev_send.at[0], prev_recv.at[0], after_place, after_z, tok)
    )

    half = x_buf.shape[0] // 2
    first = tok // 2
    at = [pl.multiple_of(first * half, half), pl.multiple_of((1 - first) * half, half)]

    def part_of(ref, n):
        return ref.at[pl.ds(at[n], half)]

    def keys_values(n):
        x = x_buf[pl.ds(at[n], half)]
        for i in range(pairs):
            if n == 0:
                weights[2 * i].wait()
                weights[2 * i + 1].wait()
            both = jnp.dot(x, wkv_buf[i], preferred_element_type=jnp.float32)
            for j in range(2):
                d = 2 * i + j
                kn = layer_norm(both[:, j * HDIM : (j + 1) * HDIM]) * kg_ref[...]
                v = both[:, pair + j * HDIM : pair + (j + 1) * HDIM]
                kv_buf[d, pl.ds(at[n], half)] = jnp.concatenate([kn, v], axis=1).astype(jnp.bfloat16)
                block = part_of(kv_buf.at[d], n)
                here = part_of(kv_all.at[z, place], n)

                @pl.when(d != place)
                def _():
                    send(block, here, kv_send.at[d, n], kv_recv.at[place, n], d, z, tok)

                @pl.when(d == place)
                def _():
                    pltpu.make_async_copy(block, here, kv_recv.at[place, n]).start()

    last = NZ // 2

    def ring_copy(hop, way, n, c):
        source = lax.rem(z + NZ - (hop - 1), NZ) if way == 0 else lax.rem(z + hop - 1, NZ)
        block = part_of(kv_all.at[source, c], n)
        return pltpu.make_async_remote_copy(
            src_ref=block,
            dst_ref=block,
            send_sem=ring_send.at[way, hop - 1, n, c],
            recv_sem=ring_recv.at[way, hop - 1, n, c],
            device_id=(queue_index(place, down if way else up), tok),
            device_id_type=MESH,
        )

    last_up = jnp.where(lax.rem(place, NYH) == 1, PLACES // 2 - 1, PLACES // 2)

    def goes(hop, way, c):
        if hop < last:
            return True
        return c < last_up if way == 0 else c >= last_up

    def pass_on(hop, n):
        @pl.when(place < HEADS_HERE)
        def _():
            for c in range(PLACES):
                if hop == 1:
                    landed(part_of(kv_all.at[z, c], n), kv_recv.at[c, n])
                for way in range(2):
                    if hop > 1:
                        source = lax.rem(z + NZ - (hop - 1), NZ) if way == 0 else lax.rem(z + hop - 1, NZ)
                        landed(part_of(kv_all.at[source, c], n), ring_recv.at[way, hop - 2, n, c])

                    @pl.when(goes(hop, way, c))
                    def _():
                        ring_copy(hop, way, n, c).start()

    rows_here = wo_ref.shape[0]
    quarter = rows_here // NX
    x_at = place // NYH
    x_next = lax.rem(place + NYH, PLACES)
    x_before = lax.rem(place + PLACES - NYH, PLACES)
    lower = tok // 2 == 0
    y_next = jnp.where(lower, place, twin)
    y_before = jnp.where(lower, twin, place)

    def part_rows(owner, shift, side):
        start = lax.rem(x_at + shift + NX, NX) * quarter
        if side is None:
            return wo_all.at[owner, pl.ds(pl.multiple_of(start, 16), quarter)]
        return wo_all.at[owner, pl.ds(pl.multiple_of(start + side * (quarter // 2), 16), quarter // 2)]

    def y_quarter():
        for side, target in ((0, y_next), (1, y_before)):
            start = pl.multiple_of(x_at * quarter + side * (quarter // 2), 16)
            part = wo_ref.at[pl.ds(start, quarter // 2)]
            started.append(
                send(part, part_rows(tok, 0, side), wo_send.at[side], wo_recv.at[side], target, z, across)
            )

    def x_ring_first():
        for side in range(2):
            landed(part_rows(across, 0, side), wo_recv.at[side])
        mine = part_rows(across, 0, None)
        for k, target in ((2, x_next), (3, x_before)):
            started.append(send(mine, mine, wo_send.at[k], wo_recv.at[k], target, z, tok))

    def x_ring_second():
        for k, shift, side, target in ((4, -1, 0, x_next), (5, 1, 1, x_before)):
            landed(part_rows(across, shift, None), wo_recv.at[k - 2])
            half_part = part_rows(across, shift, side)
            started.append(send(half_part, half_part, wo_send.at[k], wo_recv.at[k], target, z, tok))

    def share(k, block):
        started.append(send(block, block, wo_send.at[k], wo_recv.at[k], place, z, sibling))

    for c in range(CHUNKS):
        landed(x_rows(sibling, c), tok_recv.at[0, c])
    keys_values(0)
    pass_on(1, 0)
    for c in range(CHUNKS):
        theirs = x_rows(across, c)
        landed(theirs, tok_recv.at[1, c])
        started.append(send(theirs, theirs, tok_send.at[2, c], tok_recv.at[2, c], place, z, sibling))
    y_quarter()
    for c in range(CHUNKS):
        landed(x_rows(sibling_across, c), tok_recv.at[2, c])
    keys_values(1)
    pass_on(1, 1)

    started.append(send(wo_ref, wo_all.at[tok], wo_send.at[6], wo_recv.at[6], place, z, sibling))
    x_ring_first()

    weights[-1].wait()
    x = x_buf[...]
    for i in range(pairs):
        q = jnp.dot(x, wq_buf[:, i * pair : (i + 1) * pair], preferred_element_type=jnp.float32)
        for j in range(2):
            d = 2 * i + j
            qn = layer_norm(q[:, j * HDIM : (j + 1) * HDIM]) * qg_ref[...]
            qn = qn.astype(jnp.bfloat16).astype(jnp.float32) * HDIM ** (-0.5)
            q_buf[d] = jnp.concatenate([qn[:half], qn[half:]], axis=1).astype(jnp.bfloat16)
            stays = jnp.logical_and(d == place, after_z == z)

            @pl.when(jnp.logical_not(stays))
            def _():
                send(
                    q_buf.at[d], q_all.at[after_place], q_send.at[d], q_recv.at[after_place], d, after_z, tok
                )

            @pl.when(stays)
            def _():
                pltpu.make_async_copy(q_buf.at[d], q_all.at[after_place], q_recv.at[after_place]).start()

    courier = PLACES - 1
    detour = jnp.logical_and(lax.rem(place, NYH) == 1, place < courier)

    @pl.when(detour)
    def _():
        send(frames_ref, frames_way.at[x_at], prev_send.at[1], way_recv.at[x_at], courier, z, tok)

    @pl.when(jnp.logical_not(detour))
    def _():
        send(frames_ref, prev_frames, prev_send.at[1], prev_recv.at[1], after_place, after_z, tok)

    def courier_send():
        @pl.when(place == courier)
        def _():
            for x_from in range(NX - 1):
                slot = lax.rem(queue_index(x_from * NYH + 1, z) + 1, NX * NZ * NYH)
                landed(frames_way.at[x_from], way_recv.at[x_from])
                send(
                    frames_way.at[x_from], prev_frames, way_send.at[x_from], prev_recv.at[1],
                    (slot // (NZ * NYH)) * NYH + slot % NYH, (slot // NYH) % NZ, tok,
                )

    for hop in range(2, last + 1):
        for n in range(2):
            pass_on(hop, n)
        if hop == 2:
            share(7, part_rows(across, 0, None))
            x_ring_second()
            courier_send()
        elif hop == 3:
            share(8, part_rows(across, -1, None))
            share(9, part_rows(across, 1, None))
    for k in (4, 5):
        landed(part_rows(across, 2, k - 4), wo_recv.at[k])
    share(10, part_rows(across, 2, None))

    for p in range(PLACES):
        landed(rows_got.at[p], row_recv.at[p])
    table = rows_got[:, 0, :]
    lanes = table.shape[1]
    lane = lax.broadcasted_iota(jnp.int32, (PLACES, lanes), 1)
    seen = jnp.where(jnp.logical_and(table > 0, lane < slots), 1.0, 0.0)
    by_row = lax.broadcasted_iota(jnp.int32, (lanes, lanes), 0)
    by_lane = lax.broadcasted_iota(jnp.int32, (lanes, lanes), 1)
    ahead = jnp.where(by_row < by_lane, 1.0, 0.0)
    rank = jnp.dot(seen, ahead, preferred_element_type=jnp.float32)
    spot = jnp.where(seen > 0, rank, -1.0)
    spot_t = jnp.transpose(jnp.concatenate([spot] * (lanes // PLACES), axis=0))
    kept_at = ((by_row >> 1) & (NZ - 1)) * PLACES + (by_row >> 4) * NYH + (by_row & 1)
    kept_at = kept_at.astype(jnp.float32)
    lane_f = by_lane.astype(jnp.float32)
    listed = [
        jnp.sum(jnp.where(spot_t[:, p : p + 1] == lane_f, kept_at, 0.0), axis=0, keepdims=True)
        for p in range(PLACES)
    ]
    listed = jnp.concatenate(listed, axis=0).astype(jnp.int32)
    count = jnp.sum(seen, axis=1, keepdims=True).astype(jnp.int32)
    count = jnp.where(place < HEADS_HERE, count, 0)
    info_ref[...] = jnp.where(lane == slots, count, listed)

    @pl.when(place < HEADS_HERE)
    def _():
        opposite = lax.rem(z + last, NZ)
        for n in range(2):
            for c in range(PLACES):
                for way in range(2):
                    @pl.when(goes(last, way, c))
                    def _():
                        landed(part_of(kv_all.at[opposite, c], n), ring_recv.at[way, last - 1, n, c])
        for p in range(PLACES):
            landed(q_all.at[p], q_recv.at[p])
        for hop in range(1, last + 1):
            for n in range(2):
                for c in range(PLACES):
                    for way in range(2):
                        @pl.when(goes(hop, way, c))
                        def _():
                            ring_copy(hop, way, n, c).wait_send()

    landed(prev_gate, prev_recv.at[0])
    landed(prev_frames, prev_recv.at[1])
    landed(frames_ref, prev_send.at[1])

    @pl.when(place == courier)
    def _():
        for x_from in range(NX - 1):
            landed(frames_way.at[x_from], way_send.at[x_from])

    landed(wo_all.at[sibling], wo_recv.at[6])
    for k, shift in ((7, 0), (8, -1), (9, 1), (10, 2)):
        landed(part_rows(sibling_across, shift, None), wo_recv.at[k])
    for copy in started:
        copy.wait_send()
    for d in range(PLACES):
        @pl.when(jnp.logical_not(jnp.logical_and(d == place, after_z == z)))
        def _():
            landed(row_buf, row_send.at[d])
            if d < HEADS_HERE:
                landed(q_buf.at[d], q_send.at[d])

    for d in range(HEADS_HERE):
        for n in range(2):
            @pl.when(d != place)
            def _():
                landed(part_of(kv_buf.at[d], n), kv_send.at[d, n])


def gather(frames, shift, scale, gate, mask, wq, wk, wv, wo, query_gain, key_gain):
    rows, width = frames.shape
    tokens = rows * 4
    pair = 2 * HDIM
    vmem, hbm = pl.BlockSpec(memory_space=pltpu.VMEM), pl.BlockSpec(memory_space=pl.ANY)
    dma = pltpu.SemaphoreType.DMA
    return pl.pallas_call(
        gather_kernel,
        in_specs=[vmem, vmem, vmem, vmem, vmem, hbm, hbm, hbm, hbm, vmem, vmem],
        out_specs=[hbm, hbm, vmem, hbm, vmem, hbm],
        out_shape=[
            jax.ShapeDtypeStruct((PLACES, tokens // 2, pair), jnp.bfloat16),
            jax.ShapeDtypeStruct((NZ, PLACES, tokens, pair), jnp.bfloat16),
            jax.ShapeDtypeStruct((PLACES, 128), jnp.int32),
            jax.ShapeDtypeStruct(frames.shape, jnp.bfloat16),
            jax.ShapeDtypeStruct(gate.shape, jnp.float32),
            jax.ShapeDtypeStruct((4,) + wo.shape, jnp.bfloat16),
        ],
        scratch_shapes=[
            pltpu.VMEM((tokens, width), jnp.bfloat16),
            pltpu.VMEM(wq.shape, jnp.bfloat16),
            pltpu.VMEM((HEADS_HERE // 2, width, 2 * pair), jnp.bfloat16),
            pltpu.VMEM((HEADS_HERE, tokens // 2, pair), jnp.bfloat16),
            pltpu.VMEM((HEADS_HERE, tokens, pair), jnp.bfloat16),
            pltpu.VMEM((8, 128), jnp.int32),
            pltpu.VMEM((PLACES, 8, 128), jnp.int32),
            pltpu.VMEM((NX - 1,) + frames.shape, jnp.bfloat16),
            dma,
            dma((HEADS_HERE // 2, 2)),
            dma((3, CHUNKS)),
            dma((3, CHUNKS)),
            dma((PLACES,)),
            dma((PLACES,)),
            dma((HEADS_HERE, 2)),
            dma((PLACES, 2)),
            dma((HEADS_HERE,)),
            dma((PLACES,)),
            dma((2, NZ // 2, 2, PLACES)),
            dma((2, NZ // 2, 2, PLACES)),
            dma((2,)),
            dma((2,)),
            dma((11,)),
            dma((11,)),
            dma((NX - 1,)),
            dma((NX - 1,)),
        ],
        compiler_params=pltpu.CompilerParams(
            collective_id=0, has_side_effects=True, vmem_limit_bytes=52 * 1024 * 1024
        ),
    )(frames, shift, scale, gate, mask, wq, wk, wv, wo, query_gain.reshape(1, HDIM), key_gain.reshape(1, HDIM))


def attend_kernel(info_ref, q_ref, kv_ref, out_ref):
    frames_here, half, lanes = q_ref.shape
    rows = 2 * half
    slots = kv_ref.shape[0]
    low = lax.broadcasted_iota(jnp.int32, (half, lanes), 1) < HDIM

    def one_frame(i, _):
        packed = q_ref[i].astype(jnp.float32)
        top = jnp.where(low, packed, 0.0)
        bottom = jnp.where(low, pltpu.roll(packed, HDIM, 1), 0.0)
        q = jnp.concatenate([top, bottom], axis=0).astype(jnp.bfloat16)

        def blocks(state, *numbers):
            running_max, running_sum, weighted = state
            kvs = [kv_ref[info_ref[i, j]] for j in numbers]
            scores = [
                lax.dot_general(kv, q, (((1,), (1,)), ((), ())), preferred_element_type=jnp.float32) for kv in kvs
            ]
            new_max = running_max
            for s in scores:
                new_max = jnp.maximum(new_max, jnp.max(s, axis=0, keepdims=True))
            rescale = jnp.exp(running_max - new_max)
            running_sum, weighted = running_sum * rescale, weighted * rescale
            for kv, s in zip(kvs, scores):
                weights = jnp.exp(s - new_max)
                running_sum = running_sum + jnp.sum(weights, axis=0, keepdims=True)
                weighted = weighted + lax.dot_general(
                    kv, weights.astype(jnp.bfloat16), (((0,), (0,)), ((), ())), preferred_element_type=jnp.float32
                )
            return new_max, running_sum, weighted

        state = (
            jnp.full((1, rows), -1e30, jnp.float32),
            jnp.zeros((1, rows), jnp.float32),
            jnp.zeros((lanes, rows), jnp.float32),
        )
        count = info_ref[i, slots]
        twos = count // 2
        state = lax.fori_loop(0, twos, lambda j, s: blocks(s, 2 * j, 2 * j + 1), state)
        _, total, weighted = lax.fori_loop(2 * twos, count, lambda j, s: blocks(s, j), state)
        attended = jnp.transpose(weighted[HDIM:] / total)
        chunk = rows // 4
        for c in range(4):
            part = attended[c * chunk : (c + 1) * chunk]
            out_ref[i, c] = jnp.concatenate([part[: chunk // 2], part[chunk // 2 :]], axis=1).astype(jnp.bfloat16)
        return 0

    lax.fori_loop(0, frames_here, one_frame, 0)


def attend(info, q, kv):
    frames_here, half, lanes = q.shape
    return pl.pallas_call(
        attend_kernel,
        grid_spec=pltpu.PrefetchScalarGridSpec(
            num_scalar_prefetch=1,
            grid=(1,),
            in_specs=[pl.BlockSpec(memory_space=pltpu.VMEM)] * 2,
            out_specs=pl.BlockSpec((frames_here, 4, half // 4, lanes), lambda i, *_: (0, 0, 0, 0)),
        ),
        out_shape=jax.ShapeDtypeStruct((frames_here, 4, half // 4, lanes), jnp.bfloat16),
        compiler_params=pltpu.CompilerParams(vmem_limit_bytes=40 * 1024 * 1024),
    )(info, q, kv)


def finish_kernel(
    att_ref, w_ref, own_ref, frames_ref, gate_ref, out_ref, got, att_buf, w_buf, w_sem, send_sem, recv_sem
):
    place, z, tok = positions()
    width = out_ref.shape[1]
    tile = width // TILES
    rows = own_ref.shape[0]
    weights = []
    for n in range(TILES):
        cols = pl.ds(n * tile, tile)
        for other in range(4):
            block = lax.rem(tok + other, 4)
            source = own_ref.at[:, cols] if other == 0 else w_ref.at[block, :, cols]
            place_in = w_buf.at[n, pl.ds(pl.multiple_of(block * rows, rows), rows)]
            weights.append(pltpu.make_async_copy(source, place_in, w_sem.at[n, other]))
    for copy in weights:
        copy.start()
    barrier = pltpu.get_barrier_semaphore()
    for p in range(PLACES):
        for t in range(4):
            @pl.when(jnp.logical_not(jnp.logical_and(p == place, t == tok)))
            def _():
                pl.semaphore_signal(barrier, inc=1, device_id=(queue_index(p, z), t), device_id_type=MESH)
    pl.semaphore_wait(barrier, 4 * PLACES - 1)

    slot = tok * HEADS_HERE + place

    @pl.when(place < HEADS_HERE)
    def _():
        for p in range(PLACES):
            for t in range(4):
                here = jnp.logical_and(p == place, t == tok)

                @pl.when(jnp.logical_not(here))
                def _():
                    send(att_ref.at[p, t], got.at[slot], send_sem.at[p, t], recv_sem.at[slot], p, z, t)

                @pl.when(here)
                def _():
                    pltpu.make_async_copy(att_ref.at[p, t], got.at[slot], recv_sem.at[slot]).start()

    heads, half, lanes = got.shape
    low = lax.broadcasted_iota(jnp.int32, (half, lanes), 1) < HDIM
    for m in range(heads // 2):
        landed(got.at[2 * m], recv_sem.at[2 * m])
        landed(got.at[2 * m + 1], recv_sem.at[2 * m + 1])
        first, second = got[2 * m].astype(jnp.float32), got[2 * m + 1].astype(jnp.float32)
        cols = slice(m * lanes, (m + 1) * lanes)
        att_buf[:half, cols] = jnp.where(low, first, pltpu.roll(second, HDIM, 1)).astype(jnp.bfloat16)
        att_buf[half:, cols] = jnp.where(low, pltpu.roll(first, HDIM, 1), second).astype(jnp.bfloat16)
    attended = att_buf[...]
    for n in range(TILES):
        for copy in weights[4 * n : 4 * n + 4]:
            copy.wait()
        projected = jnp.dot(attended, w_buf[n], preferred_element_type=jnp.float32)
        cols = slice(n * tile, (n + 1) * tile)
        updated = frames_ref[:, cols].astype(jnp.float32) + gate_ref[:, cols] * projected
        out_ref[:, cols] = updated.astype(jnp.bfloat16)

    @pl.when(place < HEADS_HERE)
    def _():
        for p in range(PLACES):
            for t in range(4):
                @pl.when(jnp.logical_not(jnp.logical_and(p == place, t == tok)))
                def _():
                    landed(att_ref.at[p, t], send_sem.at[p, t])


def finish(attended, w_all, w_own, frames, gate):
    vmem, hbm = pl.BlockSpec(memory_space=pltpu.VMEM), pl.BlockSpec(memory_space=pl.ANY)
    dma = pltpu.SemaphoreType.DMA
    depth, width = 4 * w_own.shape[0], w_own.shape[1]
    return pl.pallas_call(
        finish_kernel,
        in_specs=[hbm, hbm, hbm, vmem, vmem],
        out_specs=vmem,
        out_shape=jax.ShapeDtypeStruct(frames.shape, jnp.bfloat16),
        scratch_shapes=[
            pltpu.VMEM((4 * HEADS_HERE,) + attended.shape[2:], jnp.bfloat16),
            pltpu.VMEM((frames.shape[0], depth), jnp.bfloat16),
            pltpu.VMEM((TILES, depth, width // TILES), jnp.bfloat16),
            dma((TILES, 4)),
            dma((PLACES, 4)),
            dma((4 * HEADS_HERE,)),
        ],
        compiler_params=pltpu.CompilerParams(
            collective_id=1, has_side_effects=True, vmem_limit_bytes=48 * 1024 * 1024
        ),
    )(attended, w_all, w_own, frames, gate)


def body(
    frames, levels, frame_mask, modulation, w_query, w_key, w_value, w_out, query_gain, key_gain
):
    width = frames.shape[2]
    slots = frame_mask.shape[1]
    own = lax.dynamic_slice(modulation, (levels[0], 0), (1, 3 * width)).astype(jnp.float32)
    q, kv, info, prev_frames, prev_gate, w_all = gather(
        frames[0], own[:, :width], own[:, width : 2 * width], own[:, 2 * width :], frame_mask,
        w_query, w_key, w_value, w_out, query_gain, key_gain,
    )
    attended = attend(info, q, kv.reshape((slots,) + kv.shape[2:]))
    return finish(attended, w_all, w_out, prev_frames, prev_gate)[None]


def solution(mesh):
    return jax.shard_map(
        body,
        mesh=mesh,
        in_specs=(
            P("queue", "tok", None),
            P("queue"),
            P("queue", None),
            P(),
            P(None, "tok"),
            P(None, "tok"),
            P(None, "tok"),
            P("tok", None),
            P(),
            P(),
        ),
        out_specs=P("queue", "tok", None),
        check_vma=False,
    )
```

```python
import jax
import jax.numpy as jnp
from jax import lax
from jax.experimental import pallas as pl
from jax.experimental.pallas import tpu as pltpu
from jax.sharding import PartitionSpec as P

HDIM = 64
NX, NZ, NYH = 4, 8, 2
PLACES = NX * NYH
HEADS_HERE = 6
CHUNKS = 4
TILES = 6
MESH = pl.DeviceIdType.MESH


def queue_index(place, z):
    return ((place // NYH) * NZ + z) * NYH + place % NYH


def layer_norm(values_in):
    center = jnp.mean(values_in, axis=-1, keepdims=True)
    spread = jnp.mean(jnp.square(values_in - center), axis=-1, keepdims=True)
    return (values_in - center) * lax.rsqrt(spread + 1e-06)


def positions():
    q_at = lax.axis_index("queue")
    return (q_at // (NZ * NYH)) * NYH + q_at % NYH, (q_at // NYH) % NZ, lax.axis_index("tok")


def send(src, dst, send_sem, recv_sem, place, z, tok):
    copy = pltpu.make_async_remote_copy(
        src_ref=src,
        dst_ref=dst,
        send_sem=send_sem,
        recv_sem=recv_sem,
        device_id=(queue_index(place, z), tok),
        device_id_type=MESH,
    )
    copy.start()
    return copy


def landed(ref, sem):
    pltpu.make_async_copy(ref, ref, sem).wait()


def gather_kernel(
    frames_ref, shift_ref, scale_ref, gate_ref, mask_ref, wq_ref, wk_ref, wv_ref, wo_ref, qg_ref, kg_ref,
    q_all, kv_all, info_ref, prev_frames, prev_gate, wo_all,
    x_buf, wq_buf, wkv_buf, q_buf, kv_buf, row_buf, rows_got, frames_way,
    wq_sem, wkv_sem, tok_send, tok_recv, row_send, row_recv, kv_send, kv_recv, q_send, q_recv,
    ring_send, ring_recv, prev_send, prev_recv, wo_send, wo_recv, way_send, way_recv,
):
    place, z, tok = positions()
    up, down = lax.rem(z + 1, NZ), lax.rem(z + NZ - 1, NZ)
    sibling = tok + 1 - 2 * lax.rem(tok, 2)
    across = lax.rem(tok + 2, 4)
    sibling_across = lax.rem(sibling + 2, 4)
    pair = 2 * HDIM
    pairs = HEADS_HERE // 2
    weights = []
    for i in range(pairs):
        for j, w in enumerate((wk_ref, wv_ref)):
            weights.append(
                pltpu.make_async_copy(
                    w.at[:, pl.ds(i * pair, pair)], wkv_buf.at[i, :, pl.ds(j * pair, pair)], wkv_sem.at[i, j]
                )
            )
    weights.append(pltpu.make_async_copy(wq_ref, wq_buf, wq_sem))
    for copy in weights:
        copy.start()
    twin = place + 1 - 2 * lax.rem(place, NYH)

    barrier = pltpu.get_barrier_semaphore()
    for other_tok in (sibling, across):
        pl.semaphore_signal(
            barrier, inc=1, device_id=(queue_index(place, z), other_tok), device_id_type=MESH
        )
    pl.semaphore_signal(barrier, inc=1, device_id=(queue_index(twin, z), across), device_id_type=MESH)
    for p in range(PLACES):
        for other_z in (up, down):
            pl.semaphore_signal(barrier, inc=1, device_id=(queue_index(p, other_z), tok), device_id_type=MESH)

        @pl.when(p != place)
        def _():
            pl.semaphore_signal(barrier, inc=1, device_id=(queue_index(p, z), tok), device_id_type=MESH)

    rows = frames_ref.shape[0]
    step = rows // CHUNKS

    def x_rows(owner, c):
        return x_buf.at[pl.ds(pl.multiple_of(owner * rows + c * step, step), step)]

    started = []
    for c in range(CHUNKS):
        part = layer_norm(frames_ref[c * step : (c + 1) * step].astype(jnp.float32))
        part = part * (1.0 + scale_ref[...]) + shift_ref[...]
        x_buf[pl.ds(pl.multiple_of(tok * rows + c * step, step), step)] = part.astype(jnp.bfloat16)
        if c == 0:
            pl.semaphore_wait(barrier, 3 + 3 * PLACES - 1)
        for way, other_tok in ((1, across), (0, sibling)):
            mine = x_rows(tok, c)
            started.append(send(mine, mine, tok_send.at[way, c], tok_recv.at[way, c], place, z, other_tok))

    after = lax.rem(queue_index(place, z) + 1, NX * NZ * NYH)
    after_place = (after // (NZ * NYH)) * NYH + after % NYH
    after_z = (after // NYH) % NZ
    slots = mask_ref.shape[1]
    row_buf[...] = jnp.zeros_like(row_buf)
    row_buf[0:1, :slots] = mask_ref[...]
    for d in range(PLACES):
        stays = jnp.logical_and(d == place, after_z == z)

        @pl.when(jnp.logical_not(stays))
        def _():
            send(row_buf, rows_got.at[after_place], row_send.at[d], row_recv.at[after_place], d, after_z, tok)

        @pl.when(stays)
        def _():
            pltpu.make_async_copy(row_buf, rows_got.at[after_place], row_recv.at[after_place]).start()

    started.append(
        send(gate_ref, prev_gate, prev_send.at[0], prev_recv.at[0], after_place, after_z, tok)
    )

    courier = PLACES - 1
    x_at = place // NYH
    detour = jnp.logical_and(lax.rem(place, NYH) == 1, place < courier)

    @pl.when(detour)
    def _():
        send(frames_ref, frames_way.at[x_at], prev_send.at[1], way_recv.at[x_at], courier, z, tok)

    def courier_send():
        @pl.when(place == courier)
        def _():
            for x_from in range(NX - 1):
                slot = lax.rem(queue_index(x_from * NYH + 1, z) + 1, NX * NZ * NYH)
                landed(frames_way.at[x_from], way_recv.at[x_from])
                send(
                    frames_way.at[x_from], prev_frames, way_send.at[x_from], prev_recv.at[1],
                    (slot // (NZ * NYH)) * NYH + slot % NYH, (slot // NYH) % NZ, tok,
                )

    half = x_buf.shape[0] // 2
    first = tok // 2
    at = [pl.multiple_of(first * half, half), pl.multiple_of((1 - first) * half, half)]

    def part_of(ref, n):
        return ref.at[pl.ds(at[n], half)]

    def keys_values(n):
        x = x_buf[pl.ds(at[n], half)]
        for i in range(pairs):
            if n == 0:
                weights[2 * i].wait()
                weights[2 * i + 1].wait()
            both = jnp.dot(x, wkv_buf[i], preferred_element_type=jnp.float32)
            for j in range(2):
                d = 2 * i + j
                kn = layer_norm(both[:, j * HDIM : (j + 1) * HDIM]) * kg_ref[...]
                v = both[:, pair + j * HDIM : pair + (j + 1) * HDIM]
                kv_buf[d, pl.ds(at[n], half)] = jnp.concatenate([kn, v], axis=1).astype(jnp.bfloat16)
                block = part_of(kv_buf.at[d], n)
                here = part_of(kv_all.at[z, place], n)

                @pl.when(d != place)
                def _():
                    send(block, here, kv_send.at[d, n], kv_recv.at[place, n], d, z, tok)

                @pl.when(d == place)
                def _():
                    pltpu.make_async_copy(block, here, kv_recv.at[place, n]).start()

    last = NZ // 2

    def ring_copy(hop, way, n, c):
        source = lax.rem(z + NZ - (hop - 1), NZ) if way == 0 else lax.rem(z + hop - 1, NZ)
        block = part_of(kv_all.at[source, c], n)
        return pltpu.make_async_remote_copy(
            src_ref=block,
            dst_ref=block,
            send_sem=ring_send.at[way, hop - 1, n, c],
            recv_sem=ring_recv.at[way, hop - 1, n, c],
            device_id=(queue_index(place, down if way else up), tok),
            device_id_type=MESH,
        )

    last_up = jnp.where(lax.rem(place, NYH) == 1, PLACES // 2 - 1, PLACES // 2)

    def goes(hop, way, c):
        if hop < last:
            return True
        return c < last_up if way == 0 else c >= last_up

    def pass_on(hop, n):
        @pl.when(place < HEADS_HERE)
        def _():
            for c in range(PLACES):
                if hop == 1:
                    landed(part_of(kv_all.at[z, c], n), kv_recv.at[c, n])
                for way in range(2):
                    if hop > 1:
                        source = lax.rem(z + NZ - (hop - 1), NZ) if way == 0 else lax.rem(z + hop - 1, NZ)
                        landed(part_of(kv_all.at[source, c], n), ring_recv.at[way, hop - 2, n, c])

                    @pl.when(goes(hop, way, c))
                    def _():
                        ring_copy(hop, way, n, c).start()

    rows_here = wo_ref.shape[0]
    quarter = rows_here // NX
    x_next = lax.rem(place + NYH, PLACES)
    x_before = lax.rem(place + PLACES - NYH, PLACES)
    lower = tok // 2 == 0
    y_next = jnp.where(lower, place, twin)
    y_before = jnp.where(lower, twin, place)

    def part_rows(owner, shift, side):
        start = lax.rem(x_at + shift + NX, NX) * quarter
        if side is None:
            return wo_all.at[owner, pl.ds(pl.multiple_of(start, 16), quarter)]
        return wo_all.at[owner, pl.ds(pl.multiple_of(start + side * (quarter // 2), 16), quarter // 2)]

    def y_quarter():
        for side, target in ((0, y_next), (1, y_before)):
            start = pl.multiple_of(x_at * quarter + side * (quarter // 2), 16)
            part = wo_ref.at[pl.ds(start, quarter // 2)]
            started.append(
                send(part, part_rows(tok, 0, side), wo_send.at[side], wo_recv.at[side], target, z, across)
            )

    def x_ring_first():
        for side in range(2):
            landed(part_rows(across, 0, side), wo_recv.at[side])
        mine = part_rows(across, 0, None)
        for k, target in ((2, x_next), (3, x_before)):
            started.append(send(mine, mine, wo_send.at[k], wo_recv.at[k], target, z, tok))

    def x_ring_second():
        for k, shift, side, target in ((4, -1, 0, x_next), (5, 1, 1, x_before)):
            landed(part_rows(across, shift, None), wo_recv.at[k - 2])
            half_part = part_rows(across, shift, side)
            started.append(send(half_part, half_part, wo_send.at[k], wo_recv.at[k], target, z, tok))

    def share(k, block):
        started.append(send(block, block, wo_send.at[k], wo_recv.at[k], place, z, sibling))

    for c in range(CHUNKS):
        landed(x_rows(sibling, c), tok_recv.at[0, c])
    keys_values(0)
    pass_on(1, 0)
    for c in range(CHUNKS):
        theirs = x_rows(across, c)
        landed(theirs, tok_recv.at[1, c])
        started.append(send(theirs, theirs, tok_send.at[2, c], tok_recv.at[2, c], place, z, sibling))
    y_quarter()
    for c in range(CHUNKS):
        landed(x_rows(sibling_across, c), tok_recv.at[2, c])
    keys_values(1)
    pass_on(1, 1)

    courier_send()
    started.append(send(wo_ref, wo_all.at[tok], wo_send.at[6], wo_recv.at[6], place, z, sibling))
    x_ring_first()

    weights[-1].wait()
    x = x_buf[...]
    for i in range(pairs):
        q = jnp.dot(x, wq_buf[:, i * pair : (i + 1) * pair], preferred_element_type=jnp.float32)
        for j in range(2):
            d = 2 * i + j
            qn = layer_norm(q[:, j * HDIM : (j + 1) * HDIM]) * qg_ref[...]
            qn = qn.astype(jnp.bfloat16).astype(jnp.float32) * HDIM ** (-0.5)
            q_buf[d] = jnp.concatenate([qn[:half], qn[half:]], axis=1).astype(jnp.bfloat16)
            stays = jnp.logical_and(d == place, after_z == z)

            @pl.when(jnp.logical_not(stays))
            def _():
                send(
                    q_buf.at[d], q_all.at[after_place], q_send.at[d], q_recv.at[after_place], d, after_z, tok
                )

            @pl.when(stays)
            def _():
                pltpu.make_async_copy(q_buf.at[d], q_all.at[after_place], q_recv.at[after_place]).start()

    @pl.when(jnp.logical_not(detour))
    def _():
        send(frames_ref, prev_frames, prev_send.at[1], prev_recv.at[1], after_place, after_z, tok)

    for hop in range(2, last + 1):
        for n in range(2):
            pass_on(hop, n)
        if hop == 2:
            share(7, part_rows(across, 0, None))
            x_ring_second()
        elif hop == 3:
            share(8, part_rows(across, -1, None))
            share(9, part_rows(across, 1, None))
    for k in (4, 5):
        landed(part_rows(across, 2, k - 4), wo_recv.at[k])
    share(10, part_rows(across, 2, None))

    for p in range(PLACES):
        landed(rows_got.at[p], row_recv.at[p])
    table = rows_got[:, 0, :]
    lanes = table.shape[1]
    lane = lax.broadcasted_iota(jnp.int32, (PLACES, lanes), 1)
    seen = jnp.where(jnp.logical_and(table > 0, lane < slots), 1.0, 0.0)
    by_row = lax.broadcasted_iota(jnp.int32, (lanes, lanes), 0)
    by_lane = lax.broadcasted_iota(jnp.int32, (lanes, lanes), 1)
    ahead = jnp.where(by_row < by_lane, 1.0, 0.0)
    rank = jnp.dot(seen, ahead, preferred_element_type=jnp.float32)
    spot = jnp.where(seen > 0, rank, -1.0)
    spot_t = jnp.transpose(jnp.concatenate([spot] * (lanes // PLACES), axis=0))
    kept_at = ((by_row >> 1) & (NZ - 1)) * PLACES + (by_row >> 4) * NYH + (by_row & 1)
    kept_at = kept_at.astype(jnp.float32)
    lane_f = by_lane.astype(jnp.float32)
    listed = [
        jnp.sum(jnp.where(spot_t[:, p : p + 1] == lane_f, kept_at, 0.0), axis=0, keepdims=True)
        for p in range(PLACES)
    ]
    listed = jnp.concatenate(listed, axis=0).astype(jnp.int32)
    count = jnp.sum(seen, axis=1, keepdims=True).astype(jnp.int32)
    count = jnp.where(place < HEADS_HERE, count, 0)
    info_ref[...] = jnp.where(lane == slots, count, listed)

    @pl.when(place < HEADS_HERE)
    def _():
        opposite = lax.rem(z + last, NZ)
        for n in range(2):
            for c in range(PLACES):
                for way in range(2):
                    @pl.when(goes(last, way, c))
                    def _():
                        landed(part_of(kv_all.at[opposite, c], n), ring_recv.at[way, last - 1, n, c])
        for p in range(PLACES):
            landed(q_all.at[p], q_recv.at[p])
        for hop in range(1, last + 1):
            for n in range(2):
                for c in range(PLACES):
                    for way in range(2):
                        @pl.when(goes(hop, way, c))
                        def _():
                            ring_copy(hop, way, n, c).wait_send()

    landed(prev_gate, prev_recv.at[0])
    landed(prev_frames, prev_recv.at[1])
    landed(frames_ref, prev_send.at[1])

    @pl.when(place == courier)
    def _():
        for x_from in range(NX - 1):
            landed(frames_way.at[x_from], way_send.at[x_from])

    landed(wo_all.at[sibling], wo_recv.at[6])
    for k, shift in ((7, 0), (8, -1), (9, 1), (10, 2)):
        landed(part_rows(sibling_across, shift, None), wo_recv.at[k])
    for copy in started:
        copy.wait_send()
    for d in range(PLACES):
        @pl.when(jnp.logical_not(jnp.logical_and(d == place, after_z == z)))
        def _():
            landed(row_buf, row_send.at[d])
            if d < HEADS_HERE:
                landed(q_buf.at[d], q_send.at[d])

    for d in range(HEADS_HERE):
        for n in range(2):
            @pl.when(d != place)
            def _():
                landed(part_of(kv_buf.at[d], n), kv_send.at[d, n])


def gather(frames, shift, scale, gate, mask, wq, wk, wv, wo, query_gain, key_gain):
    rows, width = frames.shape
    tokens = rows * 4
    pair = 2 * HDIM
    vmem, hbm = pl.BlockSpec(memory_space=pltpu.VMEM), pl.BlockSpec(memory_space=pl.ANY)
    dma = pltpu.SemaphoreType.DMA
    return pl.pallas_call(
        gather_kernel,
        in_specs=[vmem, vmem, vmem, vmem, vmem, hbm, hbm, hbm, hbm, vmem, vmem],
        out_specs=[hbm, hbm, vmem, hbm, vmem, hbm],
        out_shape=[
            jax.ShapeDtypeStruct((PLACES, tokens // 2, pair), jnp.bfloat16),
            jax.ShapeDtypeStruct((NZ, PLACES, tokens, pair), jnp.bfloat16),
            jax.ShapeDtypeStruct((PLACES, 128), jnp.int32),
            jax.ShapeDtypeStruct(frames.shape, jnp.bfloat16),
            jax.ShapeDtypeStruct(gate.shape, jnp.float32),
            jax.ShapeDtypeStruct((4,) + wo.shape, jnp.bfloat16),
        ],
        scratch_shapes=[
            pltpu.VMEM((tokens, width), jnp.bfloat16),
            pltpu.VMEM(wq.shape, jnp.bfloat16),
            pltpu.VMEM((HEADS_HERE // 2, width, 2 * pair), jnp.bfloat16),
            pltpu.VMEM((HEADS_HERE, tokens // 2, pair), jnp.bfloat16),
            pltpu.VMEM((HEADS_HERE, tokens, pair), jnp.bfloat16),
            pltpu.VMEM((8, 128), jnp.int32),
            pltpu.VMEM((PLACES, 8, 128), jnp.int32),
            pltpu.VMEM((NX - 1,) + frames.shape, jnp.bfloat16),
            dma,
            dma((HEADS_HERE // 2, 2)),
            dma((3, CHUNKS)),
            dma((3, CHUNKS)),
            dma((PLACES,)),
            dma((PLACES,)),
            dma((HEADS_HERE, 2)),
            dma((PLACES, 2)),
            dma((HEADS_HERE,)),
            dma((PLACES,)),
            dma((2, NZ // 2, 2, PLACES)),
            dma((2, NZ // 2, 2, PLACES)),
            dma((2,)),
            dma((2,)),
            dma((11,)),
            dma((11,)),
            dma((NX - 1,)),
            dma((NX - 1,)),
        ],
        compiler_params=pltpu.CompilerParams(
            collective_id=0, has_side_effects=True, vmem_limit_bytes=52 * 1024 * 1024
        ),
    )(frames, shift, scale, gate, mask, wq, wk, wv, wo, query_gain.reshape(1, HDIM), key_gain.reshape(1, HDIM))


def attend_kernel(info_ref, q_ref, kv_ref, out_ref):
    frames_here, half, lanes = q_ref.shape
    rows = 2 * half
    slots = kv_ref.shape[0]
    low = lax.broadcasted_iota(jnp.int32, (half, lanes), 1) < HDIM

    def one_frame(i, _):
        packed = q_ref[i].astype(jnp.float32)
        top = jnp.where(low, packed, 0.0)
        bottom = jnp.where(low, pltpu.roll(packed, HDIM, 1), 0.0)
        q = jnp.concatenate([top, bottom], axis=0).astype(jnp.bfloat16)

        def blocks(state, *numbers):
            running_max, running_sum, weighted = state
            kvs = [kv_ref[info_ref[i, j]] for j in numbers]
            scores = [
                lax.dot_general(kv, q, (((1,), (1,)), ((), ())), preferred_element_type=jnp.float32) for kv in kvs
            ]
            new_max = running_max
            for s in scores:
                new_max = jnp.maximum(new_max, jnp.max(s, axis=0, keepdims=True))
            rescale = jnp.exp(running_max - new_max)
            running_sum, weighted = running_sum * rescale, weighted * rescale
            for kv, s in zip(kvs, scores):
                weights = jnp.exp(s - new_max)
                running_sum = running_sum + jnp.sum(weights, axis=0, keepdims=True)
                weighted = weighted + lax.dot_general(
                    kv, weights.astype(jnp.bfloat16), (((0,), (0,)), ((), ())), preferred_element_type=jnp.float32
                )
            return new_max, running_sum, weighted

        state = (
            jnp.full((1, rows), -1e30, jnp.float32),
            jnp.zeros((1, rows), jnp.float32),
            jnp.zeros((lanes, rows), jnp.float32),
        )
        count = info_ref[i, slots]
        twos = count // 2
        state = lax.fori_loop(0, twos, lambda j, s: blocks(s, 2 * j, 2 * j + 1), state)
        _, total, weighted = lax.fori_loop(2 * twos, count, lambda j, s: blocks(s, j), state)
        attended = jnp.transpose(weighted[HDIM:] / total)
        chunk = rows // 4
        for c in range(4):
            part = attended[c * chunk : (c + 1) * chunk]
            out_ref[i, c] = jnp.concatenate([part[: chunk // 2], part[chunk // 2 :]], axis=1).astype(jnp.bfloat16)
        return 0

    lax.fori_loop(0, frames_here, one_frame, 0)


def attend(info, q, kv):
    frames_here, half, lanes = q.shape
    return pl.pallas_call(
        attend_kernel,
        grid_spec=pltpu.PrefetchScalarGridSpec(
            num_scalar_prefetch=1,
            grid=(1,),
            in_specs=[pl.BlockSpec(memory_space=pltpu.VMEM)] * 2,
            out_specs=pl.BlockSpec((frames_here, 4, half // 4, lanes), lambda i, *_: (0, 0, 0, 0)),
        ),
        out_shape=jax.ShapeDtypeStruct((frames_here, 4, half // 4, lanes), jnp.bfloat16),
        compiler_params=pltpu.CompilerParams(vmem_limit_bytes=40 * 1024 * 1024),
    )(info, q, kv)


def finish_kernel(
    att_ref, w_ref, own_ref, frames_ref, gate_ref, out_ref, got, att_buf, w_buf, w_sem, send_sem, recv_sem
):
    place, z, tok = positions()
    width = out_ref.shape[1]
    tile = width // TILES
    rows = own_ref.shape[0]
    weights = []
    for n in range(TILES):
        cols = pl.ds(n * tile, tile)
        for other in range(4):
            block = lax.rem(tok + other, 4)
            source = own_ref.at[:, cols] if other == 0 else w_ref.at[block, :, cols]
            place_in = w_buf.at[n, pl.ds(pl.multiple_of(block * rows, rows), rows)]
            weights.append(pltpu.make_async_copy(source, place_in, w_sem.at[n, other]))
    for copy in weights:
        copy.start()
    barrier = pltpu.get_barrier_semaphore()
    for p in range(PLACES):
        for t in range(4):
            @pl.when(jnp.logical_not(jnp.logical_and(p == place, t == tok)))
            def _():
                pl.semaphore_signal(barrier, inc=1, device_id=(queue_index(p, z), t), device_id_type=MESH)
    pl.semaphore_wait(barrier, 4 * PLACES - 1)

    slot = tok * HEADS_HERE + place

    @pl.when(place < HEADS_HERE)
    def _():
        for p in range(PLACES):
            for t in range(4):
                here = jnp.logical_and(p == place, t == tok)

                @pl.when(jnp.logical_not(here))
                def _():
                    send(att_ref.at[p, t], got.at[slot], send_sem.at[p, t], recv_sem.at[slot], p, z, t)

                @pl.when(here)
                def _():
                    pltpu.make_async_copy(att_ref.at[p, t], got.at[slot], recv_sem.at[slot]).start()

    heads, half, lanes = got.shape
    low = lax.broadcasted_iota(jnp.int32, (half, lanes), 1) < HDIM
    for m in range(heads // 2):
        landed(got.at[2 * m], recv_sem.at[2 * m])
        landed(got.at[2 * m + 1], recv_sem.at[2 * m + 1])
        first, second = got[2 * m].astype(jnp.float32), got[2 * m + 1].astype(jnp.float32)
        cols = slice(m * lanes, (m + 1) * lanes)
        att_buf[:half, cols] = jnp.where(low, first, pltpu.roll(second, HDIM, 1)).astype(jnp.bfloat16)
        att_buf[half:, cols] = jnp.where(low, pltpu.roll(first, HDIM, 1), second).astype(jnp.bfloat16)
    attended = att_buf[...]
    for n in range(TILES):
        for copy in weights[4 * n : 4 * n + 4]:
            copy.wait()
        projected = jnp.dot(attended, w_buf[n], preferred_element_type=jnp.float32)
        cols = slice(n * tile, (n + 1) * tile)
        updated = frames_ref[:, cols].astype(jnp.float32) + gate_ref[:, cols] * projected
        out_ref[:, cols] = updated.astype(jnp.bfloat16)

    @pl.when(place < HEADS_HERE)
    def _():
        for p in range(PLACES):
            for t in range(4):
                @pl.when(jnp.logical_not(jnp.logical_and(p == place, t == tok)))
                def _():
                    landed(att_ref.at[p, t], send_sem.at[p, t])


def finish(attended, w_all, w_own, frames, gate):
    vmem, hbm = pl.BlockSpec(memory_space=pltpu.VMEM), pl.BlockSpec(memory_space=pl.ANY)
    dma = pltpu.SemaphoreType.DMA
    depth, width = 4 * w_own.shape[0], w_own.shape[1]
    return pl.pallas_call(
        finish_kernel,
        in_specs=[hbm, hbm, hbm, vmem, vmem],
        out_specs=vmem,
        out_shape=jax.ShapeDtypeStruct(frames.shape, jnp.bfloat16),
        scratch_shapes=[
            pltpu.VMEM((4 * HEADS_HERE,) + attended.shape[2:], jnp.bfloat16),
            pltpu.VMEM((frames.shape[0], depth), jnp.bfloat16),
            pltpu.VMEM((TILES, depth, width // TILES), jnp.bfloat16),
            dma((TILES, 4)),
            dma((PLACES, 4)),
            dma((4 * HEADS_HERE,)),
        ],
        compiler_params=pltpu.CompilerParams(
            collective_id=1, has_side_effects=True, vmem_limit_bytes=48 * 1024 * 1024
        ),
    )(attended, w_all, w_own, frames, gate)


def body(
    frames, levels, frame_mask, modulation, w_query, w_key, w_value, w_out, query_gain, key_gain
):
    width = frames.shape[2]
    slots = frame_mask.shape[1]
    own = lax.dynamic_slice(modulation, (levels[0], 0), (1, 3 * width)).astype(jnp.float32)
    q, kv, info, prev_frames, prev_gate, w_all = gather(
        frames[0], own[:, :width], own[:, width : 2 * width], own[:, 2 * width :], frame_mask,
        w_query, w_key, w_value, w_out, query_gain, key_gain,
    )
    attended = attend(info, q, kv.reshape((slots,) + kv.shape[2:]))
    return finish(attended, w_all, w_out, prev_frames, prev_gate)[None]


def solution(mesh):
    return jax.shard_map(
        body,
        mesh=mesh,
        in_specs=(
            P("queue", "tok", None),
            P("queue"),
            P("queue", None),
            P(),
            P(None, "tok"),
            P(None, "tok"),
            P(None, "tok"),
            P("tok", None),
            P(),
            P(),
        ),
        out_specs=P("queue", "tok", None),
        check_vma=False,
    )
```

```python
import jax
import jax.numpy as jnp
from jax import lax
from jax.experimental import pallas as pl
from jax.experimental.pallas import tpu as pltpu
from jax.sharding import PartitionSpec as P

HDIM = 64
NX, NZ, NYH = 4, 8, 2
PLACES = NX * NYH
HEADS_HERE = 6
CHUNKS = 4
TILES = 6
MESH = pl.DeviceIdType.MESH


def queue_index(place, z):
    return ((place // NYH) * NZ + z) * NYH + place % NYH


def layer_norm(values_in):
    center = jnp.mean(values_in, axis=-1, keepdims=True)
    spread = jnp.mean(jnp.square(values_in - center), axis=-1, keepdims=True)
    return (values_in - center) * lax.rsqrt(spread + 1e-06)


def positions():
    q_at = lax.axis_index("queue")
    return (q_at // (NZ * NYH)) * NYH + q_at % NYH, (q_at // NYH) % NZ, lax.axis_index("tok")


def send(src, dst, send_sem, recv_sem, place, z, tok):
    copy = pltpu.make_async_remote_copy(
        src_ref=src,
        dst_ref=dst,
        send_sem=send_sem,
        recv_sem=recv_sem,
        device_id=(queue_index(place, z), tok),
        device_id_type=MESH,
    )
    copy.start()
    return copy


def landed(ref, sem):
    pltpu.make_async_copy(ref, ref, sem).wait()


def gather_kernel(
    frames_ref, shift_ref, scale_ref, gate_ref, mask_ref, wq_ref, wk_ref, wv_ref, wo_ref, qg_ref, kg_ref,
    q_all, kv_all, info_ref, prev_frames, prev_gate, wo_all,
    x_buf, wq_buf, wkv_buf, q_buf, kv_buf, row_buf, rows_got,
    wq_sem, wkv_sem, tok_send, tok_recv, row_send, row_recv, kv_send, kv_recv, q_send, q_recv,
    ring_send, ring_recv, prev_send, prev_recv, wo_send, wo_recv,
):
    place, z, tok = positions()
    up, down = lax.rem(z + 1, NZ), lax.rem(z + NZ - 1, NZ)
    sibling = tok + 1 - 2 * lax.rem(tok, 2)
    across = lax.rem(tok + 2, 4)
    sibling_across = lax.rem(sibling + 2, 4)
    pair = 2 * HDIM
    pairs = HEADS_HERE // 2
    weights = []
    for i in range(pairs):
        for j, w in enumerate((wk_ref, wv_ref)):
            weights.append(
                pltpu.make_async_copy(
                    w.at[:, pl.ds(i * pair, pair)], wkv_buf.at[i, :, pl.ds(j * pair, pair)], wkv_sem.at[i, j]
                )
            )
    weights.append(pltpu.make_async_copy(wq_ref, wq_buf, wq_sem))
    for copy in weights:
        copy.start()
    twin = place + 1 - 2 * lax.rem(place, NYH)

    barrier = pltpu.get_barrier_semaphore()
    for other_tok in (sibling, across):
        pl.semaphore_signal(
            barrier, inc=1, device_id=(queue_index(place, z), other_tok), device_id_type=MESH
        )
    pl.semaphore_signal(barrier, inc=1, device_id=(queue_index(twin, z), across), device_id_type=MESH)
    for p in range(PLACES):
        for other_z in (up, down):
            pl.semaphore_signal(barrier, inc=1, device_id=(queue_index(p, other_z), tok), device_id_type=MESH)

        @pl.when(p != place)
        def _():
            pl.semaphore_signal(barrier, inc=1, device_id=(queue_index(p, z), tok), device_id_type=MESH)

    rows = frames_ref.shape[0]
    step = rows // CHUNKS

    def x_rows(owner, c):
        return x_buf.at[pl.ds(pl.multiple_of(owner * rows + c * step, step), step)]

    started = []
    for c in range(CHUNKS):
        part = layer_norm(frames_ref[c * step : (c + 1) * step].astype(jnp.float32))
        part = part * (1.0 + scale_ref[...]) + shift_ref[...]
        x_buf[pl.ds(pl.multiple_of(tok * rows + c * step, step), step)] = part.astype(jnp.bfloat16)
        if c == 0:
            pl.semaphore_wait(barrier, 3 + 3 * PLACES - 1)
        for way, other_tok in ((1, across), (0, sibling)):
            mine = x_rows(tok, c)
            started.append(send(mine, mine, tok_send.at[way, c], tok_recv.at[way, c], place, z, other_tok))

    after = lax.rem(queue_index(place, z) + 1, NX * NZ * NYH)
    after_place = (after // (NZ * NYH)) * NYH + after % NYH
    after_z = (after // NYH) % NZ
    slots = mask_ref.shape[1]
    row_buf[...] = jnp.zeros_like(row_buf)
    row_buf[0:1, :slots] = mask_ref[...]
    for d in range(PLACES):
        stays = jnp.logical_and(d == place, after_z == z)

        @pl.when(jnp.logical_not(stays))
        def _():
            send(row_buf, rows_got.at[after_place], row_send.at[d], row_recv.at[after_place], d, after_z, tok)

        @pl.when(stays)
        def _():
            pltpu.make_async_copy(row_buf, rows_got.at[after_place], row_recv.at[after_place]).start()

    started.append(
        send(gate_ref, prev_gate, prev_send.at[0], prev_recv.at[0], after_place, after_z, tok)
    )

    half = x_buf.shape[0] // 2
    first = tok // 2
    at = [pl.multiple_of(first * half, half), pl.multiple_of((1 - first) * half, half)]

    def part_of(ref, n):
        return ref.at[pl.ds(at[n], half)]

    def keys_values(n):
        x = x_buf[pl.ds(at[n], half)]
        for i in range(pairs):
            if n == 0:
                weights[2 * i].wait()
                weights[2 * i + 1].wait()
            both = jnp.dot(x, wkv_buf[i], preferred_element_type=jnp.float32)
            for j in range(2):
                d = 2 * i + j
                kn = layer_norm(both[:, j * HDIM : (j + 1) * HDIM]) * kg_ref[...]
                v = both[:, pair + j * HDIM : pair + (j + 1) * HDIM]
                kv_buf[d, pl.ds(at[n], half)] = jnp.concatenate([kn, v], axis=1).astype(jnp.bfloat16)
                block = part_of(kv_buf.at[d], n)
                here = part_of(kv_all.at[z, place], n)

                @pl.when(d != place)
                def _():
                    send(block, here, kv_send.at[d, n], kv_recv.at[place, n], d, z, tok)

                @pl.when(d == place)
                def _():
                    pltpu.make_async_copy(block, here, kv_recv.at[place, n]).start()

    last = NZ // 2

    def ring_copy(hop, way, n, c):
        source = lax.rem(z + NZ - (hop - 1), NZ) if way == 0 else lax.rem(z + hop - 1, NZ)
        block = part_of(kv_all.at[source, c], n)
        return pltpu.make_async_remote_copy(
            src_ref=block,
            dst_ref=block,
            send_sem=ring_send.at[way, hop - 1, n, c],
            recv_sem=ring_recv.at[way, hop - 1, n, c],
            device_id=(queue_index(place, down if way else up), tok),
            device_id_type=MESH,
        )

    last_up = jnp.where(lax.rem(place, NYH) == 1, 0, PLACES // 2)

    def goes(hop, way, c):
        if hop < last:
            return True
        return c < last_up if way == 0 else c >= last_up

    def pass_on(hop, n):
        @pl.when(place < HEADS_HERE)
        def _():
            for c in range(PLACES):
                if hop == 1:
                    landed(part_of(kv_all.at[z, c], n), kv_recv.at[c, n])
                for way in range(2):
                    if hop > 1:
                        source = lax.rem(z + NZ - (hop - 1), NZ) if way == 0 else lax.rem(z + hop - 1, NZ)
                        landed(part_of(kv_all.at[source, c], n), ring_recv.at[way, hop - 2, n, c])

                    @pl.when(goes(hop, way, c))
                    def _():
                        ring_copy(hop, way, n, c).start()

    rows_here = wo_ref.shape[0]
    quarter = rows_here // NX
    x_at = place // NYH
    x_next = lax.rem(place + NYH, PLACES)
    x_before = lax.rem(place + PLACES - NYH, PLACES)
    lower = tok // 2 == 0
    y_next = jnp.where(lower, place, twin)
    y_before = jnp.where(lower, twin, place)

    def part_rows(owner, shift, side):
        start = lax.rem(x_at + shift + NX, NX) * quarter
        if side is None:
            return wo_all.at[owner, pl.ds(pl.multiple_of(start, 16), quarter)]
        return wo_all.at[owner, pl.ds(pl.multiple_of(start + side * (quarter // 2), 16), quarter // 2)]

    def y_quarter():
        for side, target in ((0, y_next), (1, y_before)):
            start = pl.multiple_of(x_at * quarter + side * (quarter // 2), 16)
            part = wo_ref.at[pl.ds(start, quarter // 2)]
            started.append(
                send(part, part_rows(tok, 0, side), wo_send.at[side], wo_recv.at[side], target, z, across)
            )

    def x_ring_first():
        for side in range(2):
            landed(part_rows(across, 0, side), wo_recv.at[side])
        mine = part_rows(across, 0, None)
        for k, target in ((2, x_next), (3, x_before)):
            started.append(send(mine, mine, wo_send.at[k], wo_recv.at[k], target, z, tok))

    def x_ring_second():
        for k, shift, side, target in ((4, -1, 0, x_next), (5, 1, 1, x_before)):
            landed(part_rows(across, shift, None), wo_recv.at[k - 2])
            half_part = part_rows(across, shift, side)
            started.append(send(half_part, half_part, wo_send.at[k], wo_recv.at[k], target, z, tok))

    def share(k, block):
        started.append(send(block, block, wo_send.at[k], wo_recv.at[k], place, z, sibling))

    for c in range(CHUNKS):
        landed(x_rows(sibling, c), tok_recv.at[0, c])
    keys_values(0)
    pass_on(1, 0)
    for c in range(CHUNKS):
        theirs = x_rows(across, c)
        landed(theirs, tok_recv.at[1, c])
        started.append(send(theirs, theirs, tok_send.at[2, c], tok_recv.at[2, c], place, z, sibling))
    y_quarter()
    for c in range(CHUNKS):
        landed(x_rows(sibling_across, c), tok_recv.at[2, c])
    keys_values(1)
    pass_on(1, 1)

    started.append(send(wo_ref, wo_all.at[tok], wo_send.at[6], wo_recv.at[6], place, z, sibling))
    x_ring_first()

    weights[-1].wait()
    x = x_buf[...]
    for i in range(pairs):
        q = jnp.dot(x, wq_buf[:, i * pair : (i + 1) * pair], preferred_element_type=jnp.float32)
        for j in range(2):
            d = 2 * i + j
            qn = layer_norm(q[:, j * HDIM : (j + 1) * HDIM]) * qg_ref[...]
            qn = qn.astype(jnp.bfloat16).astype(jnp.float32) * HDIM ** (-0.5)
            q_buf[d] = jnp.concatenate([qn[:half], qn[half:]], axis=1).astype(jnp.bfloat16)
            stays = jnp.logical_and(d == place, after_z == z)

            @pl.when(jnp.logical_not(stays))
            def _():
                send(
                    q_buf.at[d], q_all.at[after_place], q_send.at[d], q_recv.at[after_place], d, after_z, tok
                )

            @pl.when(stays)
            def _():
                pltpu.make_async_copy(q_buf.at[d], q_all.at[after_place], q_recv.at[after_place]).start()

    started.append(
        send(frames_ref, prev_frames, prev_send.at[1], prev_recv.at[1], after_place, after_z, tok)
    )
    for hop in range(2, last + 1):
        for n in range(2):
            pass_on(hop, n)
        if hop == 2:
            share(7, part_rows(across, 0, None))
            x_ring_second()
        elif hop == 3:
            share(8, part_rows(across, -1, None))
            share(9, part_rows(across, 1, None))
    for k in (4, 5):
        landed(part_rows(across, 2, k - 4), wo_recv.at[k])
    share(10, part_rows(across, 2, None))

    for p in range(PLACES):
        landed(rows_got.at[p], row_recv.at[p])
    table = rows_got[:, 0, :]
    lanes = table.shape[1]
    lane = lax.broadcasted_iota(jnp.int32, (PLACES, lanes), 1)
    seen = jnp.where(jnp.logical_and(table > 0, lane < slots), 1.0, 0.0)
    by_row = lax.broadcasted_iota(jnp.int32, (lanes, lanes), 0)
    by_lane = lax.broadcasted_iota(jnp.int32, (lanes, lanes), 1)
    ahead = jnp.where(by_row < by_lane, 1.0, 0.0)
    rank = jnp.dot(seen, ahead, preferred_element_type=jnp.float32)
    spot = jnp.where(seen > 0, rank, -1.0)
    spot_t = jnp.transpose(jnp.concatenate([spot] * (lanes // PLACES), axis=0))
    kept_at = ((by_row >> 1) & (NZ - 1)) * PLACES + (by_row >> 4) * NYH + (by_row & 1)
    kept_at = kept_at.astype(jnp.float32)
    lane_f = by_lane.astype(jnp.float32)
    listed = [
        jnp.sum(jnp.where(spot_t[:, p : p + 1] == lane_f, kept_at, 0.0), axis=0, keepdims=True)
        for p in range(PLACES)
    ]
    listed = jnp.concatenate(listed, axis=0).astype(jnp.int32)
    count = jnp.sum(seen, axis=1, keepdims=True).astype(jnp.int32)
    count = jnp.where(place < HEADS_HERE, count, 0)
    info_ref[...] = jnp.where(lane == slots, count, listed)

    @pl.when(place < HEADS_HERE)
    def _():
        opposite = lax.rem(z + last, NZ)
        for n in range(2):
            for c in range(PLACES):
                for way in range(2):
                    @pl.when(goes(last, way, c))
                    def _():
                        landed(part_of(kv_all.at[opposite, c], n), ring_recv.at[way, last - 1, n, c])
        for p in range(PLACES):
            landed(q_all.at[p], q_recv.at[p])
        for hop in range(1, last + 1):
            for n in range(2):
                for c in range(PLACES):
                    for way in range(2):
                        @pl.when(goes(hop, way, c))
                        def _():
                            ring_copy(hop, way, n, c).wait_send()

    landed(prev_gate, prev_recv.at[0])
    landed(prev_frames, prev_recv.at[1])
    landed(wo_all.at[sibling], wo_recv.at[6])
    for k, shift in ((7, 0), (8, -1), (9, 1), (10, 2)):
        landed(part_rows(sibling_across, shift, None), wo_recv.at[k])
    for copy in started:
        copy.wait_send()
    for d in range(PLACES):
        @pl.when(jnp.logical_not(jnp.logical_and(d == place, after_z == z)))
        def _():
            landed(row_buf, row_send.at[d])
            if d < HEADS_HERE:
                landed(q_buf.at[d], q_send.at[d])

    for d in range(HEADS_HERE):
        for n in range(2):
            @pl.when(d != place)
            def _():
                landed(part_of(kv_buf.at[d], n), kv_send.at[d, n])


def gather(frames, shift, scale, gate, mask, wq, wk, wv, wo, query_gain, key_gain):
    rows, width = frames.shape
    tokens = rows * 4
    pair = 2 * HDIM
    vmem, hbm = pl.BlockSpec(memory_space=pltpu.VMEM), pl.BlockSpec(memory_space=pl.ANY)
    dma = pltpu.SemaphoreType.DMA
    return pl.pallas_call(
        gather_kernel,
        in_specs=[vmem, vmem, vmem, vmem, vmem, hbm, hbm, hbm, hbm, vmem, vmem],
        out_specs=[hbm, hbm, vmem, hbm, vmem, hbm],
        out_shape=[
            jax.ShapeDtypeStruct((PLACES, tokens // 2, pair), jnp.bfloat16),
            jax.ShapeDtypeStruct((NZ, PLACES, tokens, pair), jnp.bfloat16),
            jax.ShapeDtypeStruct((PLACES, 128), jnp.int32),
            jax.ShapeDtypeStruct(frames.shape, jnp.bfloat16),
            jax.ShapeDtypeStruct(gate.shape, jnp.float32),
            jax.ShapeDtypeStruct((4,) + wo.shape, jnp.bfloat16),
        ],
        scratch_shapes=[
            pltpu.VMEM((tokens, width), jnp.bfloat16),
            pltpu.VMEM(wq.shape, jnp.bfloat16),
            pltpu.VMEM((HEADS_HERE // 2, width, 2 * pair), jnp.bfloat16),
            pltpu.VMEM((HEADS_HERE, tokens // 2, pair), jnp.bfloat16),
            pltpu.VMEM((HEADS_HERE, tokens, pair), jnp.bfloat16),
            pltpu.VMEM((8, 128), jnp.int32),
            pltpu.VMEM((PLACES, 8, 128), jnp.int32),
            dma,
            dma((HEADS_HERE // 2, 2)),
            dma((3, CHUNKS)),
            dma((3, CHUNKS)),
            dma((PLACES,)),
            dma((PLACES,)),
            dma((HEADS_HERE, 2)),
            dma((PLACES, 2)),
            dma((HEADS_HERE,)),
            dma((PLACES,)),
            dma((2, NZ // 2, 2, PLACES)),
            dma((2, NZ // 2, 2, PLACES)),
            dma((2,)),
            dma((2,)),
            dma((11,)),
            dma((11,)),
        ],
        compiler_params=pltpu.CompilerParams(
            collective_id=0, has_side_effects=True, vmem_limit_bytes=52 * 1024 * 1024
        ),
    )(frames, shift, scale, gate, mask, wq, wk, wv, wo, query_gain.reshape(1, HDIM), key_gain.reshape(1, HDIM))


def attend_kernel(info_ref, q_ref, kv_ref, out_ref):
    frames_here, half, lanes = q_ref.shape
    rows = 2 * half
    slots = kv_ref.shape[0]
    low = lax.broadcasted_iota(jnp.int32, (half, lanes), 1) < HDIM

    def one_frame(i, _):
        packed = q_ref[i].astype(jnp.float32)
        top = jnp.where(low, packed, 0.0)
        bottom = jnp.where(low, pltpu.roll(packed, HDIM, 1), 0.0)
        q = jnp.concatenate([top, bottom], axis=0).astype(jnp.bfloat16)

        def blocks(state, *numbers):
            running_max, running_sum, weighted = state
            kvs = [kv_ref[info_ref[i, j]] for j in numbers]
            scores = [
                lax.dot_general(kv, q, (((1,), (1,)), ((), ())), preferred_element_type=jnp.float32) for kv in kvs
            ]
            new_max = running_max
            for s in scores:
                new_max = jnp.maximum(new_max, jnp.max(s, axis=0, keepdims=True))
            rescale = jnp.exp(running_max - new_max)
            running_sum, weighted = running_sum * rescale, weighted * rescale
            for kv, s in zip(kvs, scores):
                weights = jnp.exp(s - new_max)
                running_sum = running_sum + jnp.sum(weights, axis=0, keepdims=True)
                weighted = weighted + lax.dot_general(
                    kv, weights.astype(jnp.bfloat16), (((0,), (0,)), ((), ())), preferred_element_type=jnp.float32
                )
            return new_max, running_sum, weighted

        state = (
            jnp.full((1, rows), -1e30, jnp.float32),
            jnp.zeros((1, rows), jnp.float32),
            jnp.zeros((lanes, rows), jnp.float32),
        )
        count = info_ref[i, slots]
        twos = count // 2
        state = lax.fori_loop(0, twos, lambda j, s: blocks(s, 2 * j, 2 * j + 1), state)
        _, total, weighted = lax.fori_loop(2 * twos, count, lambda j, s: blocks(s, j), state)
        attended = jnp.transpose(weighted[HDIM:] / total)
        chunk = rows // 4
        for c in range(4):
            part = attended[c * chunk : (c + 1) * chunk]
            out_ref[i, c] = jnp.concatenate([part[: chunk // 2], part[chunk // 2 :]], axis=1).astype(jnp.bfloat16)
        return 0

    lax.fori_loop(0, frames_here, one_frame, 0)


def attend(info, q, kv):
    frames_here, half, lanes = q.shape
    return pl.pallas_call(
        attend_kernel,
        grid_spec=pltpu.PrefetchScalarGridSpec(
            num_scalar_prefetch=1,
            grid=(1,),
            in_specs=[pl.BlockSpec(memory_space=pltpu.VMEM)] * 2,
            out_specs=pl.BlockSpec((frames_here, 4, half // 4, lanes), lambda i, *_: (0, 0, 0, 0)),
        ),
        out_shape=jax.ShapeDtypeStruct((frames_here, 4, half // 4, lanes), jnp.bfloat16),
        compiler_params=pltpu.CompilerParams(vmem_limit_bytes=40 * 1024 * 1024),
    )(info, q, kv)


def finish_kernel(
    att_ref, w_ref, own_ref, frames_ref, gate_ref, out_ref, got, att_buf, w_buf, w_sem, send_sem, recv_sem
):
    place, z, tok = positions()
    width = out_ref.shape[1]
    tile = width // TILES
    rows = own_ref.shape[0]
    weights = []
    for n in range(TILES):
        cols = pl.ds(n * tile, tile)
        for other in range(4):
            block = lax.rem(tok + other, 4)
            source = own_ref.at[:, cols] if other == 0 else w_ref.at[block, :, cols]
            place_in = w_buf.at[n, pl.ds(pl.multiple_of(block * rows, rows), rows)]
            weights.append(pltpu.make_async_copy(source, place_in, w_sem.at[n, other]))
    for copy in weights:
        copy.start()
    barrier = pltpu.get_barrier_semaphore()
    for p in range(PLACES):
        for t in range(4):
            @pl.when(jnp.logical_not(jnp.logical_and(p == place, t == tok)))
            def _():
                pl.semaphore_signal(barrier, inc=1, device_id=(queue_index(p, z), t), device_id_type=MESH)
    pl.semaphore_wait(barrier, 4 * PLACES - 1)

    slot = tok * HEADS_HERE + place

    @pl.when(place < HEADS_HERE)
    def _():
        for p in range(PLACES):
            for t in range(4):
                here = jnp.logical_and(p == place, t == tok)

                @pl.when(jnp.logical_not(here))
                def _():
                    send(att_ref.at[p, t], got.at[slot], send_sem.at[p, t], recv_sem.at[slot], p, z, t)

                @pl.when(here)
                def _():
                    pltpu.make_async_copy(att_ref.at[p, t], got.at[slot], recv_sem.at[slot]).start()

    heads, half, lanes = got.shape
    low = lax.broadcasted_iota(jnp.int32, (half, lanes), 1) < HDIM
    for m in range(heads // 2):
        landed(got.at[2 * m], recv_sem.at[2 * m])
        landed(got.at[2 * m + 1], recv_sem.at[2 * m + 1])
        first, second = got[2 * m].astype(jnp.float32), got[2 * m + 1].astype(jnp.float32)
        cols = slice(m * lanes, (m + 1) * lanes)
        att_buf[:half, cols] = jnp.where(low, first, pltpu.roll(second, HDIM, 1)).astype(jnp.bfloat16)
        att_buf[half:, cols] = jnp.where(low, pltpu.roll(first, HDIM, 1), second).astype(jnp.bfloat16)
    attended = att_buf[...]
    for n in range(TILES):
        for copy in weights[4 * n : 4 * n + 4]:
            copy.wait()
        projected = jnp.dot(attended, w_buf[n], preferred_element_type=jnp.float32)
        cols = slice(n * tile, (n + 1) * tile)
        updated = frames_ref[:, cols].astype(jnp.float32) + gate_ref[:, cols] * projected
        out_ref[:, cols] = updated.astype(jnp.bfloat16)

    @pl.when(place < HEADS_HERE)
    def _():
        for p in range(PLACES):
            for t in range(4):
                @pl.when(jnp.logical_not(jnp.logical_and(p == place, t == tok)))
                def _():
                    landed(att_ref.at[p, t], send_sem.at[p, t])


def finish(attended, w_all, w_own, frames, gate):
    vmem, hbm = pl.BlockSpec(memory_space=pltpu.VMEM), pl.BlockSpec(memory_space=pl.ANY)
    dma = pltpu.SemaphoreType.DMA
    depth, width = 4 * w_own.shape[0], w_own.shape[1]
    return pl.pallas_call(
        finish_kernel,
        in_specs=[hbm, hbm, hbm, vmem, vmem],
        out_specs=vmem,
        out_shape=jax.ShapeDtypeStruct(frames.shape, jnp.bfloat16),
        scratch_shapes=[
            pltpu.VMEM((4 * HEADS_HERE,) + attended.shape[2:], jnp.bfloat16),
            pltpu.VMEM((frames.shape[0], depth), jnp.bfloat16),
            pltpu.VMEM((TILES, depth, width // TILES), jnp.bfloat16),
            dma((TILES, 4)),
            dma((PLACES, 4)),
            dma((4 * HEADS_HERE,)),
        ],
        compiler_params=pltpu.CompilerParams(
            collective_id=1, has_side_effects=True, vmem_limit_bytes=48 * 1024 * 1024
        ),
    )(attended, w_all, w_own, frames, gate)


def body(
    frames, levels, frame_mask, modulation, w_query, w_key, w_value, w_out, query_gain, key_gain
):
    width = frames.shape[2]
    slots = frame_mask.shape[1]
    own = lax.dynamic_slice(modulation, (levels[0], 0), (1, 3 * width)).astype(jnp.float32)
    q, kv, info, prev_frames, prev_gate, w_all = gather(
        frames[0], own[:, :width], own[:, width : 2 * width], own[:, 2 * width :], frame_mask,
        w_query, w_key, w_value, w_out, query_gain, key_gain,
    )
    attended = attend(info, q, kv.reshape((slots,) + kv.shape[2:]))
    return finish(attended, w_all, w_out, prev_frames, prev_gate)[None]


def solution(mesh):
    return jax.shard_map(
        body,
        mesh=mesh,
        in_specs=(
            P("queue", "tok", None),
            P("queue"),
            P("queue", None),
            P(),
            P(None, "tok"),
            P(None, "tok"),
            P(None, "tok"),
            P("tok", None),
            P(),
            P(),
        ),
        out_specs=P("queue", "tok", None),
        check_vma=False,
    )
```

```python
import jax
import jax.numpy as jnp
from jax import lax
from jax.experimental import pallas as pl
from jax.experimental.pallas import tpu as pltpu
from jax.sharding import PartitionSpec as P

HDIM = 64
NX, NZ, NYH = 4, 8, 2
PLACES = NX * NYH
HEADS_HERE = 6
CHUNKS = 4
TILES = 6
MESH = pl.DeviceIdType.MESH


def queue_index(place, z):
    return ((place // NYH) * NZ + z) * NYH + place % NYH


def layer_norm(values_in):
    center = jnp.mean(values_in, axis=-1, keepdims=True)
    spread = jnp.mean(jnp.square(values_in - center), axis=-1, keepdims=True)
    return (values_in - center) * lax.rsqrt(spread + 1e-06)


def positions():
    q_at = lax.axis_index("queue")
    return (q_at // (NZ * NYH)) * NYH + q_at % NYH, (q_at // NYH) % NZ, lax.axis_index("tok")


def send(src, dst, send_sem, recv_sem, place, z, tok):
    copy = pltpu.make_async_remote_copy(
        src_ref=src,
        dst_ref=dst,
        send_sem=send_sem,
        recv_sem=recv_sem,
        device_id=(queue_index(place, z), tok),
        device_id_type=MESH,
    )
    copy.start()
    return copy


def landed(ref, sem):
    pltpu.make_async_copy(ref, ref, sem).wait()


def gather_kernel(
    frames_ref, shift_ref, scale_ref, gate_ref, mask_ref, wq_ref, wk_ref, wv_ref, wo_ref, qg_ref, kg_ref,
    q_all, kv_all, info_ref, prev_frames, prev_gate, wo_all,
    x_buf, wq_buf, wkv_buf, q_buf, kv_buf, row_buf, rows_got,
    wq_sem, wkv_sem, tok_send, tok_recv, row_send, row_recv, kv_send, kv_recv, q_send, q_recv,
    ring_send, ring_recv, prev_send, prev_recv, wo_send, wo_recv,
):
    place, z, tok = positions()
    up, down = lax.rem(z + 1, NZ), lax.rem(z + NZ - 1, NZ)
    sibling = tok + 1 - 2 * lax.rem(tok, 2)
    across = lax.rem(tok + 2, 4)
    sibling_across = lax.rem(sibling + 2, 4)
    pair = 2 * HDIM
    pairs = HEADS_HERE // 2
    weights = []
    for i in range(pairs):
        for j, w in enumerate((wk_ref, wv_ref)):
            weights.append(
                pltpu.make_async_copy(
                    w.at[:, pl.ds(i * pair, pair)], wkv_buf.at[i, :, pl.ds(j * pair, pair)], wkv_sem.at[i, j]
                )
            )
    weights.append(pltpu.make_async_copy(wq_ref, wq_buf, wq_sem))
    for copy in weights:
        copy.start()
    twin = place + 1 - 2 * lax.rem(place, NYH)

    barrier = pltpu.get_barrier_semaphore()
    for other_tok in (sibling, across):
        pl.semaphore_signal(
            barrier, inc=1, device_id=(queue_index(place, z), other_tok), device_id_type=MESH
        )
    pl.semaphore_signal(barrier, inc=1, device_id=(queue_index(twin, z), across), device_id_type=MESH)
    for p in range(PLACES):
        for other_z in (up, down):
            pl.semaphore_signal(barrier, inc=1, device_id=(queue_index(p, other_z), tok), device_id_type=MESH)

        @pl.when(p != place)
        def _():
            pl.semaphore_signal(barrier, inc=1, device_id=(queue_index(p, z), tok), device_id_type=MESH)

    rows = frames_ref.shape[0]
    step = rows // CHUNKS

    def x_rows(owner, c):
        return x_buf.at[pl.ds(pl.multiple_of(owner * rows + c * step, step), step)]

    started = []
    for c in range(CHUNKS):
        part = layer_norm(frames_ref[c * step : (c + 1) * step].astype(jnp.float32))
        part = part * (1.0 + scale_ref[...]) + shift_ref[...]
        x_buf[pl.ds(pl.multiple_of(tok * rows + c * step, step), step)] = part.astype(jnp.bfloat16)
        if c == 0:
            pl.semaphore_wait(barrier, 3 + 3 * PLACES - 1)
        for way, other_tok in ((1, across), (0, sibling)):
            mine = x_rows(tok, c)
            started.append(send(mine, mine, tok_send.at[way, c], tok_recv.at[way, c], place, z, other_tok))

    after = lax.rem(queue_index(place, z) + 1, NX * NZ * NYH)
    after_place = (after // (NZ * NYH)) * NYH + after % NYH
    after_z = (after // NYH) % NZ
    slots = mask_ref.shape[1]
    row_buf[...] = jnp.zeros_like(row_buf)
    row_buf[0:1, :slots] = mask_ref[...]
    for d in range(PLACES):
        stays = jnp.logical_and(d == place, after_z == z)

        @pl.when(jnp.logical_not(stays))
        def _():
            send(row_buf, rows_got.at[after_place], row_send.at[d], row_recv.at[after_place], d, after_z, tok)

        @pl.when(stays)
        def _():
            pltpu.make_async_copy(row_buf, rows_got.at[after_place], row_recv.at[after_place]).start()

    started.append(
        send(gate_ref, prev_gate, prev_send.at[0], prev_recv.at[0], after_place, after_z, tok)
    )

    @pl.when(lax.rem(place, NYH) == 1)
    def _():
        send(frames_ref, prev_frames, prev_send.at[1], prev_recv.at[1], after_place, after_z, tok)

    half = x_buf.shape[0] // 2
    first = tok // 2
    at = [pl.multiple_of(first * half, half), pl.multiple_of((1 - first) * half, half)]

    def part_of(ref, n):
        return ref.at[pl.ds(at[n], half)]

    def keys_values(n):
        x = x_buf[pl.ds(at[n], half)]
        for i in range(pairs):
            if n == 0:
                weights[2 * i].wait()
                weights[2 * i + 1].wait()
            both = jnp.dot(x, wkv_buf[i], preferred_element_type=jnp.float32)
            for j in range(2):
                d = 2 * i + j
                kn = layer_norm(both[:, j * HDIM : (j + 1) * HDIM]) * kg_ref[...]
                v = both[:, pair + j * HDIM : pair + (j + 1) * HDIM]
                kv_buf[d, pl.ds(at[n], half)] = jnp.concatenate([kn, v], axis=1).astype(jnp.bfloat16)
                block = part_of(kv_buf.at[d], n)
                here = part_of(kv_all.at[z, place], n)

                @pl.when(d != place)
                def _():
                    send(block, here, kv_send.at[d, n], kv_recv.at[place, n], d, z, tok)

                @pl.when(d == place)
                def _():
                    pltpu.make_async_copy(block, here, kv_recv.at[place, n]).start()

    last = NZ // 2

    def ring_copy(hop, way, n, c):
        source = lax.rem(z + NZ - (hop - 1), NZ) if way == 0 else lax.rem(z + hop - 1, NZ)
        block = part_of(kv_all.at[source, c], n)
        return pltpu.make_async_remote_copy(
            src_ref=block,
            dst_ref=block,
            send_sem=ring_send.at[way, hop - 1, n, c],
            recv_sem=ring_recv.at[way, hop - 1, n, c],
            device_id=(queue_index(place, down if way else up), tok),
            device_id_type=MESH,
        )

    last_up = jnp.where(lax.rem(place, NYH) == 1, 2, PLACES // 2)

    def goes(hop, way, c):
        if hop < last:
            return True
        return c < last_up if way == 0 else c >= last_up

    def pass_on(hop, n):
        @pl.when(place < HEADS_HERE)
        def _():
            for c in range(PLACES):
                if hop == 1:
                    landed(part_of(kv_all.at[z, c], n), kv_recv.at[c, n])
                for way in range(2):
                    if hop > 1:
                        source = lax.rem(z + NZ - (hop - 1), NZ) if way == 0 else lax.rem(z + hop - 1, NZ)
                        landed(part_of(kv_all.at[source, c], n), ring_recv.at[way, hop - 2, n, c])

                    @pl.when(goes(hop, way, c))
                    def _():
                        ring_copy(hop, way, n, c).start()

    rows_here = wo_ref.shape[0]
    quarter = rows_here // NX
    x_at = place // NYH
    x_next = lax.rem(place + NYH, PLACES)
    x_before = lax.rem(place + PLACES - NYH, PLACES)
    lower = tok // 2 == 0
    y_next = jnp.where(lower, place, twin)
    y_before = jnp.where(lower, twin, place)

    def part_rows(owner, shift, side):
        start = lax.rem(x_at + shift + NX, NX) * quarter
        if side is None:
            return wo_all.at[owner, pl.ds(pl.multiple_of(start, 16), quarter)]
        return wo_all.at[owner, pl.ds(pl.multiple_of(start + side * (quarter // 2), 16), quarter // 2)]

    def y_quarter():
        for side, target in ((0, y_next), (1, y_before)):
            start = pl.multiple_of(x_at * quarter + side * (quarter // 2), 16)
            part = wo_ref.at[pl.ds(start, quarter // 2)]
            started.append(
                send(part, part_rows(tok, 0, side), wo_send.at[side], wo_recv.at[side], target, z, across)
            )

    def x_ring_first():
        for side in range(2):
            landed(part_rows(across, 0, side), wo_recv.at[side])
        mine = part_rows(across, 0, None)
        for k, target in ((2, x_next), (3, x_before)):
            started.append(send(mine, mine, wo_send.at[k], wo_recv.at[k], target, z, tok))

    def x_ring_second():
        for k, shift, side, target in ((4, -1, 0, x_next), (5, 1, 1, x_before)):
            landed(part_rows(across, shift, None), wo_recv.at[k - 2])
            half_part = part_rows(across, shift, side)
            started.append(send(half_part, half_part, wo_send.at[k], wo_recv.at[k], target, z, tok))

    def share(k, block):
        started.append(send(block, block, wo_send.at[k], wo_recv.at[k], place, z, sibling))

    for c in range(CHUNKS):
        landed(x_rows(sibling, c), tok_recv.at[0, c])
    keys_values(0)
    pass_on(1, 0)
    for c in range(CHUNKS):
        theirs = x_rows(across, c)
        landed(theirs, tok_recv.at[1, c])
        started.append(send(theirs, theirs, tok_send.at[2, c], tok_recv.at[2, c], place, z, sibling))
    y_quarter()
    for c in range(CHUNKS):
        landed(x_rows(sibling_across, c), tok_recv.at[2, c])
    keys_values(1)
    pass_on(1, 1)

    started.append(send(wo_ref, wo_all.at[tok], wo_send.at[6], wo_recv.at[6], place, z, sibling))
    x_ring_first()

    weights[-1].wait()
    x = x_buf[...]
    for i in range(pairs):
        q = jnp.dot(x, wq_buf[:, i * pair : (i + 1) * pair], preferred_element_type=jnp.float32)
        for j in range(2):
            d = 2 * i + j
            qn = layer_norm(q[:, j * HDIM : (j + 1) * HDIM]) * qg_ref[...]
            qn = qn.astype(jnp.bfloat16).astype(jnp.float32) * HDIM ** (-0.5)
            q_buf[d] = jnp.concatenate([qn[:half], qn[half:]], axis=1).astype(jnp.bfloat16)
            stays = jnp.logical_and(d == place, after_z == z)

            @pl.when(jnp.logical_not(stays))
            def _():
                send(
                    q_buf.at[d], q_all.at[after_place], q_send.at[d], q_recv.at[after_place], d, after_z, tok
                )

            @pl.when(stays)
            def _():
                pltpu.make_async_copy(q_buf.at[d], q_all.at[after_place], q_recv.at[after_place]).start()

    @pl.when(lax.rem(place, NYH) == 0)
    def _():
        send(frames_ref, prev_frames, prev_send.at[1], prev_recv.at[1], after_place, after_z, tok)

    for hop in range(2, last + 1):
        for n in range(2):
            pass_on(hop, n)
        if hop == 2:
            share(7, part_rows(across, 0, None))
            x_ring_second()
        elif hop == 3:
            share(8, part_rows(across, -1, None))
            share(9, part_rows(across, 1, None))
    for k in (4, 5):
        landed(part_rows(across, 2, k - 4), wo_recv.at[k])
    share(10, part_rows(across, 2, None))

    for p in range(PLACES):
        landed(rows_got.at[p], row_recv.at[p])
    table = rows_got[:, 0, :]
    lanes = table.shape[1]
    lane = lax.broadcasted_iota(jnp.int32, (PLACES, lanes), 1)
    seen = jnp.where(jnp.logical_and(table > 0, lane < slots), 1.0, 0.0)
    by_row = lax.broadcasted_iota(jnp.int32, (lanes, lanes), 0)
    by_lane = lax.broadcasted_iota(jnp.int32, (lanes, lanes), 1)
    ahead = jnp.where(by_row < by_lane, 1.0, 0.0)
    rank = jnp.dot(seen, ahead, preferred_element_type=jnp.float32)
    spot = jnp.where(seen > 0, rank, -1.0)
    spot_t = jnp.transpose(jnp.concatenate([spot] * (lanes // PLACES), axis=0))
    kept_at = ((by_row >> 1) & (NZ - 1)) * PLACES + (by_row >> 4) * NYH + (by_row & 1)
    kept_at = kept_at.astype(jnp.float32)
    lane_f = by_lane.astype(jnp.float32)
    listed = [
        jnp.sum(jnp.where(spot_t[:, p : p + 1] == lane_f, kept_at, 0.0), axis=0, keepdims=True)
        for p in range(PLACES)
    ]
    listed = jnp.concatenate(listed, axis=0).astype(jnp.int32)
    count = jnp.sum(seen, axis=1, keepdims=True).astype(jnp.int32)
    count = jnp.where(place < HEADS_HERE, count, 0)
    info_ref[...] = jnp.where(lane == slots, count, listed)

    @pl.when(place < HEADS_HERE)
    def _():
        opposite = lax.rem(z + last, NZ)
        for n in range(2):
            for c in range(PLACES):
                for way in range(2):
                    @pl.when(goes(last, way, c))
                    def _():
                        landed(part_of(kv_all.at[opposite, c], n), ring_recv.at[way, last - 1, n, c])
        for p in range(PLACES):
            landed(q_all.at[p], q_recv.at[p])
        for hop in range(1, last + 1):
            for n in range(2):
                for c in range(PLACES):
                    for way in range(2):
                        @pl.when(goes(hop, way, c))
                        def _():
                            ring_copy(hop, way, n, c).wait_send()

    landed(prev_gate, prev_recv.at[0])
    landed(prev_frames, prev_recv.at[1])
    landed(frames_ref, prev_send.at[1])
    landed(wo_all.at[sibling], wo_recv.at[6])
    for k, shift in ((7, 0), (8, -1), (9, 1), (10, 2)):
        landed(part_rows(sibling_across, shift, None), wo_recv.at[k])
    for copy in started:
        copy.wait_send()
    for d in range(PLACES):
        @pl.when(jnp.logical_not(jnp.logical_and(d == place, after_z == z)))
        def _():
            landed(row_buf, row_send.at[d])
            if d < HEADS_HERE:
                landed(q_buf.at[d], q_send.at[d])

    for d in range(HEADS_HERE):
        for n in range(2):
            @pl.when(d != place)
            def _():
                landed(part_of(kv_buf.at[d], n), kv_send.at[d, n])


def gather(frames, shift, scale, gate, mask, wq, wk, wv, wo, query_gain, key_gain):
    rows, width = frames.shape
    tokens = rows * 4
    pair = 2 * HDIM
    vmem, hbm = pl.BlockSpec(memory_space=pltpu.VMEM), pl.BlockSpec(memory_space=pl.ANY)
    dma = pltpu.SemaphoreType.DMA
    return pl.pallas_call(
        gather_kernel,
        in_specs=[vmem, vmem, vmem, vmem, vmem, hbm, hbm, hbm, hbm, vmem, vmem],
        out_specs=[hbm, hbm, vmem, hbm, vmem, hbm],
        out_shape=[
            jax.ShapeDtypeStruct((PLACES, tokens // 2, pair), jnp.bfloat16),
            jax.ShapeDtypeStruct((NZ, PLACES, tokens, pair), jnp.bfloat16),
            jax.ShapeDtypeStruct((PLACES, 128), jnp.int32),
            jax.ShapeDtypeStruct(frames.shape, jnp.bfloat16),
            jax.ShapeDtypeStruct(gate.shape, jnp.float32),
            jax.ShapeDtypeStruct((4,) + wo.shape, jnp.bfloat16),
        ],
        scratch_shapes=[
            pltpu.VMEM((tokens, width), jnp.bfloat16),
            pltpu.VMEM(wq.shape, jnp.bfloat16),
            pltpu.VMEM((HEADS_HERE // 2, width, 2 * pair), jnp.bfloat16),
            pltpu.VMEM((HEADS_HERE, tokens // 2, pair), jnp.bfloat16),
            pltpu.VMEM((HEADS_HERE, tokens, pair), jnp.bfloat16),
            pltpu.VMEM((8, 128), jnp.int32),
            pltpu.VMEM((PLACES, 8, 128), jnp.int32),
            dma,
            dma((HEADS_HERE // 2, 2)),
            dma((3, CHUNKS)),
            dma((3, CHUNKS)),
            dma((PLACES,)),
            dma((PLACES,)),
            dma((HEADS_HERE, 2)),
            dma((PLACES, 2)),
            dma((HEADS_HERE,)),
            dma((PLACES,)),
            dma((2, NZ // 2, 2, PLACES)),
            dma((2, NZ // 2, 2, PLACES)),
            dma((2,)),
            dma((2,)),
            dma((11,)),
            dma((11,)),
        ],
        compiler_params=pltpu.CompilerParams(
            collective_id=0, has_side_effects=True, vmem_limit_bytes=52 * 1024 * 1024
        ),
    )(frames, shift, scale, gate, mask, wq, wk, wv, wo, query_gain.reshape(1, HDIM), key_gain.reshape(1, HDIM))


def attend_kernel(info_ref, q_ref, kv_ref, out_ref):
    frames_here, half, lanes = q_ref.shape
    rows = 2 * half
    slots = kv_ref.shape[0]
    low = lax.broadcasted_iota(jnp.int32, (half, lanes), 1) < HDIM

    def one_frame(i, _):
        packed = q_ref[i].astype(jnp.float32)
        top = jnp.where(low, packed, 0.0)
        bottom = jnp.where(low, pltpu.roll(packed, HDIM, 1), 0.0)
        q = jnp.concatenate([top, bottom], axis=0).astype(jnp.bfloat16)

        def blocks(state, *numbers):
            running_max, running_sum, weighted = state
            kvs = [kv_ref[info_ref[i, j]] for j in numbers]
            scores = [
                lax.dot_general(kv, q, (((1,), (1,)), ((), ())), preferred_element_type=jnp.float32) for kv in kvs
            ]
            new_max = running_max
            for s in scores:
                new_max = jnp.maximum(new_max, jnp.max(s, axis=0, keepdims=True))
            rescale = jnp.exp(running_max - new_max)
            running_sum, weighted = running_sum * rescale, weighted * rescale
            for kv, s in zip(kvs, scores):
                weights = jnp.exp(s - new_max)
                running_sum = running_sum + jnp.sum(weights, axis=0, keepdims=True)
                weighted = weighted + lax.dot_general(
                    kv, weights.astype(jnp.bfloat16), (((0,), (0,)), ((), ())), preferred_element_type=jnp.float32
                )
            return new_max, running_sum, weighted

        state = (
            jnp.full((1, rows), -1e30, jnp.float32),
            jnp.zeros((1, rows), jnp.float32),
            jnp.zeros((lanes, rows), jnp.float32),
        )
        count = info_ref[i, slots]
        twos = count // 2
        state = lax.fori_loop(0, twos, lambda j, s: blocks(s, 2 * j, 2 * j + 1), state)
        _, total, weighted = lax.fori_loop(2 * twos, count, lambda j, s: blocks(s, j), state)
        attended = jnp.transpose(weighted[HDIM:] / total)
        chunk = rows // 4
        for c in range(4):
            part = attended[c * chunk : (c + 1) * chunk]
            out_ref[i, c] = jnp.concatenate([part[: chunk // 2], part[chunk // 2 :]], axis=1).astype(jnp.bfloat16)
        return 0

    lax.fori_loop(0, frames_here, one_frame, 0)


def attend(info, q, kv):
    frames_here, half, lanes = q.shape
    return pl.pallas_call(
        attend_kernel,
        grid_spec=pltpu.PrefetchScalarGridSpec(
            num_scalar_prefetch=1,
            grid=(1,),
            in_specs=[pl.BlockSpec(memory_space=pltpu.VMEM)] * 2,
            out_specs=pl.BlockSpec((frames_here, 4, half // 4, lanes), lambda i, *_: (0, 0, 0, 0)),
        ),
        out_shape=jax.ShapeDtypeStruct((frames_here, 4, half // 4, lanes), jnp.bfloat16),
        compiler_params=pltpu.CompilerParams(vmem_limit_bytes=40 * 1024 * 1024),
    )(info, q, kv)


def finish_kernel(
    att_ref, w_ref, own_ref, frames_ref, gate_ref, out_ref, got, att_buf, w_buf, w_sem, send_sem, recv_sem
):
    place, z, tok = positions()
    width = out_ref.shape[1]
    tile = width // TILES
    rows = own_ref.shape[0]
    weights = []
    for n in range(TILES):
        cols = pl.ds(n * tile, tile)
        for other in range(4):
            block = lax.rem(tok + other, 4)
            source = own_ref.at[:, cols] if other == 0 else w_ref.at[block, :, cols]
            place_in = w_buf.at[n, pl.ds(pl.multiple_of(block * rows, rows), rows)]
            weights.append(pltpu.make_async_copy(source, place_in, w_sem.at[n, other]))
    for copy in weights:
        copy.start()
    barrier = pltpu.get_barrier_semaphore()
    for p in range(PLACES):
        for t in range(4):
            @pl.when(jnp.logical_not(jnp.logical_and(p == place, t == tok)))
            def _():
                pl.semaphore_signal(barrier, inc=1, device_id=(queue_index(p, z), t), device_id_type=MESH)
    pl.semaphore_wait(barrier, 4 * PLACES - 1)

    slot = tok * HEADS_HERE + place

    @pl.when(place < HEADS_HERE)
    def _():
        for p in range(PLACES):
            for t in range(4):
                here = jnp.logical_and(p == place, t == tok)

                @pl.when(jnp.logical_not(here))
                def _():
                    send(att_ref.at[p, t], got.at[slot], send_sem.at[p, t], recv_sem.at[slot], p, z, t)

                @pl.when(here)
                def _():
                    pltpu.make_async_copy(att_ref.at[p, t], got.at[slot], recv_sem.at[slot]).start()

    heads, half, lanes = got.shape
    low = lax.broadcasted_iota(jnp.int32, (half, lanes), 1) < HDIM
    for m in range(heads // 2):
        landed(got.at[2 * m], recv_sem.at[2 * m])
        landed(got.at[2 * m + 1], recv_sem.at[2 * m + 1])
        first, second = got[2 * m].astype(jnp.float32), got[2 * m + 1].astype(jnp.float32)
        cols = slice(m * lanes, (m + 1) * lanes)
        att_buf[:half, cols] = jnp.where(low, first, pltpu.roll(second, HDIM, 1)).astype(jnp.bfloat16)
        att_buf[half:, cols] = jnp.where(low, pltpu.roll(first, HDIM, 1), second).astype(jnp.bfloat16)
    attended = att_buf[...]
    for n in range(TILES):
        for copy in weights[4 * n : 4 * n + 4]:
            copy.wait()
        projected = jnp.dot(attended, w_buf[n], preferred_element_type=jnp.float32)
        cols = slice(n * tile, (n + 1) * tile)
        updated = frames_ref[:, cols].astype(jnp.float32) + gate_ref[:, cols] * projected
        out_ref[:, cols] = updated.astype(jnp.bfloat16)

    @pl.when(place < HEADS_HERE)
    def _():
        for p in range(PLACES):
            for t in range(4):
                @pl.when(jnp.logical_not(jnp.logical_and(p == place, t == tok)))
                def _():
                    landed(att_ref.at[p, t], send_sem.at[p, t])


def finish(attended, w_all, w_own, frames, gate):
    vmem, hbm = pl.BlockSpec(memory_space=pltpu.VMEM), pl.BlockSpec(memory_space=pl.ANY)
    dma = pltpu.SemaphoreType.DMA
    depth, width = 4 * w_own.shape[0], w_own.shape[1]
    return pl.pallas_call(
        finish_kernel,
        in_specs=[hbm, hbm, hbm, vmem, vmem],
        out_specs=vmem,
        out_shape=jax.ShapeDtypeStruct(frames.shape, jnp.bfloat16),
        scratch_shapes=[
            pltpu.VMEM((4 * HEADS_HERE,) + attended.shape[2:], jnp.bfloat16),
            pltpu.VMEM((frames.shape[0], depth), jnp.bfloat16),
            pltpu.VMEM((TILES, depth, width // TILES), jnp.bfloat16),
            dma((TILES, 4)),
            dma((PLACES, 4)),
            dma((4 * HEADS_HERE,)),
        ],
        compiler_params=pltpu.CompilerParams(
            collective_id=1, has_side_effects=True, vmem_limit_bytes=48 * 1024 * 1024
        ),
    )(attended, w_all, w_own, frames, gate)


def body(
    frames, levels, frame_mask, modulation, w_query, w_key, w_value, w_out, query_gain, key_gain
):
    width = frames.shape[2]
    slots = frame_mask.shape[1]
    own = lax.dynamic_slice(modulation, (levels[0], 0), (1, 3 * width)).astype(jnp.float32)
    q, kv, info, prev_frames, prev_gate, w_all = gather(
        frames[0], own[:, :width], own[:, width : 2 * width], own[:, 2 * width :], frame_mask,
        w_query, w_key, w_value, w_out, query_gain, key_gain,
    )
    attended = attend(info, q, kv.reshape((slots,) + kv.shape[2:]))
    return finish(attended, w_all, w_out, prev_frames, prev_gate)[None]


def solution(mesh):
    return jax.shard_map(
        body,
        mesh=mesh,
        in_specs=(
            P("queue", "tok", None),
            P("queue"),
            P("queue", None),
            P(),
            P(None, "tok"),
            P(None, "tok"),
            P(None, "tok"),
            P("tok", None),
            P(),
            P(),
        ),
        out_specs=P("queue", "tok", None),
        check_vma=False,
    )
```
